32 devices in a mesh: dp: 8 (over z, x), mp: 4 (over y, core).
Axes of the slice: x: 2, y: 2, z: 4, core: 2. Of those that a mesh axis runs over, the one named last changes fastest.
Arguments:
- byte_embeds: bfloat16 [16384, 768], P('dp'), may hold values from -6 to 6
- lengths: int32 [8], P('dp'), may hold values from 200 to 2048, as said below
- score_weight: bfloat16 [768], replicated, may hold values from -0.21875 to 0.21875
- norm1_gain: bfloat16 [768], replicated, may hold values from 0.099609375 to 1.8984375
- w_query: bfloat16 [768, 768], P(None, 'mp'), may hold values from -0.046875 to 0.046875
- w_key: bfloat16 [768, 768], P(None, 'mp'), may hold values from -0.21875 to 0.21875
- w_value: bfloat16 [768, 768], P(None, 'mp'), may hold values from -0.21875 to 0.21875
- rel_table: bfloat16 [32, 12], P(None, 'mp'), may hold values from -4 to 4
- w_out: bfloat16 [768, 768], P('mp'), may hold values from -0.875 to 0.875
- norm2_gain: bfloat16 [768], replicated, may hold values from 0.099609375 to 1.8984375
- w_gate: bfloat16 [768, 2048], P(None, 'mp'), may hold values from -0.21875 to 0.21875
- w_up: bfloat16 [768, 2048], P(None, 'mp'), may hold values from -0.21875 to 0.21875
- w_down: bfloat16 [2048, 768], P('mp'), may hold values from -0.125 to 0.125
- cotangent: bfloat16 [8192, 768], P(('dp', 'mp')), may hold values from -6 to 6
Outputs:
- out_rows: bfloat16 [8192, 768], P(('dp', 'mp'))
- byte_grad: bfloat16 [16384, 768], P('dp')
- score_grad: float32 [768], P('dp')
- gain1_grad: float32 [768], replicated
- query_grad: float32 [768, 768], P('dp', 'mp')
- key_grad: float32 [768, 768], P('dp', 'mp')
- value_grad: float32 [768, 768], P('dp', 'mp')
- table_grad: float32 [32, 12], P(None, 'mp')
- out_grad: float32 [768, 768], P('mp', 'dp')
- gain2_grad: float32 [768], replicated
- gate_grad: float32 [768, 2048], P('dp', 'mp')
- up_grad: float32 [768, 2048], P('dp', 'mp')
- down_grad: float32 [2048, 768], P('mp', 'dp')
- size_dist: float32 [4], replicated
The draws below stay inside these ranges and needn't reach their ends.
Inputs may be any that keep to these rules, and one draw needn't show every extreme that they name: Document d occupies bytes 0 to lengths[d] - 1 of its slot of 2048 bytes; in every draw one document has exactly 2048 bytes and one exactly 200.
All inputs are finite; a program needn't handle non-finite values.
Results may differ from the reference program's by a relative error of at most 0.019.
The reference program's roundings to bfloat16 on the way count: a program that leaves them out, or rounds other values in their place, can miss the bound.
Values may be sent and summed in bfloat16 or wider, within the bound.
No kernel may reach another device: no remote copies, remote signals or barrier semaphores. Data moves between devices by JAX's collectives and lax.ppermute only.
A program may use at most 640 MiB of HBM per device.

```python
import jax
import jax.numpy as jnp
from jax import lax

D = 768
H = 12
DH = 64
FF = 2048
BUCKETS = 32
SLOT_BYTES = 2048
MIN_BYTES = 200
DOCS = 8
SLOT_ROWS = 1024
ROWS = 8192
BYTES = 16384


def draw_lengths(key, part):
    key = jax.random.fold_in(key, 7)
    first_key, second_key = jax.random.split(key)
    doc_ids = jnp.arange(DOCS, dtype=jnp.int32)
    spread = (SLOT_BYTES - MIN_BYTES) // 3
    low_end = MIN_BYTES + 2 * spread * doc_ids // max(DOCS - 1, 1)
    drawn = low_end + jax.random.randint(first_key, (DOCS,), 0, spread, dtype=jnp.int32)
    picked = jax.random.permutation(second_key, DOCS)
    drawn = jnp.where(doc_ids == picked[0], SLOT_BYTES, drawn)
    drawn = jnp.where(doc_ids == picked[1], MIN_BYTES, drawn)
    return drawn.astype(jnp.int32)


def block_scale(own_key, extent, pieces, least, largest):
    def one(dim, blocks):
        steps = jax.random.uniform(jax.random.fold_in(jax.random.fold_in(own_key, 6), dim), (blocks,), jnp.float32, least / len(pieces), largest / len(pieces))
        return jnp.repeat(jnp.exp(steps), extent[dim] // blocks).reshape((-1,) + (1,) * (len(extent) - dim - 1))

    gain = one(*pieces[0])
    for cut in pieces[1:]:
        gain = gain * one(*cut)
    return gain


def centred(stream_key, extent, width, most, pieces=(), kind=jnp.bfloat16):
    loudness = block_scale(stream_key, extent, pieces, -0.22, 0.18) if pieces else 1.0
    array = jax.random.normal(stream_key, extent, jnp.float32) * width * loudness
    return jnp.minimum(jnp.maximum(array, -most), most).astype(kind)


def setup_inputs(seed: int = 0) -> dict:
    seeds = jax.random.split(jax.random.key(seed), 15)
    return {
        "byte_embeds": centred(seeds[0], (BYTES, D), 1.0, 6.0, ((0, 8),)),
        "lengths": draw_lengths(jax.random.fold_in(seeds[14], 71), 0),
        "score_weight": centred(seeds[2], (D,), D ** -0.5, 0.21875),
        "norm1_gain": jnp.clip(1.0 + 0.18 * jax.random.normal(seeds[3], (D,), jnp.float32), 0.099609375, 1.8984375).astype(jnp.bfloat16),
        "w_query": centred(seeds[4], (D, D), (D * 24) ** -0.5, 0.046875, ((1, 4),)),
        "w_key": centred(seeds[5], (D, D), D ** -0.5, 0.21875, ((1, 4),)),
        "w_value": centred(seeds[6], (D, D), D ** -0.5, 0.21875, ((1, 4),)),
        "rel_table": centred(seeds[7], (BUCKETS, H), 1.0, 4.0, ((1, 4),)),
        "w_out": centred(seeds[8], (D, D), (D // 16) ** -0.5, 0.875, ((0, 4),)),
        "norm2_gain": jnp.clip(1.0 + 0.18 * jax.random.normal(seeds[9], (D,), jnp.float32), 0.099609375, 1.8984375).astype(jnp.bfloat16),
        "w_gate": centred(seeds[10], (D, FF), D ** -0.5, 0.21875, ((1, 4),)),
        "w_up": centred(seeds[11], (D, FF), D ** -0.5, 0.21875, ((1, 4),)),
        "w_down": centred(seeds[12], (FF, D), FF ** -0.5, 0.125, ((0, 4),)),
        "cotangent": centred(seeds[13], (ROWS, D), 1.0, 6.0, ((0, 32),)),
    }


epsilon = 1e-06
bucket_edges = (12, 16, 23, 32, 46, 64, 91)
highest = lax.Precision.HIGHEST

@jax.custom_vjp
def low(v):
    return lax.optimization_barrier(v.astype(jnp.bfloat16)).astype(jnp.float32)

@jax.custom_vjp
def low_back(v):
    return v

def low_keep(v):
    return (low(v), None)

def low_pass(kept, grad):
    return (grad,)

def back_keep(v):
    return (v, None)

def back_low(kept, grad):
    return (low(grad),)
low.defvjp(low_keep, low_pass)
low_back.defvjp(back_keep, back_low)

def both_ways(value):
    return low_back(low(value))

def pooled(raw_doc, score_vector, length):
    byte_count = raw_doc.shape[0]
    model_width = raw_doc.shape[1]
    padded = (byte_count + 11) // 12 * 12
    inside = (jnp.arange(byte_count, dtype=jnp.int32) < length).astype(jnp.float32)
    filled = jnp.pad(raw_doc * inside[:, None], ((0, padded - byte_count), (0, 0)))
    byte_scores = jnp.dot(filled, score_vector, precision=highest)
    logit_list = []
    mean_list = []
    for block_len in (1, 2, 3, 4):
        block_means = lax.optimization_barrier(jnp.mean(filled.reshape(padded // block_len, block_len, model_width), axis=1))
        mean_list.append(jnp.repeat(block_means, block_len, axis=0))
        logit_list.append(jnp.repeat(lax.optimization_barrier(jnp.mean(byte_scores.reshape(padded // block_len, block_len), axis=1)), block_len))
    logits = jnp.stack(logit_list)
    shifted = jnp.exp(logits - lax.optimization_barrier(jnp.max(logits, axis=0, keepdims=True)))
    weights = shifted / lax.optimization_barrier(jnp.sum(shifted, axis=0, keepdims=True))
    mixture = weights[0][:, None] * mean_list[0]
    for slot_id in range(1, 4):
        mixture = mixture + weights[slot_id][:, None] * mean_list[slot_id]
    row_vals = lax.optimization_barrier(jnp.mean(mixture[:byte_count].reshape(byte_count // 2, 2, model_width), axis=1))
    size_sums = lax.optimization_barrier(jnp.sum(weights[:, :byte_count] * inside[None, :], axis=1))
    return (row_vals, size_sums)

def normed(values, gain_vec):
    return values * lax.rsqrt(lax.optimization_barrier(jnp.mean(values * values, axis=-1, keepdims=True)) + epsilon) * gain_vec

def bucket_of(offsets):
    distance = jnp.abs(offsets)
    far_bucket = 8 + sum(((distance >= edge).astype(jnp.int32) for edge in bucket_edges))
    near_bucket = jnp.where(distance < 8, distance, far_bucket)
    return near_bucket + jnp.where(offsets > 0, 16, 0).astype(jnp.int32)

def relative_t(bias_table, row_count):
    offsets = jnp.arange(2 * row_count - 1, dtype=jnp.int32) - (row_count - 1)
    numbers = jnp.arange(bias_table.shape[0], dtype=jnp.int32)
    onehot = (bucket_of(offsets)[:, None] == numbers[None, :]).astype(jnp.float32)
    return jnp.dot(onehot, bias_table, precision=highest).T

def bias_block(rel_t, row_start, row_total, row_count):
    query_pos = row_start + jnp.arange(row_total, dtype=jnp.int32)[:, None]
    key_pos = jnp.arange(row_count, dtype=jnp.int32)[None, :]
    return jnp.take(rel_t, key_pos - query_pos + (row_count - 1), axis=1)

def key_mask(row_count, valid_rows):
    return jnp.where(jnp.arange(row_count, dtype=jnp.int32) < valid_rows, 0.0, -1e+30).astype(jnp.float32)

def layer_rows(row_vals, valid_rows, norm1_gain, w_query, w_key, w_value, rel_table, w_out, norm2_gain, w_gate, w_up, w_down):
    row_count = row_vals.shape[0]
    first_norm = low(normed(row_vals, norm1_gain))
    queries = both_ways(jnp.dot(first_norm, w_query, precision=highest)).reshape(row_count, H, DH)
    keys_all = both_ways(jnp.dot(first_norm, w_key, precision=highest)).reshape(row_count, H, DH)
    values_all = both_ways(jnp.dot(first_norm, w_value, precision=highest)).reshape(row_count, H, DH)
    rel_t = relative_t(rel_table, row_count)
    scores = jnp.einsum('qhd,khd->hqk', queries, keys_all, precision=highest)
    scores = scores + bias_block(rel_t, 0, row_count, row_count) + key_mask(row_count, valid_rows)[None, None, :]
    scores = low_back(scores)
    shifted = jnp.exp(scores - lax.optimization_barrier(jnp.max(scores, axis=-1, keepdims=True)))
    prob_vals = shifted / lax.optimization_barrier(jnp.sum(shifted, axis=-1, keepdims=True))
    mixed_heads = jnp.einsum('hqk,khd->qhd', low(prob_vals), values_all, precision=highest).reshape(row_count, H * DH)
    mixed_heads = both_ways(mixed_heads)
    after_attn = row_vals + low_back(jnp.dot(mixed_heads, w_out, precision=highest))
    second_norm = low(normed(after_attn, norm2_gain))
    gate_vals = low_back(jnp.dot(second_norm, w_gate, precision=highest))
    up_vals = low_back(jnp.dot(second_norm, w_up, precision=highest))
    hidden = low(jax.nn.gelu(gate_vals, approximate=True) * up_vals)
    return after_attn + low_back(jnp.dot(hidden, w_down, precision=highest))

def reference(byte_embeds, lengths, score_weight, norm1_gain, w_query, w_key, w_value, rel_table, w_out, norm2_gain, w_gate, w_up, w_down, cotangent):
    weights_f = tuple((element.astype(jnp.float32) for element in (score_weight, norm1_gain, w_query, w_key, w_value, rel_table, w_out, norm2_gain, w_gate, w_up, w_down)))
    raw_docs = byte_embeds.astype(jnp.float32).reshape(DOCS, SLOT_BYTES, D)
    cot_docs = cotangent.astype(jnp.float32).reshape(DOCS, SLOT_ROWS, D)

    def one_doc(running, inputs):
        grad_sums, size_total = running
        raw_doc, cot_doc, length = inputs

        def forward(raw_in, *params):
            row_vals, size_mass = pooled(raw_in, params[0], length)
            return (layer_rows(row_vals, (length + 1) // 2, *params[1:]), size_mass)
        result, pull_back, size_mass = jax.vjp(forward, raw_doc, *weights_f, has_aux=True)
        gradients = pull_back(cot_doc)
        grad_sums = tuple((summed + latest for summed, latest in zip(grad_sums, gradients[1:])))
        return ((grad_sums, size_total + size_mass), (result, gradients[0]))
    start_grads = tuple((jnp.zeros_like(element) for element in weights_f))
    (grad_sums, size_total), (results, raw_grads) = lax.scan(one_doc, (start_grads, jnp.zeros((4,), jnp.float32)), (raw_docs, cot_docs, lengths))
    size_dist = size_total / jnp.sum(lengths).astype(jnp.float32)
    return (results.reshape(ROWS, D).astype(jnp.bfloat16), raw_grads.reshape(BYTES, D).astype(jnp.bfloat16), grad_sums[0], grad_sums[1], grad_sums[2], grad_sums[3], grad_sums[4], grad_sums[5], grad_sums[6], grad_sums[7], grad_sums[8], grad_sums[9], grad_sums[10], size_dist)
```

```python
import math

import jax
import jax.numpy as jnp
from jax import lax
from jax.sharding import PartitionSpec as P

DH = 64
BUCKETS = 32


epsilon = 1e-06
bucket_edges = (12, 16, 23, 32, 46, 64, 91)
highest = lax.Precision.HIGHEST


def shortened(shard):
    return jax.tree.map(lambda a: a.astype(jnp.bfloat16) if a.dtype == jnp.float32 else a, shard)


def in_blocks(shard, dim, peers):
    lengths = shard.shape
    blocks = shard.reshape(*lengths[:dim], peers, lengths[dim] // peers, *lengths[dim + 1 :])
    return jnp.moveaxis(blocks, dim, 0)


def summed_on_arrival(shard, axis, dim):
    peers = lax.axis_size(axis)
    blocks = lax.all_to_all(in_blocks(shard, dim, peers), axis, 0, 0, tiled=True)
    return jnp.sum(blocks.astype(jnp.float32), axis=0)


def side_by_side(arrays, axis, dim, along):
    widths = [math.prod(a.shape[along:]) for a in arrays]
    both = jnp.concatenate(
        [a.reshape(*a.shape[:along], w) for a, w in zip(arrays, widths)], axis=along
    )
    filled = summed_on_arrival(both, axis, dim)
    blocks = jnp.split(filled, [sum(widths[:k]) for k in range(1, len(widths))], axis=along)
    return tuple(
        (b.reshape(*filled.shape[:along], *a.shape[along:]) for a, b in zip(arrays, blocks))
    )


def sent_together(arrays, axis, dim, along):
    both = jnp.concatenate(arrays, axis=along)
    filled, at, done = (summed_on_arrival(both, axis, dim), 0, [])
    for a in arrays:
        done.append(lax.slice_in_dim(filled, at, at + a.shape[along], axis=along))
        at += a.shape[along]
    return tuple(done)


def spread_blocks(block_vals, block_len, padded):
    width = block_vals.shape[-1]
    return jnp.broadcast_to(
        block_vals[:, None, :], (padded // block_len, block_len, width)
    ).reshape(padded, width)


def pooled(raw_doc, score_vector, length):
    byte_count = raw_doc.shape[0]
    model_width = raw_doc.shape[1]
    padded = (byte_count + 11) // 12 * 12
    inside = (jnp.arange(byte_count, dtype=jnp.int32) < length).astype(jnp.float32)
    filled = jnp.pad(raw_doc * inside[:, None], ((0, padded - byte_count), (0, 0)))
    byte_scores = jnp.dot(filled, score_vector, precision=highest)
    logit_list = []
    for block_len in (1, 2, 3, 4):
        block_logit = jnp.mean(byte_scores.reshape(padded // block_len, block_len), axis=1)
        logit_list.append(
            jnp.broadcast_to(block_logit[:, None], (padded // block_len, block_len)).reshape(padded)
        )
    logits = jnp.stack(logit_list)
    shifted = jnp.exp(logits - jnp.max(logits, axis=0, keepdims=True))
    weights = shifted / jnp.sum(shifted, axis=0, keepdims=True)
    mixture = weights[0][:, None] * filled
    for block_len in (2, 3, 4):
        block_means = jnp.mean(filled.reshape(padded // block_len, block_len, model_width), axis=1)
        mixture = mixture + weights[block_len - 1][:, None] * spread_blocks(
            block_means, block_len, padded
        )
    row_vals = jnp.mean(mixture[:byte_count].reshape(byte_count // 2, 2, model_width), axis=1)
    size_sums = jnp.sum(weights[:, :byte_count] * inside[None, :], axis=1)
    return (row_vals, size_sums)


def normed(values, gain_vec):
    return (
        values * lax.rsqrt(jnp.mean(values * values, axis=-1, keepdims=True) + epsilon) * gain_vec
    )


def bucket_of(offsets):
    distance = jnp.abs(offsets)
    far_bucket = 8 + sum(((distance >= edge).astype(jnp.int32) for edge in bucket_edges))
    near_bucket = jnp.where(distance < 8, distance, far_bucket)
    return near_bucket + jnp.where(offsets > 0, 16, 0).astype(jnp.int32)


def pair_buckets(row_start, row_total, row_count):
    query_pos = row_start + jnp.arange(row_total, dtype=jnp.int32)[:, None]
    key_pos = jnp.arange(row_count, dtype=jnp.int32)[None, :]
    return bucket_of(key_pos - query_pos)


def bias_of(table, buckets):
    bias = jnp.zeros((table.shape[1], *buckets.shape), jnp.float32)
    for bucket_id in range(BUCKETS):
        hit = (buckets == bucket_id)[None]
        bias = jnp.where(hit, table[bucket_id][:, None, None], bias)
    return bias


def key_mask(row_count, valid_rows):
    return jnp.where(jnp.arange(row_count, dtype=jnp.int32) < valid_rows, 0.0, -1e30).astype(
        jnp.float32
    )


def contract(left, right, left_dim, right_dim):
    return lax.dot_general(
        left, right, (((left_dim,), (right_dim,)), ((), ())), preferred_element_type=jnp.float32
    )


def gated(gate_in, up_in):
    return jax.nn.gelu(gate_in, approximate=True) * up_in


def attend(query_doc, key_doc, value_doc, bias_full, valid_rows):
    row_count = query_doc.shape[0]
    step_rows = min(512, row_count)
    masking = key_mask(row_count, valid_rows)
    mixed_parts = []
    sum_parts = []
    for row_start in range(0, row_count, step_rows):
        query_block = query_doc[row_start : row_start + step_rows]
        scores = jnp.einsum(
            "qhd,khd->hqk", query_block, key_doc, preferred_element_type=jnp.float32
        )
        scores = scores + bias_full[:, row_start : row_start + step_rows] + masking
        row_peak = jnp.max(scores, axis=-1, keepdims=True)
        shifted = jnp.exp(scores - row_peak)
        total_mass = jnp.sum(shifted, axis=-1, keepdims=True)
        prob_low = (shifted / total_mass).astype(jnp.bfloat16)
        mixed_parts.append(
            jnp.einsum("hqk,khd->qhd", prob_low, value_doc, preferred_element_type=jnp.float32)
        )
        sum_parts.append(row_peak[..., 0] + jnp.log(total_mass[..., 0]))
    mixed_heads = jnp.concatenate(mixed_parts, axis=0).reshape(row_count, -1).astype(jnp.bfloat16)
    return (mixed_heads, jnp.concatenate(sum_parts, axis=1))


def attend_back(query_doc, key_doc, value_doc, grad_doc, sums_doc, bias_full, valid_rows):
    row_count = query_doc.shape[0]
    step_rows = min(512, row_count)
    inner_rows = min(128, step_rows)
    masking = key_mask(row_count, valid_rows)
    bucket_ids = jnp.arange(BUCKETS, dtype=jnp.int32)
    query_parts = []
    key_back = jnp.zeros(key_doc.shape, jnp.float32)
    value_back = jnp.zeros(value_doc.shape, jnp.float32)
    table_back = jnp.zeros((BUCKETS, query_doc.shape[1]), jnp.float32)
    for row_start in range(0, row_count, step_rows):
        query_block = query_doc[row_start : row_start + step_rows]
        grad_block = grad_doc[row_start : row_start + step_rows]
        scores = jnp.einsum(
            "qhd,khd->hqk", query_block, key_doc, preferred_element_type=jnp.float32
        )
        scores = scores + bias_full[:, row_start : row_start + step_rows] + masking
        prob_vals = jnp.exp(scores - sums_doc[:, row_start : row_start + step_rows, None])
        prob_low = prob_vals.astype(jnp.bfloat16)
        prob_back = jnp.einsum(
            "qhd,khd->hqk", grad_block, value_doc, preferred_element_type=jnp.float32
        )
        inner_sum = jnp.sum(prob_vals * prob_back, axis=-1, keepdims=True)
        score_back = (prob_vals * (prob_back - inner_sum)).astype(jnp.bfloat16)
        query_parts.append(
            jnp.einsum("hqk,khd->qhd", score_back, key_doc, preferred_element_type=jnp.float32)
        )
        key_back = key_back + jnp.einsum(
            "hqk,qhd->khd", score_back, query_block, preferred_element_type=jnp.float32
        )
        value_back = value_back + jnp.einsum(
            "hqk,qhd->khd", prob_low, grad_block, preferred_element_type=jnp.float32
        )
        for inner_start in range(0, step_rows, inner_rows):
            inner_ids = pair_buckets(row_start + inner_start, inner_rows, row_count)
            onehot = (inner_ids[:, :, None] == bucket_ids).astype(jnp.bfloat16)
            table_back = table_back + jnp.einsum(
                "hqk,qkb->bh",
                score_back[:, inner_start : inner_start + inner_rows],
                onehot,
                preferred_element_type=jnp.float32,
            )
    return (jnp.concatenate(query_parts, axis=0), key_back, value_back, table_back)


def body(
    byte_embeds,
    lengths,
    score_weight,
    norm1_gain,
    w_query,
    w_key,
    w_value,
    rel_table,
    w_out,
    norm2_gain,
    w_gate,
    w_up,
    w_down,
    cotangent,
):
    model_width = byte_embeds.shape[1]
    doc_count = lengths.shape[0]
    slot_bytes = byte_embeds.shape[0] // doc_count
    slot_rows = slot_bytes // 2
    all_rows = doc_count * slot_rows
    own_rows = cotangent.shape[0]
    row_base = lax.axis_index("mp") * own_rows
    local_heads = w_query.shape[1] // DH
    score_vec = score_weight.astype(jnp.float32)
    gain_one = norm1_gain.astype(jnp.float32)
    gain_two = norm2_gain.astype(jnp.float32)
    raw_docs = byte_embeds.reshape(doc_count, slot_bytes, model_width)
    valid_rows = (lengths + 1) // 2

    def pool_one(inputs):
        raw_doc, length = inputs
        return pooled(raw_doc.astype(jnp.float32), score_vec, length)

    pooled_rows, size_mass = lax.map(pool_one, (raw_docs, lengths))
    start_rows = lax.dynamic_slice_in_dim(
        pooled_rows.reshape(all_rows, model_width), row_base, own_rows, 0
    )
    first_norm = normed(start_rows, gain_one).astype(jnp.bfloat16)
    gathered_one = lax.all_gather(first_norm, "mp", axis=0, tiled=True)
    w_joint = jnp.concatenate((w_query, w_key, w_value), axis=1)
    joint_low = jnp.dot(gathered_one, w_joint, preferred_element_type=jnp.float32).astype(
        jnp.bfloat16
    )
    joint_low = joint_low.reshape(doc_count, slot_rows, 3, local_heads, DH)
    queries = joint_low[:, :, 0]
    keys_all = joint_low[:, :, 1]
    values_all = joint_low[:, :, 2]
    bias_full = bias_of(rel_table.astype(jnp.float32), pair_buckets(0, slot_rows, slot_rows))

    def attend_one(inputs):
        query_doc, key_doc, value_doc, valid_count = inputs
        return attend(query_doc, key_doc, value_doc, bias_full, valid_count)

    mixed_heads, log_sums = lax.map(attend_one, (queries, keys_all, values_all, valid_rows))
    mixed_flat = mixed_heads.reshape(all_rows, local_heads * DH)
    after_attn = start_rows + lax.psum_scatter(
        jnp.dot(mixed_flat, w_out, preferred_element_type=jnp.float32),
        "mp",
        scatter_dimension=0,
        tiled=True,
    )
    second_norm = normed(after_attn, gain_two).astype(jnp.bfloat16)
    cot_float = cotangent.astype(jnp.float32)
    gathered_two = lax.all_gather(second_norm, "mp", axis=0, tiled=True)
    gate_vals = jnp.dot(gathered_two, w_gate, preferred_element_type=jnp.float32)
    up_vals = jnp.dot(gathered_two, w_up, preferred_element_type=jnp.float32)
    hidden = gated(gate_vals, up_vals).astype(jnp.bfloat16)
    out_float = after_attn + lax.psum_scatter(
        jnp.dot(hidden, w_down, preferred_element_type=jnp.float32).astype(jnp.bfloat16),
        "mp",
        scatter_dimension=0,
        tiled=True,
    ).astype(jnp.float32)
    shard_rows = lax.all_gather(cotangent, "mp", axis=0, tiled=True)
    hidden_acc = contract(shard_rows, w_down, 1, 1)
    down_sum = contract(hidden, shard_rows, 0, 0)
    unused, pull_gate = jax.vjp(gated, gate_vals, up_vals)
    gate_back, up_back = pull_gate(hidden_acc)
    gate_low = gate_back.astype(jnp.bfloat16)
    up_low = up_back.astype(jnp.bfloat16)
    gate_sum = contract(gathered_two, gate_low, 0, 0)
    up_sum = contract(gathered_two, up_low, 0, 0)
    norm_two_back = lax.psum_scatter(
        contract(gate_low, w_gate, 1, 1) + contract(up_low, w_up, 1, 1),
        "mp",
        scatter_dimension=0,
        tiled=True,
    )
    out_rows = out_float.astype(jnp.bfloat16)
    unused, pull_second = jax.vjp(normed, after_attn, gain_two)
    attn_back_in, gain_two_grad = pull_second(norm_two_back)
    resid_back = cot_float + attn_back_in
    shard_rows = lax.all_gather(resid_back.astype(jnp.bfloat16), "mp", axis=0, tiled=True)
    mixed_acc = contract(shard_rows, w_out, 1, 1)
    out_sum = contract(mixed_flat, shard_rows, 0, 0)
    mixed_low = mixed_acc.astype(jnp.bfloat16).reshape(doc_count, slot_rows, local_heads, DH)

    def attend_back_one(table_acc, inputs):
        query_doc, key_doc, value_doc, grad_doc, sums_doc, valid_count = inputs
        query_doc_back, key_doc_back, value_doc_back, table_doc_back = attend_back(
            query_doc, key_doc, value_doc, grad_doc, sums_doc, bias_full, valid_count
        )
        return (table_acc + table_doc_back, (query_doc_back, key_doc_back, value_doc_back))

    table_sum, (query_back, key_back, value_back) = lax.scan(
        attend_back_one,
        jnp.zeros((BUCKETS, local_heads), jnp.float32),
        (queries, keys_all, values_all, mixed_low, log_sums, valid_rows),
    )
    joint_back = (
        jnp.stack((query_back, key_back, value_back), axis=2)
        .astype(jnp.bfloat16)
        .reshape(all_rows, 3 * local_heads * DH)
    )
    joint_sum = contract(gathered_one, joint_back, 0, 0)
    query_sum, key_sum, value_sum = jnp.split(joint_sum, 3, axis=1)
    norm_one_back = lax.psum_scatter(
        contract(joint_back, w_joint, 1, 1).astype(jnp.bfloat16),
        "mp",
        scatter_dimension=0,
        tiled=True,
    ).astype(jnp.float32)
    unused, pull_first = jax.vjp(normed, start_rows, gain_one)
    start_back, gain_one_grad = pull_first(norm_one_back)
    pooled_back = resid_back + start_back
    full_back = (
        lax.all_gather(shortened(pooled_back), "mp", axis=0, tiled=True)
        .astype(pooled_back.dtype)
        .reshape(doc_count, slot_rows, model_width)
    )

    def pool_back(inputs):
        raw_doc, length, grad_doc = inputs
        unused_rows, pull_pool = jax.vjp(
            lambda raw_in, score_in: pooled(raw_in, score_in, length)[0],
            raw_doc.astype(jnp.float32),
            score_vec,
        )
        return pull_pool(grad_doc)

    raw_backs, score_backs = lax.map(pool_back, (raw_docs, lengths, full_back))
    byte_grad = raw_backs.reshape(doc_count * slot_bytes, model_width).astype(jnp.bfloat16)
    score_sum = jnp.sum(score_backs, axis=0)
    score_part, query_part, key_part, value_part, out_part, gate_part, up_part, down_part = (
        *side_by_side(
            (
                score_sum.astype(jnp.bfloat16),
                query_sum.astype(jnp.bfloat16),
                key_sum.astype(jnp.bfloat16),
                value_sum.astype(jnp.bfloat16),
            ),
            "dp",
            0,
            1,
        ),
        summed_on_arrival(out_sum.astype(jnp.bfloat16), "dp", 1),
        *sent_together((gate_sum.astype(jnp.bfloat16), up_sum.astype(jnp.bfloat16)), "dp", 0, 1),
        summed_on_arrival(down_sum.astype(jnp.bfloat16), "dp", 1),
    )
    gain_one_part, gain_two_part = lax.psum((gain_one_grad, gain_two_grad), ("dp", "mp"))
    table_part, size_total, byte_total = lax.psum(
        (table_sum, jnp.sum(size_mass, axis=0), jnp.sum(lengths).astype(jnp.float32)), "dp"
    )
    size_dist = size_total / byte_total
    return (
        out_rows,
        byte_grad,
        score_part,
        gain_one_part,
        query_part,
        key_part,
        value_part,
        table_part,
        out_part,
        gain_two_part,
        gate_part,
        up_part,
        down_part,
        size_dist,
    )


def solution(mesh):
    placed = (
        P("dp", None),
        P("dp"),
        P(),
        P(),
        P(None, "mp"),
        P(None, "mp"),
        P(None, "mp"),
        P(None, "mp"),
        P("mp", None),
        P(),
        P(None, "mp"),
        P(None, "mp"),
        P("mp", None),
        P(("dp", "mp"), None),
    )
    return jax.shard_map(
        body,
        mesh=mesh,
        in_specs=placed,
        out_specs=(
            P(("dp", "mp"), None),
            P("dp", None),
            P("dp"),
            P(),
            P("dp", "mp"),
            P("dp", "mp"),
            P("dp", "mp"),
            P(None, "mp"),
            P("mp", "dp"),
            P(),
            P("dp", "mp"),
            P("dp", "mp"),
            P("mp", "dp"),
            P(),
        ),
        check_vma=False,
    )
```

```python
import functools

import jax
import jax.numpy as jnp
from jax import lax
from jax.experimental import pallas as pl
from jax.experimental.pallas import tpu as pltpu
from jax.sharding import PartitionSpec as P

DH = 64
BUCKETS = 32
TILE = 128
POOL_BYTES = 384
QUERY_ROWS = 256

epsilon = 1e-06
bucket_edges = (12, 16, 23, 32, 46, 64, 91)
highest = lax.Precision.HIGHEST
f32 = jnp.float32
bf16 = jnp.bfloat16
SMEM = pltpu.SMEM
VMEM = pltpu.VMEM


def bucket_of(offset):
    distance = abs(offset)
    near = distance if distance < 8 else 8 + sum(distance >= edge for edge in bucket_edges)
    return near + (16 if offset > 0 else 0)


def bucket_runs(least, most):
    runs = [(least, bucket_of(least))]
    for offset in range(least + 1, most + 1):
        if bucket_of(offset) != runs[-1][1]:
            runs.append((offset, bucket_of(offset)))
    return runs


def iota(shape, dim):
    return lax.broadcasted_iota(jnp.int32, shape, dim)


def dot(left, right, left_dim=1, right_dim=0, precision=None):
    return lax.dot_general(
        left,
        right,
        (((left_dim,), (right_dim,)), ((), ())),
        precision=precision,
        preferred_element_type=f32,
    )


def two_parts(value):
    high = value.astype(bf16)
    return high, (value - high.astype(f32)).astype(bf16)


def call(kernel, outs, args, in_specs=None, out_specs=None, grid=(), scratch=(), mib=40):
    params = pltpu.CompilerParams(
        vmem_limit_bytes=mib * 2**20,
        dimension_semantics=("arbitrary",) * len(grid) if grid else None,
    )
    options = {}
    if in_specs is not None:
        options["in_specs"] = in_specs
    if out_specs is not None:
        options["out_specs"] = out_specs
    if grid:
        options["grid"] = grid
    return pl.pallas_call(
        kernel,
        out_shape=[jax.ShapeDtypeStruct(shape, dtype) for shape, dtype in outs],
        scratch_shapes=list(scratch),
        compiler_params=params,
        **options,
    )(*args)


def whole(memory_space=VMEM):
    return pl.BlockSpec(memory_space=memory_space)


def block_sums(value):
    count = value.shape[1]
    lane = iota(value.shape, 1)
    sums = [value]
    for b in (2, 3, 4):
        place = lax.rem(lane, b)
        total = value
        for k in range(1, b):
            total = total + jnp.where(lane < count - k, pltpu.roll(value, count - k, 1), 0.0)
        spread = total
        for k in range(1, b):
            spread = jnp.where(place == k, pltpu.roll(total, k, 1), spread)
        sums.append(spread)
    return sums


def by_row(rows):
    shape = (8, rows[0].shape[1])
    place = iota(shape, 0)
    result = jnp.zeros(shape, f32)
    for k, row in enumerate(rows):
        result = jnp.where(place == k, row, result)
    return result


def pair_pick(byte_count, odd):
    shape = (byte_count, byte_count // 2)
    return jnp.where(iota(shape, 0) == 2 * iota(shape, 1) + odd, 1.0, 0.0).astype(f32)


def pool_masks(byte_count):
    byte = iota((byte_count, 1), 0)
    row = iota((1, byte_count // 2), 1)
    return [
        (0, True, False, byte == 2 * row),
        (0, False, True, byte == 2 * row + 1),
        (1, True, True, lax.div(byte, 2) == row),
        (2, True, False, lax.div(byte, 3) == lax.div(2 * row, 3)),
        (2, False, True, lax.div(byte, 3) == lax.div(2 * row + 1, 3)),
        (3, True, True, lax.div(byte, 4) == lax.div(row, 2)),
    ]


def pool_chunks(byte_total):
    return [(at, min(POOL_BYTES, byte_total - at)) for at in range(0, byte_total, POOL_BYTES)]


def near_bias(table_ref, heads, near_ref):
    runs = bucket_runs(-2 * TILE, 2 * TILE)
    for k in range(5):
        offset = TILE * (k - 2) + iota((TILE, TILE), 0) - iota((TILE, TILE), 1)
        values = [jnp.full((TILE, TILE), table_ref[runs[0][1], h], f32) for h in range(heads)]
        for first, bucket in runs[1:]:
            past = offset >= first
            values = [jnp.where(past, table_ref[bucket, h], values[h]) for h in range(heads)]
        for h in range(heads):
            near_ref[(5 * h + k) * TILE : (5 * h + k + 1) * TILE, :] = values[h]


def pool_kernel(
    heads,
    length_ref,
    table_ref,
    x_ref,
    score_ref,
    gain_ref,
    wq_ref,
    wk_ref,
    wv_ref,
    h0_ref,
    n1_ref,
    q_ref,
    k_ref,
    v_ref,
    weight_ref,
    mass_ref,
    high_ref,
    low_ref,
    near_ref,
):
    byte_total, width = x_ref.shape
    length = length_ref[0]
    valid = lax.div(length + 1, 2)
    vector = jnp.broadcast_to(score_ref[...].astype(f32), (16, width)).astype(bf16)
    inside = iota((8, byte_total), 1) < length
    scores = jnp.where(inside, dot(vector, x_ref[...], 1, 1)[:8], 0.0)
    logits = [total / b for b, total in zip((1, 2, 3, 4), block_sums(scores))]
    peak = functools.reduce(jnp.maximum, logits)
    shifted = [jnp.exp(logit - peak) for logit in logits]
    mass = functools.reduce(jnp.add, shifted)
    weights = by_row([s / mass for s in shifted])
    weight_ref[...] = weights
    mass_ref[...] = jnp.broadcast_to(
        jnp.sum(jnp.where(inside, weights, 0.0), axis=1, keepdims=True), mass_ref.shape
    )
    near_bias(table_ref, heads, near_ref)
    own = heads * DH
    padding = q_ref.shape[1] - own
    gain = gain_ref[...].astype(f32)
    for at, count in pool_chunks(byte_total):
        rows = count // 2
        start = at // 2
        local = weights[:, at : at + count]
        even = dot(local, pair_pick(count, 0), precision=highest)
        odd = dot(local, pair_pick(count, 1), precision=highest)
        mixing = jnp.zeros((count, rows), f32)
        for b, for_even, for_odd, mask in pool_masks(count):
            row = even if not for_odd else odd if not for_even else even + odd
            mixing = mixing + jnp.where(mask, row[b : b + 1] / (2 * b + 2), 0.0)
        mixing = jnp.where(iota((count, 1), 0) + at < length, mixing, 0.0)
        high, low = two_parts(mixing)
        high_ref[at : at + count, :rows] = high
        low_ref[at : at + count, :rows] = low
        x = x_ref[at : at + count, :]
        h0 = dot(high, x, 0, 0) + dot(low, x, 0, 0)
        h0_ref[start : start + rows, :] = h0
        scale = lax.rsqrt(jnp.mean(h0 * h0, axis=1, keepdims=True) + epsilon)
        n1 = (h0 * scale * gain).astype(bf16)
        n1_ref[start : start + rows, :] = n1
        q_ref[start : start + rows, :own] = dot(n1, wq_ref[...]).astype(bf16)
        k_ref[start : start + rows, :own] = dot(n1, wk_ref[...]).astype(bf16)
        v_ref[start : start + rows, :own] = dot(n1, wv_ref[...]).astype(bf16)
        first = iota((rows, padding), 1) == 0
        key = iota((rows, padding), 0) + start
        q_ref[start : start + rows, own:] = jnp.where(first, 1.0, 0.0).astype(bf16)
        k_ref[start : start + rows, own:] = jnp.where(
            first & (key >= valid), -1e30, 0.0
        ).astype(bf16)
        v_ref[start : start + rows, own:] = jnp.zeros((rows, padding), bf16)


def pool_forward(length, table, x, score_row, gain_row, wq, wk, wv):
    byte_total, width = x.shape
    rows = byte_total // 2
    heads = wq.shape[1] // DH
    padded = wq.shape[1] + DH
    return call(
        functools.partial(pool_kernel, heads),
        [
            ((rows, width), f32),
            ((rows, width), bf16),
            ((rows, padded), bf16),
            ((rows, padded), bf16),
            ((rows, padded), bf16),
            ((8, byte_total), f32),
            ((8, TILE), f32),
            ((byte_total, POOL_BYTES // 2), bf16),
            ((byte_total, POOL_BYTES // 2), bf16),
            ((5 * heads * TILE, TILE), f32),
        ],
        (length, table, x, score_row, gain_row, wq, wk, wv),
        in_specs=[whole(SMEM), whole(SMEM)] + [whole()] * 6,
    )


def pool_back_kernel(
    length_ref,
    core_ref,
    x_ref,
    score_ref,
    weight_ref,
    high_ref,
    low_ref,
    g0_ref,
    g1_ref,
    g2_ref,
    g3_ref,
    byte_ref,
    grad_ref,
    grad_rows,
    back_ref,
):
    byte_total, width = x_ref.shape
    length = length_ref[0]
    core = core_ref[0]
    quarter = g0_ref.shape[0]
    for chunk, (mine, other) in enumerate(((g0_ref, g1_ref), (g2_ref, g3_ref))):
        base = 2 * quarter * chunk
        grad_rows[pl.ds(pl.multiple_of(base + core * quarter, quarter), quarter), :] = mine[...]
        grad_rows[pl.ds(pl.multiple_of(base + (1 - core) * quarter, quarter), quarter), :] = other[...]
    for at, count in pool_chunks(byte_total):
        rows = count // 2
        x = x_ref[at : at + count, :]
        g = grad_rows[at // 2 : at // 2 + rows, :]
        product = dot(x, g, 1, 1)
        product = jnp.where(iota((count, 1), 0) + at < length, product, 0.0)
        even, odd = [None] * 4, [None] * 4
        for b, for_even, for_odd, mask in pool_masks(count):
            total = jnp.sum(jnp.where(mask, product, 0.0), axis=0, keepdims=True) / (2 * b + 2)
            if for_even:
                even[b] = total
            if for_odd:
                odd[b] = total
        back_ref[:, at : at + count] = dot(
            by_row(even), pair_pick(count, 0), 1, 1, precision=highest
        ) + dot(by_row(odd), pair_pick(count, 1), 1, 1, precision=highest)
    weights = weight_ref[...]
    back = back_ref[...]
    logit_back = weights * (back - jnp.sum(weights * back, axis=0, keepdims=True))
    place = iota(logit_back.shape, 0)
    summed = jnp.zeros_like(logit_back)
    for b, total in enumerate(block_sums(logit_back)):
        summed = summed + jnp.where(place == b, total / (b + 1), 0.0)
    score_back = jnp.sum(summed, axis=0, keepdims=True)
    score_back = jnp.where(iota((1, byte_total), 1) < length, score_back, 0.0)
    high, low = two_parts(score_back)
    place = iota((16, byte_total), 0)
    factors = jnp.where(
        place == 0, high.astype(f32), jnp.where(place == 1, low.astype(f32), 0.0)
    ).astype(bf16)
    vector = jnp.broadcast_to(score_ref[...].astype(f32), (16, width)).astype(bf16)
    score_grad = jnp.zeros((16, width), f32)
    for at, count in pool_chunks(byte_total):
        rows = count // 2
        x = x_ref[at : at + count, :]
        g = grad_rows[at // 2 : at // 2 + rows, :]
        part = factors[:, at : at + count]
        back = dot(high_ref[at : at + count, :rows], g) + dot(low_ref[at : at + count, :rows], g)
        back = back + dot(part, vector, 0, 0)
        byte_ref[at : at + count, :] = back.astype(bf16)
        score_grad = score_grad + dot(part, x)
    grad_ref[...] = jnp.sum(score_grad, axis=0, keepdims=True)


def pool_backward(length, core, x, score_row, weights, high, low, pieces):
    byte_total, width = x.shape
    return call(
        pool_back_kernel,
        [((byte_total, width), bf16), ((1, width), f32)],
        (length, core, x, score_row, weights, high, low, *pieces),
        in_specs=[whole(SMEM), whole(SMEM)] + [whole()] * 9,
        scratch=[VMEM((byte_total // 2, width), bf16), VMEM((8, byte_total), f32)],
    )


def head_lanes(width, first, last, more=None):
    lane = iota((1, width), 1)
    keep = (lane >= first) & (lane < last)
    if more is not None:
        keep = keep | (lane == more)
    return jnp.where(keep, 1.0, 0.0).astype(bf16)


def bias_tile(near_ref, head, key_tile, query_tile):
    place = jnp.clip(key_tile - query_tile + 2, 0, 4)
    return pl.ds(pl.multiple_of((5 * head + place) * TILE, TILE), TILE)


def folded(value, op):
    return op(value.reshape(-1, 8, value.shape[1]), axis=0)


def attend_kernel(heads, first_block, near_ref, q_ref, k_ref, v_ref, mix_ref, sums_ref, vt_ref):
    step = pl.program_id(0)

    @pl.when(step == 0)
    def transposed():
        vt_ref[...] = v_ref[...].T

    own = heads * DH
    q = q_ref[...]
    k = k_ref[...]
    key_rows, width = k.shape
    halves = q.shape[0] // TILE
    mixed = []
    for h in range(heads):
        scores = dot(k, q * head_lanes(width, h * DH, h * DH + DH, own), 1, 1)
        probs, log_sums, masses = [], [], []
        for half in range(halves):
            query_tile = (first_block + step) * halves + half
            tiles, peak = [], None
            for j in range(key_rows // TILE):
                tile = scores[j * TILE : (j + 1) * TILE, half * TILE : (half + 1) * TILE]
                tile = tile + near_ref[bias_tile(near_ref, h, j, query_tile), :]
                top = folded(tile, jnp.max)
                peak = top if peak is None else jnp.maximum(peak, top)
                tiles.append(tile)
            peak = jnp.max(peak, axis=0, keepdims=True)
            mass, column = None, []
            for tile in tiles:
                shifted = jnp.exp(tile - peak)
                part = folded(shifted, jnp.sum)
                mass = part if mass is None else mass + part
                column.append(shifted.astype(bf16))
            mass = jnp.sum(mass, axis=0, keepdims=True)
            probs.append(jnp.concatenate(column, axis=0))
            masses.append(mass)
            log_sums.append(peak + jnp.log(mass))
        prob = jnp.concatenate(probs, axis=1)
        out = dot(vt_ref[h * DH : (h + 1) * DH, :], prob)
        mixed.append(out / jnp.concatenate(masses, axis=1))
        sums_ref[h : h + 1, :] = jnp.concatenate(log_sums, axis=1)
    mixed.append(jnp.zeros((width - own, q.shape[0]), f32))
    mix_ref[...] = jnp.concatenate(mixed, axis=0).T[:, :own].astype(bf16)


def attend(near, q, k, v, first_row, row_count):
    key_rows, width = k.shape
    heads = (width - DH) // DH
    first = first_row // QUERY_ROWS
    full = lambda shape: pl.BlockSpec(shape, lambda i: (0, 0))
    return call(
        functools.partial(attend_kernel, heads, first),
        [((row_count, heads * DH), bf16), ((8, row_count), f32)],
        (near, q, k, v),
        grid=(row_count // QUERY_ROWS,),
        in_specs=[
            full(near.shape),
            pl.BlockSpec((QUERY_ROWS, width), lambda i: (first + i, 0)),
            full(k.shape),
            full(v.shape),
        ],
        out_specs=[
            pl.BlockSpec((QUERY_ROWS, heads * DH), lambda i: (i, 0)),
            pl.BlockSpec((8, QUERY_ROWS), lambda i: (0, i)),
        ],
        scratch=[VMEM((width, key_rows), bf16)],
    )


def attend_back_kernel(
    heads,
    first_block,
    resumed,
    core_ref,
    near_ref,
    sums_ref,
    q_ref,
    k_ref,
    v_ref,
    mine_ref,
    other_ref,
    wo_ref,
    *refs,
):
    if resumed:
        dk_in, dv_in, table_in = refs[:3]
        refs = refs[3:]
    dq_ref, dk_ref, dv_ref, table_ref, kt_ref, rows_ref, mb_ref = refs
    step = pl.program_id(0)
    own = heads * DH

    @pl.when(step == 0)
    def started():
        kt_ref[...] = k_ref[...].T
        if resumed:
            dk_ref[...] = dk_in[...]
            dv_ref[...] = dv_in[...]
            table_ref[...] = table_in[...]
        else:
            dk_ref[...] = jnp.zeros_like(dk_ref)
            dv_ref[...] = jnp.zeros_like(dv_ref)
            table_ref[...] = jnp.zeros_like(table_ref)
        mb_ref[...] = jnp.zeros_like(mb_ref)

    @pl.when(step == core_ref[0])
    def take_mine():
        rows_ref[...] = mine_ref[...]

    @pl.when(step != core_ref[0])
    def take_other():
        rows_ref[...] = other_ref[...]

    mb_ref[:, :own] = dot(rows_ref[...], wo_ref[...], 1, 1).astype(bf16)
    mb = mb_ref[...]
    q = q_ref[...]
    k = k_ref[...]
    v = v_ref[...]
    key_rows, width = k.shape
    halves = q.shape[0] // TILE
    all_probs, all_backs, all_mb, all_q, query_back = [], [], [], [], []
    for h in range(heads):
        only = head_lanes(width, h * DH, h * DH + DH)
        scores = dot(k, q * head_lanes(width, h * DH, h * DH + DH, own), 1, 1)
        own_mb = mb * only
        prob_back = dot(v, own_mb, 1, 1)
        low_columns, back_columns = [], []
        for half in range(halves):
            query_tile = (first_block + step) * halves + half
            lanes = slice(half * TILE, (half + 1) * TILE)
            log_sum = sums_ref[h : h + 1, lanes]
            probs, inner = [], None
            for j in range(key_rows // TILE):
                at = slice(j * TILE, (j + 1) * TILE)
                tile = scores[at, lanes] + near_ref[bias_tile(near_ref, h, j, query_tile), :]
                prob = jnp.exp(tile - log_sum)
                part = folded(prob * prob_back[at, lanes], jnp.sum)
                inner = part if inner is None else inner + part
                probs.append(prob)
            inner = jnp.sum(inner, axis=0, keepdims=True)
            column = []
            for j, prob in enumerate(probs):
                at = slice(j * TILE, (j + 1) * TILE)
                back = (prob * (prob_back[at, lanes] - inner)).astype(bf16)
                table_at = bias_tile(near_ref, h, j, query_tile)
                table_ref[table_at, :] = table_ref[table_at, :] + back.astype(f32)
                column.append(back)
            low_columns.append(jnp.concatenate([p.astype(bf16) for p in probs], axis=0))
            back_columns.append(jnp.concatenate(column, axis=0))
        back = jnp.concatenate(back_columns, axis=1)
        all_probs.append(jnp.concatenate(low_columns, axis=1))
        all_backs.append(back)
        all_mb.append(own_mb)
        all_q.append(q * only)
        query_back.append(dot(kt_ref[h * DH : (h + 1) * DH, :], back))
    dv_ref[...] += dot(jnp.concatenate(all_probs, axis=1), jnp.concatenate(all_mb, axis=0))
    dk_ref[...] += dot(jnp.concatenate(all_backs, axis=1), jnp.concatenate(all_q, axis=0))
    query_back.append(jnp.zeros((width - own, q.shape[0]), f32))
    dq_ref[...] = jnp.concatenate(query_back, axis=0).T[:, :own].astype(bf16)


def attend_back(core, near, sums, q, k, v, mine, other, wo, first_row, kept):
    key_rows, width = k.shape
    heads = (width - DH) // DH
    row_count = mine.shape[0] + other.shape[0]
    first = first_row // QUERY_ROWS
    full = lambda a: pl.BlockSpec(a.shape, lambda i: (0, 0))
    accumulators = [((key_rows, width), f32), ((key_rows, width), f32), (near.shape, f32)]
    return call(
        functools.partial(attend_back_kernel, heads, first, kept is not None),
        [((row_count, heads * DH), bf16), *accumulators],
        (core, near, sums, q, k, v, mine, other, wo, *(kept or ())),
        grid=(row_count // QUERY_ROWS,),
        in_specs=[
            whole(SMEM),
            full(near),
            pl.BlockSpec((8, QUERY_ROWS), lambda i: (0, i)),
            pl.BlockSpec((QUERY_ROWS, width), lambda i: (first + i, 0)),
            full(k),
            full(v),
            full(mine),
            full(other),
            full(wo),
            *[full(a) for a in kept or ()],
        ],
        out_specs=[
            pl.BlockSpec((QUERY_ROWS, heads * DH), lambda i: (i, 0)),
            *[pl.BlockSpec(shape, lambda i: (0, 0)) for shape, _ in accumulators],
        ],
        scratch=[
            VMEM((width, key_rows), bf16),
            VMEM((QUERY_ROWS, mine.shape[1]), bf16),
            VMEM((QUERY_ROWS, width), bf16),
        ],
    )


def join_kernel(core_ref, dqa_ref, dqb_ref, dk_ref, dv_ref, wq_ref, wk_ref, wv_ref, keep_ref, send_ref, dkv_ref):
    core = core_ref[0]
    own = wq_ref.shape[1]
    quarter = keep_ref.shape[1]
    dkv_ref[:, :own] = dk_ref[:, :own].astype(bf16)
    dkv_ref[:, own:] = dv_ref[:, :own].astype(bf16)
    for chunk, dq_ref in enumerate((dqa_ref, dqb_ref)):
        for place, out_ref in ((core, keep_ref), (1 - core, send_ref)):
            local = pl.ds(pl.multiple_of(place * quarter, quarter), quarter)
            rows = pl.ds(pl.multiple_of((2 * chunk + place) * quarter, quarter), quarter)
            total = dot(dq_ref[local, :], wq_ref[...], 1, 1)
            total = total + dot(dkv_ref[rows, :own], wk_ref[...], 1, 1)
            total = total + dot(dkv_ref[rows, own:], wv_ref[...], 1, 1)
            out_ref[chunk] = total.astype(out_ref.dtype)


def join(core, dqa, dqb, dk, dv, wq, wk, wv):
    width, own = wq.shape
    quarter = dqa.shape[0] // 2
    return call(
        join_kernel,
        [
            ((2, quarter, width), f32),
            ((2, quarter, width), bf16),
            ((dk.shape[0], 2 * own), bf16),
        ],
        (core, dqa, dqb, dk, dv, wq, wk, wv),
        in_specs=[whole(SMEM)] + [whole()] * 7,
    )


def gelu_parts(gate):
    factor = (2.0 / jnp.pi) ** 0.5
    square = gate * gate
    bent = jnp.tanh(factor * gate * (1.0 + 0.044715 * square))
    value = 0.5 * gate * (1.0 + bent)
    slope = 0.5 * (1.0 + bent) + 0.5 * gate * (1.0 - bent * bent) * (
        factor * (1.0 + 3 * 0.044715 * square)
    )
    return value, slope


def feed_kernel(
    place_ref,
    h0_ref,
    dy_ref,
    gain_ref,
    wg_ref,
    wu_ref,
    wd_ref,
    m0_ref,
    m1_ref,
    m2_ref,
    m3_ref,
    o0_ref,
    o1_ref,
    o2_ref,
    o3_ref,
    h1_ref,
    n2_ref,
    hidden_ref,
    backs_ref,
    keep_ref,
    send_ref,
    mix_ref,
    out_ref,
):
    place = place_ref[0]
    core = lax.rem(place, 2)
    for d, (m, o) in enumerate(((m0_ref, o0_ref), (m1_ref, o1_ref), (m2_ref, o2_ref), (m3_ref, o3_ref))):
        mix_ref[d] = m[...]
        out_ref[d] = o[...]
    quarter = keep_ref.shape[0]
    units = wg_ref.shape[1]
    gain = gain_ref[...].astype(f32)
    for half, target_ref in ((1 - core, send_ref), (core, keep_ref)):
        rows = pl.ds(pl.multiple_of(half * quarter, quarter), quarter)
        h1 = h0_ref[rows, :]
        for owner in range(4):
            d = lax.bitwise_xor(place, owner)
            h1 = h1 + dot(mix_ref[d, rows, :], out_ref[d])
        h1_ref[rows, :] = h1
        scale = lax.rsqrt(jnp.mean(h1 * h1, axis=1, keepdims=True) + epsilon)
        n2 = (h1 * scale * gain).astype(bf16)
        n2_ref[rows, :] = n2
        gate = dot(n2, wg_ref[...])
        up = dot(n2, wu_ref[...])
        value, slope = gelu_parts(gate)
        hidden_ref[rows, :] = (value * up).astype(bf16)
        hidden_back = dot(dy_ref[rows, :], wd_ref[...], 1, 1)
        gate_back = (hidden_back * up * slope).astype(bf16)
        up_back = (hidden_back * value).astype(bf16)
        backs_ref[rows, :units] = gate_back
        backs_ref[rows, units:] = up_back
        total = dot(gate_back, wg_ref[...], 1, 1) + dot(up_back, wu_ref[...], 1, 1)
        target_ref[...] = total.astype(target_ref.dtype)


def feed(place, h0, dy, gain_row, wg, wu, wd, mixes, outs, chunk):
    rows, width = mixes[0].shape[0], h0.shape[1]
    units = wg.shape[1]
    quarter = rows // 2
    part = pl.BlockSpec((rows, width), lambda i: (chunk, 0))
    return call(
        feed_kernel,
        [
            ((rows, width), f32),
            ((rows, width), bf16),
            ((rows, units), bf16),
            ((rows, 2 * units), bf16),
            ((quarter, width), f32),
            ((quarter, width), bf16),
        ],
        (place, h0, dy, gain_row, wg, wu, wd, *mixes, *outs),
        in_specs=[whole(SMEM), part, part] + [whole()] * 12,
        grid=(1,),
        scratch=[VMEM((4, *mixes[0].shape), bf16), VMEM((4, *outs[0].shape), bf16)],
    )


def feed_grads_kernel(
    core_ref,
    n2a_ref,
    n2b_ref,
    hiddena_ref,
    hiddenb_ref,
    backsa_ref,
    backsb_ref,
    dy_ref,
    wd_ref,
    grads_ref,
    keep_ref,
    send_ref,
):
    core = core_ref[0]
    rows, units = hiddena_ref.shape
    quarter = rows // 2
    grads_ref[:, : 2 * units] = dot(n2a_ref[...], backsa_ref[...], 0, 0) + dot(
        n2b_ref[...], backsb_ref[...], 0, 0
    )
    grads_ref[:, 2 * units :] = dot(dy_ref[:rows, :], hiddena_ref[...], 0, 0) + dot(
        dy_ref[rows:, :], hiddenb_ref[...], 0, 0
    )
    for chunk, hidden_ref in enumerate((hiddena_ref, hiddenb_ref)):
        for half, target_ref in ((core, keep_ref), (1 - core, send_ref)):
            at = pl.ds(pl.multiple_of(half * quarter, quarter), quarter)
            target_ref[chunk] = dot(hidden_ref[at, :], wd_ref[...]).astype(target_ref.dtype)


def feed_grads(core, n2s, hiddens, backs, dy, wd):
    units, width = wd.shape
    quarter = n2s[0].shape[0] // 2
    return call(
        feed_grads_kernel,
        [
            ((width, 3 * units), f32),
            ((2, quarter, width), f32),
            ((2, quarter, width), bf16),
        ],
        (core, *n2s, *hiddens, *backs, dy, wd),
        in_specs=[whole(SMEM)] + [whole()] * 8,
    )


def norm_back_kernel(core_ref, values_ref, gain_ref, added_ref, mine_ref, other_ref, back_ref, low_ref, grad_ref):
    quarter = mine_ref.shape[0]
    core = core_ref[0]

    def rows_of(ref):
        if ref.shape[0] == quarter:
            return ref[...].astype(f32)
        return ref[pl.ds(pl.multiple_of(core * quarter, quarter), quarter), :].astype(f32)

    values = rows_of(values_ref)
    gain = gain_ref[...].astype(f32)
    incoming = mine_ref[...].astype(f32) + other_ref[...].astype(f32)
    scale = lax.rsqrt(jnp.mean(values * values, axis=1, keepdims=True) + epsilon)
    unit = values * scale
    product = incoming * unit
    grad_ref[...] = jnp.sum(product, axis=0, keepdims=True)
    inner = jnp.mean(product * gain, axis=1, keepdims=True)
    back = rows_of(added_ref) + scale * (incoming * gain - unit * inner)
    back_ref[...] = back
    low_ref[...] = back.astype(bf16)


def norm_back(core, values, gain_row, added, mine, other, chunk):
    quarter, width = mine.shape

    def spec(array):
        if array.shape[0] == quarter:
            return whole()
        if array.shape[0] == 2 * quarter:
            return whole()
        return pl.BlockSpec((2 * quarter, width), lambda i: (chunk, 0))

    return call(
        norm_back_kernel,
        [((quarter, width), f32), ((quarter, width), bf16), ((1, width), f32)],
        (core, values, gain_row, added, mine, other),
        in_specs=[whole(SMEM), spec(values), whole(), spec(added), whole(), whole()],
        grid=(1,),
    )


def joint_grads_kernel(
    heads,
    core_ref,
    n1_ref,
    dqa_ref,
    dqb_ref,
    dkv_ref,
    mixa_ref,
    mixb_ref,
    h0_ref,
    h1_ref,
    h2_ref,
    h3_ref,
    tiles_ref,
    grads_ref,
    table_ref,
    rows_ref,
):
    core = core_ref[0]
    rows, own = dqa_ref.shape
    quarter = rows // 2
    for chunk, (mine, other) in enumerate(((h0_ref, h1_ref), (h2_ref, h3_ref))):
        base = 2 * quarter * chunk
        rows_ref[pl.ds(pl.multiple_of(base + core * quarter, quarter), quarter), :] = mine[...]
        rows_ref[pl.ds(pl.multiple_of(base + (1 - core) * quarter, quarter), quarter), :] = other[...]
    grads_ref[:, :own] = dot(n1_ref[:rows, :], dqa_ref[...], 0, 0) + dot(
        n1_ref[rows:, :], dqb_ref[...], 0, 0
    )
    grads_ref[:, own : 3 * own] = dot(n1_ref[...], dkv_ref[...], 0, 0)
    grads_ref[:, 3 * own :] = dot(rows_ref[:rows, :], mixa_ref[...], 0, 0) + dot(
        rows_ref[rows:, :], mixb_ref[...], 0, 0
    )
    bucket = iota((BUCKETS, TILE), 0)
    head = iota((BUCKETS, TILE), 1)
    table = jnp.zeros((BUCKETS, TILE), f32)
    for h in range(heads):
        sums = {}
        for k in range(5):
            least, most = TILE * (k - 2) - TILE + 1, TILE * (k - 2) + TILE - 1
            tile = tiles_ref[(5 * h + k) * TILE : (5 * h + k + 1) * TILE, :]
            if k in (0, 4):
                b = bucket_of(least if k == 0 else most)
                sums[b] = sums.get(b, 0.0) + folded(tile, jnp.sum)
                continue
            offset = TILE * (k - 2) + iota((TILE, TILE), 0) - iota((TILE, TILE), 1)
            runs = bucket_runs(least, most)
            for n, (first, b) in enumerate(runs):
                held = offset >= first
                if n + 1 < len(runs):
                    held = held & (offset < runs[n + 1][0])
                sums[b] = sums.get(b, 0.0) + folded(jnp.where(held, tile, 0.0), jnp.sum)
        for b, part in sums.items():
            total = jnp.sum(jnp.sum(part, axis=0, keepdims=True), axis=1, keepdims=True)
            table = jnp.where((bucket == b) & (head == h), total, table)
    table_ref[...] = table


def joint_grads(core, n1, dqa, dqb, dkv, mixes, lows, tiles):
    width, own = n1.shape[1], dqa.shape[1]
    return call(
        functools.partial(joint_grads_kernel, own // DH),
        [((width, 4 * own), f32), ((BUCKETS, TILE), f32)],
        (core, n1, dqa, dqb, dkv, *mixes, *lows, tiles),
        in_specs=[whole(SMEM)] + [whole()] * 11,
        scratch=[VMEM(n1.shape, bf16)],
    )


def swapped(shard, axis, distance):
    peers = lax.axis_size(axis)
    return lax.ppermute(shard, axis, [(i, i ^ distance) for i in range(peers)])


def gathered(shard):
    far = swapped(shard, "mp", 2)
    near = swapped(shard, "mp", 1)
    return shard, near, far, swapped(far, "mp", 1)


def summed_over(value, axis):
    distance = 1
    while distance < lax.axis_size(axis):
        value = value + swapped(value, axis, distance)
        distance *= 2
    return value


def scattered(partial):
    peers = lax.axis_size("dp")
    me = lax.axis_index("dp")
    blocks = partial.reshape(peers, partial.shape[0] // peers, partial.shape[1])
    distance = 1
    while distance < peers:
        pairs = blocks.reshape(blocks.shape[0] // 2, 2, *blocks.shape[1:])
        bit = lax.rem(lax.div(me, distance), 2)
        kept = lax.dynamic_index_in_dim(pairs, bit, 1, keepdims=False)
        sent = lax.dynamic_index_in_dim(pairs, 1 - bit, 1, keepdims=False)
        blocks = kept + swapped(sent.astype(bf16), "dp", distance).astype(f32)
        distance *= 2
    return blocks[0]


def body(
    byte_embeds,
    lengths,
    score_weight,
    norm1_gain,
    w_query,
    w_key,
    w_value,
    rel_table,
    w_out,
    norm2_gain,
    w_gate,
    w_up,
    w_down,
    cotangent,
):
    width = byte_embeds.shape[1]
    assert lengths.shape[0] == 1 and lax.axis_size("mp") == 4
    quarter = cotangent.shape[0]
    half = 2 * quarter
    heads = w_query.shape[1] // DH
    units = w_gate.shape[1]
    own = heads * DH
    place = lax.axis_index("mp")
    core = lax.rem(place, 2)
    side = lax.div(place, 2)
    place_ref = place.reshape(1)
    core_ref = core.reshape(1)
    score_row = score_weight.reshape(1, width)
    gain_one = norm1_gain.reshape(1, width)
    gain_two = norm2_gain.reshape(1, width)

    outs = gathered(w_out)
    dy = jnp.zeros((4 * quarter, width), bf16)
    for d, piece in enumerate(gathered(cotangent)):
        dy = lax.dynamic_update_slice_in_dim(dy, piece, lax.bitwise_xor(place, d) * quarter, 0)

    h0, n1, q, k, v, weights, masses, high, low, near = pool_forward(
        lengths, rel_table.astype(f32), byte_embeds, score_row, gain_one, w_query, w_key, w_value
    )
    mixes, sums, fed, partial = [], [], [], []
    for chunk in range(2):
        mix, log_sums = attend(near, q, k, v, chunk * half, half)
        mixes.append(mix)
        sums.append(log_sums)
    for chunk in range(2):
        fed.append(
            feed(place_ref, h0, dy, gain_two, w_gate, w_up, w_down, gathered(mixes[chunk]), outs, chunk)
        )
    h1s, n2s, hiddens, backs, keeps, sends = zip(*fed)

    def summed_over_mp(keep, send):
        near_sum = (keep + swapped(send, "mp", 1).astype(f32)).astype(bf16)
        return near_sum, swapped(near_sum, "mp", 2)

    second = [summed_over_mp(keep, send) for keep, send in zip(keeps, sends)]
    feed_sums, out_keep, out_send = feed_grads(core_ref, n2s, hiddens, backs, dy, w_down)

    h1_backs, lows, gain_two_parts, kept, dqs = [], [], [], None, []
    for chunk in range(2):
        h1_back, mine, gain_part = norm_back(
            core_ref, h1s[chunk], gain_two, dy, *second[chunk], chunk
        )
        h1_backs.append(h1_back)
        gain_two_parts.append(gain_part)
        lows += [mine, swapped(mine, "mp", 1)]
    for chunk in range(2):
        dq, *kept = attend_back(
            core_ref, near, sums[chunk], q, k, v, *lows[2 * chunk : 2 * chunk + 2], w_out, chunk * half, kept
        )
        dqs.append(dq)
    dk, dv, tiles = kept
    first_keep, first_send, dkv = join(core_ref, *dqs, dk, dv, w_query, w_key, w_value)
    first = [summed_over_mp(first_keep[chunk], first_send[chunk]) for chunk in range(2)]
    joint_sums, table_sum = joint_grads(core_ref, n1, *dqs, dkv, mixes, lows, tiles)

    gain_one_parts, pieces = [], []
    for chunk in range(2):
        unused, mine, gain_part = norm_back(
            core_ref, h0, gain_one, h1_backs[chunk], *first[chunk], chunk
        )
        gain_one_parts.append(gain_part)
        pieces += [mine, swapped(mine, "mp", 1)]
    byte_grad, score_sum = pool_backward(
        lengths, core_ref, byte_embeds, score_row, weights, high, low, pieces
    )

    feed_part = scattered(feed_sums)
    joint_part = scattered(joint_sums)
    out_near = out_keep + swapped(out_send, "mp", 1).astype(f32)
    out_mine = lax.dynamic_index_in_dim(out_near, side, 0, keepdims=False)
    out_far = lax.dynamic_index_in_dim(out_near, 1 - side, 0, keepdims=False).astype(bf16)
    h1_own = jnp.where(side == 0, h1s[0], h1s[1])
    h1_own = lax.dynamic_slice_in_dim(h1_own, core * quarter, quarter, 0)
    out_rows = (h1_own + out_mine + swapped(out_far, "mp", 2).astype(f32)).astype(bf16)

    gains = jnp.concatenate(
        (gain_one_parts[0] + gain_one_parts[1], gain_two_parts[0] + gain_two_parts[1]), axis=0
    )
    gains = gains + swapped(gains, "mp", 1)
    small = jnp.concatenate((score_sum, gains), axis=0)
    small = summed_over(small, "dp")
    lists = jnp.concatenate(
        (table_sum, masses, jnp.full((8, TILE), lengths[0].astype(f32))), axis=0
    )
    lists = summed_over(lists, "dp")
    table_part = lists[:BUCKETS, :heads]
    size_dist = lists[BUCKETS : BUCKETS + 4, 0] / lists[BUCKETS + 8, 0]
    share = width // lax.axis_size("dp")
    score_part = lax.dynamic_slice_in_dim(small[0], lax.axis_index("dp") * share, share, 0)
    return (
        out_rows,
        byte_grad,
        score_part,
        small[1],
        joint_part[:, :own],
        joint_part[:, own : 2 * own],
        joint_part[:, 2 * own : 3 * own],
        table_part,
        joint_part[:, 3 * own :].T,
        small[2],
        feed_part[:, :units],
        feed_part[:, units : 2 * units],
        feed_part[:, 2 * units :].T,
        size_dist,
    )


def solution(mesh):
    placed = (
        P("dp", None),
        P("dp"),
        P(),
        P(),
        P(None, "mp"),
        P(None, "mp"),
        P(None, "mp"),
        P(None, "mp"),
        P("mp", None),
        P(),
        P(None, "mp"),
        P(None, "mp"),
        P("mp", None),
        P(("dp", "mp"), None),
    )
    return jax.shard_map(
        body,
        mesh=mesh,
        in_specs=placed,
        out_specs=(
            P(("dp", "mp"), None),
            P("dp", None),
            P("dp"),
            P(),
            P("dp", "mp"),
            P("dp", "mp"),
            P("dp", "mp"),
            P(None, "mp"),
            P("mp", "dp"),
            P(),
            P("dp", "mp"),
            P("dp", "mp"),
            P("mp", "dp"),
            P(),
        ),
        check_vma=False,
    )
```

```python
import functools

import jax
import jax.numpy as jnp
from jax import lax
from jax.experimental import pallas as pl
from jax.experimental.pallas import tpu as pltpu
from jax.sharding import PartitionSpec as P

DH = 64
BUCKETS = 32
TILE = 128
POOL_BYTES = 192
QUERY_ROWS = 256

epsilon = 1e-06
bucket_edges = (12, 16, 23, 32, 46, 64, 91)
highest = lax.Precision.HIGHEST
f32 = jnp.float32
bf16 = jnp.bfloat16
SMEM = pltpu.SMEM
VMEM = pltpu.VMEM


def bucket_of(offset):
    distance = abs(offset)
    near = distance if distance < 8 else 8 + sum(distance >= edge for edge in bucket_edges)
    return near + (16 if offset > 0 else 0)


def bucket_runs(least, most):
    runs = [(least, bucket_of(least))]
    for offset in range(least + 1, most + 1):
        if bucket_of(offset) != runs[-1][1]:
            runs.append((offset, bucket_of(offset)))
    return runs


def iota(shape, dim):
    return lax.broadcasted_iota(jnp.int32, shape, dim)


def dot(left, right, left_dim=1, right_dim=0, precision=None):
    return lax.dot_general(
        left,
        right,
        (((left_dim,), (right_dim,)), ((), ())),
        precision=precision,
        preferred_element_type=f32,
    )


def two_parts(value):
    high = value.astype(bf16)
    return high, (value - high.astype(f32)).astype(bf16)


class Held:
    def __init__(self, ref):
        self.ref = self.target = ref

    def upto(self, row):
        return self.ref

    def send(self, *at):
        pass


class Loaded:
    def __init__(self, source, target, semaphores):
        rows = source.shape[0] // len(semaphores)
        self.rows, self.target, self.waited = rows, target, set()
        if len(semaphores) == 1:
            self.copies = [pltpu.make_async_copy(source, target, semaphores[0])]
            return
        self.copies = [
            pltpu.make_async_copy(
                source.at[pl.ds(k * rows, rows)], target.at[pl.ds(k * rows, rows)], semaphore
            )
            for k, semaphore in enumerate(semaphores)
        ]

    def start(self):
        for copy in self.copies:
            copy.start()

    def upto(self, row):
        for k, copy in enumerate(self.copies):
            if k * self.rows < row and k not in self.waited:
                copy.wait()
                self.waited.add(k)
        return self.target

    @property
    def ref(self):
        return self.upto(self.target.shape[0])


class Stored:
    def __init__(self, source, target, semaphores):
        self.ref, self.target, self.semaphores, self.copies = source, target, semaphores, []

    def send(self, *at):
        source, target = (self.ref.at[at], self.target.at[at]) if at else (self.ref, self.target)
        copy = pltpu.make_async_copy(source, target, self.semaphores[len(self.copies)])
        copy.start()
        self.copies.append(copy)


SENDS = 4


def run(body, ins, outs, us, scratch=(), mib=24, after=()):
    loaded = [(array, how) for array, how in ins if isinstance(how, int)]
    copied = [len(out) == 3 for out in outs]
    count, more = len(ins), len(after)

    def kernel(*refs):
        sources = refs[:count]
        targets = refs[count + more : count + more + len(outs)]
        rest = list(refs[count + more + len(outs) :])
        stages = [rest.pop(0) for _ in loaded]
        results = [rest.pop(0) if moved else None for moved in copied]
        load_semaphores, store_semaphores = rest.pop(0), rest.pop(0)
        given, used = [], 0
        for source, (_, how) in zip(sources, ins):
            if how == "vmem":
                given.append(Held(source))
            elif not isinstance(how, int):
                given.append(source)
            else:
                semaphores = [load_semaphores.at[used + k] for k in range(how)]
                given.append(Loaded(source, stages.pop(0), semaphores))
                given[-1].start()
                used += how
        stored = [
            Stored(result, target, [store_semaphores.at[SENDS * k + n] for n in range(SENDS)])
            if moved
            else Held(target)
            for k, (result, target, moved) in enumerate(zip(results, targets, copied))
        ]
        body(given, stored, *rest)
        for array in given:
            if isinstance(array, Loaded):
                array.ref
        for result in stored:
            if isinstance(result, Stored):
                if not result.copies:
                    result.send()
                for copy in result.copies:
                    copy.wait()

    spaces = {"smem": SMEM, "vmem": VMEM, "any": pl.ANY}
    arrays = [
        pltpu.with_memory_space_constraint(array, pltpu.HBM)
        if how == "hbm" or isinstance(how, int)
        else array
        for array, how in ins
    ]
    return pl.pallas_call(
        kernel,
        out_shape=[
            pltpu.HBM(*out[:2]) if moved else jax.ShapeDtypeStruct(*out)
            for out, moved in zip(outs, copied)
        ],
        in_specs=[
            *[pl.BlockSpec(memory_space=spaces.get(how, pltpu.HBM)) for _, how in ins],
            *[pl.BlockSpec(memory_space=pl.ANY)] * more,
        ],
        out_specs=[pl.BlockSpec(memory_space=pltpu.HBM if moved else VMEM) for moved in copied],
        scratch_shapes=[
            *[VMEM(array.shape, array.dtype) for array, _ in loaded],
            *[VMEM(*out[:2]) for out, moved in zip(outs, copied) if moved],
            pltpu.SemaphoreType.DMA((max(1, sum(how for _, how in loaded)),)),
            pltpu.SemaphoreType.DMA((SENDS * len(outs),)),
            *scratch,
        ],
        cost_estimate=pl.CostEstimate(flops=int(us * 1.1e9), transcendentals=0, bytes_accessed=0),
        compiler_params=pltpu.CompilerParams(vmem_limit_bytes=mib * 2**20),
    )(*arrays, *after)


def held(*arrays):
    return [(array, "vmem") for array in arrays]


def started(*copies):
    for copy in copies:
        copy.start()
    return copies


def fetch_owned(pieces, owners, place, target, semaphores):
    waits = []
    for n, owner in enumerate(owners):
        for d, piece in enumerate(pieces):
            pl.when(lax.bitwise_xor(place, d) == owner)(
                pltpu.make_async_copy(piece, target.at[n], semaphores.at[n]).start
            )
        waits.append(pltpu.make_async_copy(pieces[0], target.at[n], semaphores.at[n]))
    return waits


def fetch_pair(core, mine, other, target, at, semaphores):
    return started(
        pltpu.make_async_copy(mine, target.at[at + core], semaphores.at[0]),
        pltpu.make_async_copy(other, target.at[at + 1 - core], semaphores.at[1]),
    )


def rows_at(index, count):
    return pl.ds(pl.multiple_of(index * count, count), count)


def pair_sums(even, odd):
    count = even.shape[1]
    lane = iota(even.shape, 1)

    def after(value, k):
        return jnp.where(lane < count - k, pltpu.roll(value, count - k, 1), 0.0)

    def before(value, k):
        return pltpu.roll(value, k, 1)

    two = even + odd
    first = lax.rem(lane, 2) == 0
    four = two + after(two, 1)
    four = jnp.where(first, four, before(four, 1))
    place = lax.rem(lane, 3)
    early = two + after(even, 1)
    late = after(odd, 1) + after(two, 2)
    far = before(late, 2)
    three_even = jnp.where(place == 0, early, jnp.where(place == 1, before(early, 1), far))
    three_odd = jnp.where(place == 0, early, jnp.where(place == 1, before(late, 1), far))
    return [(even, odd), (two, two), (three_even, three_odd), (four, four)]


def by_row(rows):
    shape = (8, rows[0].shape[1])
    place = iota(shape, 0)
    result = jnp.zeros(shape, f32)
    for k, row in enumerate(rows):
        result = jnp.where(place == k, row, result)
    return result


def pool_masks(byte_count, lanes):
    byte = iota((byte_count, 1), 0)
    row = iota((1, lanes), 1)
    return [
        (0, True, False, byte == 2 * row),
        (0, False, True, byte == 2 * row + 1),
        (1, True, True, lax.div(byte, 2) == row),
        (2, True, False, lax.div(byte, 3) == lax.div(2 * row, 3)),
        (2, False, True, lax.div(byte, 3) == lax.div(2 * row + 1, 3)),
        (3, True, True, lax.div(byte, 4) == lax.div(row, 2)),
    ]


def pool_chunks(byte_total):
    return [(at, min(POOL_BYTES, byte_total - at)) for at in range(0, byte_total, POOL_BYTES)]


def near_bias(table, heads, near_ref):
    runs = bucket_runs(-2 * TILE, 2 * TILE)
    values = [[table[h : h + 1, bucket : bucket + 1] for _, bucket in runs] for h in range(heads)]
    for k in range(5):
        offset = TILE * (k - 2) + iota((TILE, TILE), 0) - iota((TILE, TILE), 1)
        tiles = [jnp.broadcast_to(values[h][0], (TILE, TILE)) for h in range(heads)]
        for n in range(1, len(runs)):
            past = offset >= runs[n][0]
            tiles = [jnp.where(past, values[h][n], tiles[h]) for h in range(heads)]
        for h in range(heads):
            near_ref[(5 * h + k) * TILE : (5 * h + k + 1) * TILE, :] = tiles[h]


def as_row(vector_ref):
    return vector_ref[...].astype(f32).reshape(1, -1)


def byte_scores(parts, vector, scores_ref):
    columns = jnp.broadcast_to(vector, (TILE, vector.shape[1])).T.astype(bf16)
    for part in parts:
        at, x = part()
        scores_ref[at, :] = dot(x, columns)
    half = scores_ref.shape[0] // 2
    return [scores_ref[pl.ds(k, half, stride=2), :].T[:8] for k in range(2)]


X_PARTS = 4
PLACE, GROUP, LENGTH = 0, 1, 2


def pool_body(ins, outs, scores_ref, semaphores):
    spot_ref, table, x, *sources = ins
    h0, n1, q, k, v, weights, masses, mixing, near, *fetched = outs
    copies = started(
        *[
            pltpu.make_async_copy(source, target.ref, semaphores.at[n])
            for n, (source, target) in enumerate(zip(sources, fetched))
        ]
    )
    score_row, gain_row, wq, wk, wv = fetched[:5]
    byte_total, width = x.target.shape
    share = byte_total // X_PARTS
    heads = table.target.shape[0]
    own = heads * DH
    length = spot_ref[LENGTH]
    valid = lax.div(length + 1, 2)
    near_bias(table.ref[...].astype(f32), heads, near.ref)
    for copy in copies[:2]:
        copy.wait()

    def part(n):
        x.upto((n + 1) * share)
        return pl.ds(n * share, share), x.target[n * share : (n + 1) * share, :]

    row = iota((8, byte_total // 2), 1)
    inside = (2 * row < length, 2 * row + 1 < length)
    parts = [functools.partial(part, n) for n in range(X_PARTS)]
    scores = byte_scores(parts, as_row(score_row.ref), scores_ref)
    scores = [jnp.where(known, score, 0.0) for known, score in zip(inside, scores)]
    sums = pair_sums(*scores)
    sized = []
    for odd in range(2):
        logits = [pair[odd] / (b + 1) for b, pair in enumerate(sums)]
        peak = functools.reduce(jnp.maximum, logits)
        shifted = [jnp.exp(logit - peak) for logit in logits]
        mass = functools.reduce(jnp.add, shifted)
        sized.append(by_row([one / mass for one in shifted]))
    weights.ref[:8] = sized[0]
    weights.ref[8:] = sized[1]
    total = sum(
        jnp.sum(jnp.where(known, one, 0.0), axis=1, keepdims=True) for known, one in zip(inside, sized)
    )
    masses.ref[...] = jnp.broadcast_to(total, masses.ref.shape)
    gain = as_row(gain_row.ref)
    for at, count in pool_chunks(byte_total):
        rows = count // 2
        start = at // 2
        blank = jnp.zeros((8, TILE - rows), f32)
        even, odd = [jnp.concatenate((one[:, start : start + rows], blank), axis=1) for one in sized]
        part = jnp.zeros((count, TILE), f32)
        for b, for_even, for_odd, mask in pool_masks(count, TILE):
            line = even if not for_odd else odd if not for_even else even + odd
            part = part + jnp.where(mask, line[b : b + 1] / (2 * b + 2), 0.0)
        part = jnp.where(iota((count, 1), 0) + at < length, part, 0.0)
        both = jnp.concatenate(two_parts(part), axis=1)
        mixing.ref[at : at + count, :] = both
        pooled = dot(both, x.ref[at : at + count, :], 0, 0)
        pooled = pooled[:rows] + pooled[TILE : TILE + rows]
        h0.ref[start : start + rows, :] = pooled
        scale = lax.rsqrt(jnp.mean(pooled * pooled, axis=1, keepdims=True) + epsilon)
        n1.ref[start : start + rows, :] = (pooled * scale * gain).astype(bf16)
    for copy in copies[2:]:
        copy.wait()
    normed = n1.ref[...]
    rows, padding = normed.shape[0], q.ref.shape[1] - own
    first = iota((rows, padding), 1) == 0
    masked = iota((rows, padding), 0) >= valid
    q.ref[:, own:] = jnp.where(first, 1.0, 0.0).astype(bf16)
    k.ref[:, own:] = jnp.where(first & masked, -1e30, 0.0).astype(bf16)
    v.ref[:, own:] = jnp.zeros((rows, padding), bf16)
    for out, weight in ((q, wq), (k, wk), (v, wv)):
        out.ref[:, :own] = dot(normed, weight.ref[...], 1, 1).astype(bf16)
        out.send()


def pool_forward(spot, table, x, *fetched):
    byte_total, width = x.shape
    rows = byte_total // 2
    heads = table.shape[0]
    padded = heads * DH + DH
    return run(
        pool_body,
        [(spot, "smem"), (table, 1), (x, X_PARTS), *[(array, "hbm") for array in fetched]],
        [
            ((rows, width), f32),
            ((rows, width), bf16),
            ((rows, padded), bf16),
            ((rows, padded), bf16),
            ((rows, padded), bf16),
            ((16, rows), f32),
            ((8, TILE), f32),
            ((byte_total, 2 * TILE), bf16),
            ((5 * heads * TILE, TILE), f32),
            *[(array.shape, array.dtype) for array in fetched],
        ],
        us=10,
        scratch=[
            VMEM((byte_total, TILE), f32),
            pltpu.SemaphoreType.DMA((len(fetched),)),
        ],
    )


def pool_scores_body(ins, outs, back_ref, rows_ref, semaphores):
    spot_ref, x, h0, backa, backb, gain, weights, gain_grad, table, masses, *pieces = ins
    factors, small, rows_out = outs
    core = lax.rem(spot_ref[PLACE], 2)
    mine, other = pieces
    waits = [
        fetch_pair(
            core, mine.at[n], other.at[n], rows_ref, 2 * n, semaphores.at[pl.ds(2 * n, 2)]
        )
        for n in range(2)
    ]
    byte_total, width = x.target.shape
    rows_total = byte_total // 2
    quarter = rows_ref.shape[1]
    length = spot_ref[LENGTH]
    gain = as_row(gain.ref)
    grad_rows = rows_out.ref
    gain_sum = jnp.zeros((1, width), f32)
    for chunk, back in enumerate((backa, backb)):
        for copy in waits[chunk]:
            copy.wait()
        for half in range(2):
            n = 2 * chunk + half
            at = slice(n * quarter, (n + 1) * quarter)
            total, added = norm_back(h0.ref[at, :], gain, rows_ref[n])
            gain_sum = gain_sum + added
            total = total + back.ref[half * quarter : (half + 1) * quarter, :]
            grad_rows[at, :] = total.astype(bf16)
    rows_out.send()
    for at, count in pool_chunks(byte_total):
        rows = count // 2
        start = at // 2
        product = dot(x.upto(at + count)[at : at + count, :], grad_rows[start : start + rows, :], 1, 1)
        product = jnp.where(iota((count, 1), 0) + at < length, product, 0.0)
        even, odd = [None] * 4, [None] * 4
        for b, for_even, for_odd, mask in pool_masks(count, rows):
            total = jnp.sum(jnp.where(mask, product, 0.0), axis=0, keepdims=True) / (2 * b + 2)
            if for_even:
                even[b] = total
            if for_odd:
                odd[b] = total
        back_ref[:8, start : start + rows] = by_row(even)
        back_ref[8:, start : start + rows] = by_row(odd)
    logit_back = []
    for odd in range(2):
        weight = weights.ref[8 * odd : 8 * odd + 8, :]
        back = back_ref[8 * odd : 8 * odd + 8, :]
        logit_back.append(weight * (back - jnp.sum(weight * back, axis=0, keepdims=True)))
    place = iota((8, rows_total), 0)
    row = iota((1, rows_total), 1)
    sums = pair_sums(*logit_back)
    lines = []
    for odd in range(2):
        picked = jnp.zeros((8, rows_total), f32)
        for b, pair in enumerate(sums):
            picked = picked + jnp.where(place == b, pair[odd] / (b + 1), 0.0)
        total = jnp.sum(picked, axis=0, keepdims=True)
        lines += two_parts(jnp.where(2 * row + odd < length, total, 0.0))
    place = iota((16, rows_total), 0)
    stacked = jnp.zeros((16, rows_total), f32)
    for k, line in enumerate(lines):
        stacked = jnp.where(place == k, line.astype(f32), stacked)
    stacked = stacked.astype(bf16)
    total = jnp.zeros((16, width), f32)
    for at, count in pool_chunks(byte_total):
        rows = count // 2
        part = stacked[:, at // 2 : at // 2 + rows]
        byte = iota((rows, count), 1)
        row = iota((rows, count), 0)
        picks = [jnp.where(byte == 2 * row + odd, 1.0, 0.0).astype(bf16) for odd in range(2)]
        upper = iota((16, rows), 0) < 2
        zero = jnp.zeros_like(part)
        spread = dot(jnp.where(upper, part.astype(f32), 0.0).astype(bf16), picks[0]) + dot(
            jnp.where(upper, 0.0, part.astype(f32)).astype(bf16), picks[1]
        )
        spread = spread.astype(bf16)
        factors.ref[:, at : at + count] = spread
        total = total + dot(spread, x.ref[at : at + count, :])
    small.ref[0:1, :] = jnp.sum(total, axis=0, keepdims=True)
    small.ref[1:2, :] = gain_sum
    small.ref[2:3, :] = gain_grad.ref[...]
    small.ref[3:, :] = jnp.zeros((5, width), f32)
    lane = iota((1, TILE), 1)
    sizes = jnp.where(lane == 4, length.astype(f32), 0.0)
    for b in range(4):
        sizes = sizes + jnp.where(lane == b, masses.ref[b : b + 1, :], 0.0)
    small.ref[3:4, :TILE] = sizes
    small.ref[4:8, :TILE] = table.ref[:4, :]


def pool_scores(spot, x, h0, backs, gain, weights, gain_grad, table, masses, pieces, after):
    byte_total, width = x.shape
    quarter = pieces[0].shape[1]
    return run(
        pool_scores_body,
        [
            (spot, "smem"),
            (x, X_PARTS),
            *held(h0, *backs, gain, weights, gain_grad, table, masses),
            *[(piece, "any") for piece in pieces],
        ],
        [
            ((16, byte_total), bf16),
            ((8, width), f32),
            ((byte_total // 2, width), bf16),
        ],
        us=6,
        scratch=[
            VMEM((16, byte_total // 2), f32),
            VMEM((4, quarter, width), bf16),
            pltpu.SemaphoreType.DMA((4,)),
        ],
        after=after,
    )


def pool_bytes_body(ins, outs):
    score_row, mixing, factors, grad_rows = [one.ref for one in ins]
    (byte_grad,) = outs
    byte_total, width = byte_grad.ref.shape
    vector = jnp.broadcast_to(as_row(score_row), (16, width)).astype(bf16)
    chunks = pool_chunks(byte_total)
    sent = 0
    for n, (at, count) in enumerate(chunks):
        rows = count // 2
        g = grad_rows[at // 2 : at // 2 + rows, :]
        both = mixing[at : at + count, :]
        back = dot(both[:, :rows], g) + dot(both[:, TILE : TILE + rows], g)
        back = back + dot(factors[:, at : at + count], vector, 0, 0)
        byte_grad.ref[at : at + count, :] = back.astype(bf16)
        if n % 4 == 3 or n + 1 == len(chunks):
            byte_grad.send(pl.ds(sent, at + count - sent))
            sent = at + count


def pool_bytes(score_weight, mixing, factors, grad_rows, after):
    byte_total, width = mixing.shape[0], grad_rows.shape[1]
    return run(
        pool_bytes_body,
        held(score_weight, mixing, factors, grad_rows),
        [((byte_total, width), bf16, "hbm")],
        us=5,
        after=after,
    )


def norm_back(value, gain, incoming):
    incoming = incoming.astype(f32)
    scale = lax.rsqrt(jnp.mean(value * value, axis=1, keepdims=True) + epsilon)
    unit = value * scale
    product = incoming * unit
    inner = jnp.mean(product * gain, axis=1, keepdims=True)
    return scale * (incoming * gain - unit * inner), jnp.sum(product, axis=0, keepdims=True)


def head_lanes(width, first, last, more=None):
    lane = iota((1, width), 1)
    keep = (lane >= first) & (lane < last)
    if more is not None:
        keep = keep | (lane == more)
    return jnp.where(keep, 1.0, 0.0).astype(bf16)


def bias_rows(head, distance):
    place = 5 * head + min(max(distance + 2, 0), 4)
    return slice(place * TILE, (place + 1) * TILE)


def folded(value, op):
    return op(value.reshape(-1, 8, value.shape[1]), axis=0)


def attend_body(heads, first_block, ins, outs, vt_ref):
    q, k, near, v = ins
    mix, sums = outs
    own = heads * DH
    key_rows, width = k.target.shape
    halves = QUERY_ROWS // TILE
    keys = k.ref[...]
    for step in range(mix.ref.shape[0] // QUERY_ROWS):
        first = (first_block + step) * QUERY_ROWS
        queries = q.ref[first : first + QUERY_ROWS, :]
        columns = slice(step * QUERY_ROWS, (step + 1) * QUERY_ROWS)
        mixed = []
        for h in range(heads):
            scores = dot(keys, queries * head_lanes(width, h * DH, h * DH + DH, own), 1, 1)
            probs, log_sums, masses = [], [], []
            for half in range(halves):
                query_tile = first // TILE + half
                tiles, peak = [], None
                for j in range(key_rows // TILE):
                    tile = scores[j * TILE : (j + 1) * TILE, half * TILE : (half + 1) * TILE]
                    tile = tile + near.ref[bias_rows(h, j - query_tile), :]
                    top = folded(tile, jnp.max)
                    peak = top if peak is None else jnp.maximum(peak, top)
                    tiles.append(tile)
                peak = jnp.max(peak, axis=0, keepdims=True)
                mass, column = None, []
                for tile in tiles:
                    shifted = jnp.exp(tile - peak)
                    part = folded(shifted, jnp.sum)
                    mass = part if mass is None else mass + part
                    column.append(shifted.astype(bf16))
                mass = jnp.sum(mass, axis=0, keepdims=True)
                probs.append(jnp.concatenate(column, axis=0))
                masses.append(mass)
                log_sums.append(peak + jnp.log(mass))
            prob = jnp.concatenate(probs, axis=1)
            if step == 0 and h == 0:
                vt_ref[...] = v.ref[...].T
            out = dot(vt_ref[h * DH : (h + 1) * DH, :], prob)
            mixed.append(out / jnp.concatenate(masses, axis=1))
            sums.ref[h : h + 1, columns] = jnp.concatenate(log_sums, axis=1)
        mixed.append(jnp.zeros((width - own, QUERY_ROWS), f32))
        mix.ref[columns, :] = jnp.concatenate(mixed, axis=0).T[:, :own].astype(bf16)
        mix.send(pl.ds(step * QUERY_ROWS, QUERY_ROWS))


def attend(near, q, k, v, first_row, row_count, after):
    key_rows, width = k.shape
    heads = (width - DH) // DH
    return run(
        functools.partial(attend_body, heads, first_row // QUERY_ROWS),
        held(q, k, near, v),
        [((row_count, heads * DH), bf16), ((8, row_count), f32)],
        us=4,
        scratch=[VMEM((width, key_rows), bf16)],
        mib=16,
        after=after,
    )


def attend_back_body(chunk, last, ins, outs, rows_ref, dy_ref, kt_ref, mb_ref, *scratch):
    spot_ref, gain, h1, q, k, near, sums, v, wo, *ins = ins
    if last:
        dk_in, dv_in, tiles_in, gain_in, dqa, wq, wk, wv, *ins = ins
        low, back, gain_out, dq, tiles_out, keep, send, dkv = outs
        dk_ref, dv_ref, *scratch = scratch
    else:
        low, back, gain_out, dq, tiles_out, dk_out, dv_out = outs
        dk_ref, dv_ref = dk_out.ref, dv_out.ref
    (semaphores,) = scratch
    place = spot_ref[PLACE]
    core = lax.rem(place, 2)
    waits = [
        *fetch_pair(core, ins[0], ins[1], rows_ref, 0, semaphores.at[pl.ds(0, 2)]),
        *fetch_owned(ins[2:], (2 * chunk, 2 * chunk + 1), place, dy_ref, semaphores.at[pl.ds(2, 2)]),
    ]
    for copy in waits:
        copy.wait()
    quarter, model = dy_ref.shape[1:]
    gain = as_row(gain.ref)
    gain_sum = gain_in.ref[...] if last else jnp.zeros((1, model), f32)
    for half in range(2):
        at = slice(half * quarter, (half + 1) * quarter)
        total, added = norm_back(h1.ref[at, :], gain, rows_ref[half])
        gain_sum = gain_sum + added
        total = total + dy_ref[half].astype(f32)
        back.ref[at, :] = total
        low.ref[at, :] = total.astype(bf16)
    gain_out.ref[...] = gain_sum
    gain_out.send()
    back.send()
    low.send()

    key_rows, width = k.target.shape
    own = wo.target.shape[0]
    heads = own // DH
    halves = QUERY_ROWS // TILE
    kt_ref[...] = k.ref[...].T
    if last:
        dk_ref, dv_ref = dk_in.ref, dv_in.ref
        tiles_out.ref[...] = tiles_in.ref[...]
    else:
        tiles_out.ref[...] = jnp.zeros_like(tiles_out.ref)
    keys, values = k.ref[...], v.ref[...]
    for step in range(2 * quarter // QUERY_ROWS):
        columns = slice(step * QUERY_ROWS, (step + 1) * QUERY_ROWS)
        first = chunk * 2 * quarter + step * QUERY_ROWS
        queries = q.ref[first : first + QUERY_ROWS, :]
        mb_ref[:, :own] = dot(low.ref[columns, :], wo.ref[...], 1, 1).astype(bf16)
        mb_ref[:, own:] = jnp.zeros((QUERY_ROWS, width - own), bf16)
        mb = mb_ref[...]
        all_probs, all_backs, all_mb, all_q, query_back = [], [], [], [], []
        for h in range(heads):
            only = head_lanes(width, h * DH, h * DH + DH)
            scores = dot(keys, queries * head_lanes(width, h * DH, h * DH + DH, own), 1, 1)
            own_mb = mb * only
            prob_back = dot(values, own_mb, 1, 1)
            low_columns, back_columns = [], []
            for half in range(halves):
                query_tile = first // TILE + half
                lanes = slice(half * TILE, (half + 1) * TILE)
                at = step * QUERY_ROWS + half * TILE
                log_sum = sums.ref[h : h + 1, at : at + TILE]
                probs, inner = [], None
                for j in range(key_rows // TILE):
                    rows = slice(j * TILE, (j + 1) * TILE)
                    tile = scores[rows, lanes] + near.ref[bias_rows(h, j - query_tile), :]
                    prob = jnp.exp(tile - log_sum)
                    part = folded(prob * prob_back[rows, lanes], jnp.sum)
                    inner = part if inner is None else inner + part
                    probs.append(prob)
                inner = jnp.sum(inner, axis=0, keepdims=True)
                column = []
                for j, prob in enumerate(probs):
                    rows = slice(j * TILE, (j + 1) * TILE)
                    score_back = (prob * (prob_back[rows, lanes] - inner)).astype(bf16)
                    table_rows = bias_rows(h, j - query_tile)
                    tiles_out.ref[table_rows, :] += score_back.astype(f32)
                    column.append(score_back)
                low_columns.append(jnp.concatenate([p.astype(bf16) for p in probs], axis=0))
                back_columns.append(jnp.concatenate(column, axis=0))
            score_back = jnp.concatenate(back_columns, axis=1)
            all_probs.append(jnp.concatenate(low_columns, axis=1))
            all_backs.append(score_back)
            all_mb.append(own_mb)
            all_q.append(queries * only)
            query_back.append(dot(kt_ref[h * DH : (h + 1) * DH, :], score_back))
        value_back = dot(jnp.concatenate(all_probs, axis=1), jnp.concatenate(all_mb, axis=0))
        key_back = dot(jnp.concatenate(all_backs, axis=1), jnp.concatenate(all_q, axis=0))
        if last or step:
            dv_ref[...] += value_back
            dk_ref[...] += key_back
        else:
            dv_ref[...] = value_back
            dk_ref[...] = key_back
        query_back.append(jnp.zeros((width - own, QUERY_ROWS), f32))
        dq.ref[columns, :] = jnp.concatenate(query_back, axis=0).T[:, :own].astype(bf16)
    tiles_out.send()
    dq.send()
    if not last:
        return
    dkv.ref[:, :own] = dk_ref[:, :own].astype(bf16)
    dkv.ref[:, own:] = dv_ref[:, :own].astype(bf16)
    dkv.send()
    for place, out in ((1 - core, send), (core, keep)):
        local = rows_at(place, quarter)
        for chunk, query_back in enumerate((dqa, dq)):
            rows = rows_at(2 * chunk + place, quarter)
            total = dot(query_back.ref[local, :], wq.ref[...])
            total = total + dot(dkv.ref[rows, :own], wk.ref[...])
            total = total + dot(dkv.ref[rows, own:], wv.ref[...])
            out.ref[chunk] = total.astype(out.ref.dtype)
        out.send()


def attend_back(spot, gain, h1, q, k, near, sums, v, wo, pieces, cots, chunk, kept=None, after=()):
    key_rows, width = k.shape
    rows, model = h1.shape
    own = wo.shape[0]
    quarter = rows // 2
    last = kept is not None
    outs = [
        ((rows, model), bf16),
        ((rows, model), f32),
        ((1, model), f32),
        ((rows, own), bf16),
        (near.shape, f32),
    ]
    sums_shape = ((key_rows, width), f32)
    if last:
        outs += [
            ((2, quarter, model), f32),
            ((2, quarter, model), bf16),
            ((key_rows, 2 * own), bf16),
        ]
    else:
        outs += [sums_shape, sums_shape]
    return run(
        functools.partial(attend_back_body, chunk, last),
        [
            (spot, "smem"),
            *held(gain, h1, q, k, near, sums, v, wo, *(kept or ())),
            *[(array, "any") for array in (*pieces, *cots)],
        ],
        outs,
        us=12 if last else 10,
        scratch=[
            VMEM((2, quarter, model), bf16),
            VMEM((2, quarter, model), bf16),
            VMEM((width, key_rows), bf16),
            VMEM((QUERY_ROWS, width), bf16),
            *([VMEM(*sums_shape), VMEM(*sums_shape)] if last else []),
            pltpu.SemaphoreType.DMA((4,)),
        ],
        mib=20,
        after=after,
    )


def gelu_parts(gate):
    factor = (2.0 / jnp.pi) ** 0.5
    square = gate * gate
    bent = jnp.tanh(factor * gate * (1.0 + 0.044715 * square))
    value = 0.5 * gate * (1.0 + bent)
    slope = 0.5 * (1.0 + bent) + 0.5 * gate * (1.0 - bent * bent) * (
        factor * (1.0 + 3 * 0.044715 * square)
    )
    return value, slope


def feed_body(chunk, ins, outs, dy_ref, mix_ref, out_ref, semaphores):
    spot_ref, h0, gain, wg, wu, wd, *pieces = ins
    cots, mixes, projections = pieces[:4], pieces[4:8], pieces[8:12]
    h1, n2, hidden, backs, keep, send = [one.ref for one in outs]
    place = spot_ref[PLACE]
    core = lax.rem(place, 2)
    quarter = keep.shape[0]
    rows = 2 * quarter
    units = wg.ref.shape[1]
    copies = []
    for d in range(4):
        owner = lax.bitwise_xor(place, d)
        copies += started(
            pltpu.make_async_copy(mixes[d], mix_ref.at[owner], semaphores.at[2 * d]),
            pltpu.make_async_copy(projections[d], out_ref.at[owner], semaphores.at[1 + 2 * d]),
        )
    owners = (2 * chunk, 2 * chunk + 1)
    more = fetch_owned(cots, owners, place, dy_ref, semaphores.at[pl.ds(8, 2)])
    for copy in copies:
        copy.wait()
    gain = as_row(gain.ref)
    for half in range(2):
        at = slice(half * quarter, (half + 1) * quarter)
        after = h0.ref[chunk * rows + half * quarter : chunk * rows + (half + 1) * quarter, :]
        for owner in range(4):
            after = after + dot(mix_ref[owner, at, :], out_ref[owner])
        h1[at, :] = after
        scale = lax.rsqrt(jnp.mean(after * after, axis=1, keepdims=True) + epsilon)
        n2[at, :] = (after * scale * gain).astype(bf16)
    for copy in more:
        copy.wait()
    for half, target in ((1 - core, send), (core, keep)):
        at = rows_at(half, quarter)
        normed = n2[at, :]
        gate = dot(normed, wg.ref[...])
        up = dot(normed, wu.ref[...])
        value, slope = gelu_parts(gate)
        hidden[at, :] = (value * up).astype(bf16)
        hidden_back = dot(dy_ref[half], wd.ref[...], 1, 1)
        gate_back = (hidden_back * up * slope).astype(bf16)
        up_back = (hidden_back * value).astype(bf16)
        backs[at, :units] = gate_back
        backs[at, units:] = up_back
        total = dot(gate_back, wg.ref[...], 1, 1) + dot(up_back, wu.ref[...], 1, 1)
        target[...] = total.astype(target.dtype)


def feed(spot, h0, cots, gain, wg, wu, wd, mixes, projections, chunk, after):
    rows, width = mixes[0].shape[0], h0.shape[1]
    units = wg.shape[1]
    quarter = rows // 2
    return run(
        functools.partial(feed_body, chunk),
        [
            (spot, "smem"),
            *held(h0, gain, wg, wu, wd),
            *[(array, "any") for array in (*cots, *mixes, *projections)],
        ],
        [
            ((rows, width), f32),
            ((rows, width), bf16),
            ((rows, units), bf16),
            ((rows, 2 * units), bf16),
            ((quarter, width), f32),
            ((quarter, width), bf16),
        ],
        us=6,
        scratch=[
            VMEM((2, quarter, width), bf16),
            VMEM((4, *mixes[0].shape), bf16),
            VMEM((4, *projections[0].shape), bf16),
            pltpu.SemaphoreType.DMA((10,)),
        ],
        after=after,
    )


STREAMS = (1, 2)


def bit_of(spot_ref, distance):
    return lax.rem(lax.div(spot_ref[GROUP], distance), 2)


def split_sums(spot_ref, total_ref, outs):
    if len(outs) == 1:
        outs[0].ref[...] = total_ref[...]
        outs[0].send()
        return
    for n, distance in enumerate(STREAMS):
        keep, send = outs[2 * n : 2 * n + 2]
        pairs, block, columns = keep.ref.shape
        lanes = slice(n * columns, (n + 1) * columns)
        bit = bit_of(spot_ref, distance)
        for t in range(pairs):
            first = t // distance * 2 * distance + t % distance
            send.ref[t] = total_ref[
                rows_at(first + (1 - bit) * distance, block), lanes
            ].astype(bf16)
            keep.ref[t] = total_ref[rows_at(first + bit * distance, block), lanes]
        send.send()
        keep.send()


def sums_outs(width, columns, peers):
    block = width // peers
    if peers >= 4 and block % 16 == 0:
        shape = (peers // 2, block, columns // 2)
        return [(shape, f32, "hbm"), (shape, bf16, "hbm")] * 2
    return [((width, columns), f32, "hbm")]


def feed_grads_body(ins, outs, total_ref):
    spot_ref, n2a, n2b, hiddena, hiddenb, backsa, backsb, wd, *cots = ins
    keep, send = outs[:2]
    place = spot_ref[PLACE]
    core = lax.rem(place, 2)
    quarter = cots[0].target.shape[0]
    units = hiddena.target.shape[1]
    total_ref[:, : 2 * units] = dot(n2a.ref[...], backsa.ref[...], 0, 0) + dot(
        n2b.ref[...], backsb.ref[...], 0, 0
    )
    here = lax.div(place, 2) == 0
    arrays = [one.ref for one in (hiddena, hiddenb, *cots)]
    hiddena, hiddenb, cots = arrays[0], arrays[1], arrays[2:]
    for one, two in ((hiddena, hiddenb), (hiddenb, hiddena)):

        @pl.when(here if one is hiddena else jnp.logical_not(here))
        def summed():
            total = None
            for d, hidden in zip(range(4), (one, one, two, two)):
                at = rows_at(lax.bitwise_xor(core, d % 2), quarter)
                part = dot(cots[d][...], hidden[at, :], 0, 0)
                total = part if total is None else total + part
            total_ref[:, 2 * units :] = total

    split_sums(spot_ref, total_ref, outs[2:])
    for half, target in ((1 - core, send), (core, keep)):
        for chunk, hidden in enumerate((hiddena, hiddenb)):
            target.ref[chunk] = dot(hidden[rows_at(half, quarter), :], wd.ref[...]).astype(
                target.ref.dtype
            )


def feed_grads(spot, n2s, hiddens, backs, wd, cots, peers, after):
    units, width = wd.shape
    quarter = cots[0].shape[0]
    return run(
        feed_grads_body,
        [(spot, "smem"), *held(*n2s, *hiddens, *backs, wd, *cots)],
        [
            ((2, quarter, width), f32),
            ((2, quarter, width), bf16),
            *sums_outs(width, 3 * units, peers),
        ],
        us=6,
        scratch=[VMEM((width, 3 * units), f32)],
        after=after,
    )


def joint_grads_body(heads, ins, outs, total_ref):
    spot_ref, n1, dqa, dqb, dkv, lowa, lowb, mixa, mixb, tiles = ins
    table_out = outs[0]
    rows, own = dqa.target.shape
    total_ref[:, :own] = dot(n1.ref[:rows, :], dqa.ref[...], 0, 0) + dot(
        n1.ref[rows:, :], dqb.ref[...], 0, 0
    )
    total_ref[:, own : 3 * own] = dot(n1.ref[...], dkv.ref[...], 0, 0)
    total_ref[:, 3 * own :] = dot(lowa.ref[...], mixa.ref[...], 0, 0) + dot(
        lowb.ref[...], mixb.ref[...], 0, 0
    )
    split_sums(spot_ref, total_ref, outs[1:])
    head = iota((8, TILE), 0)
    bucket = iota((8, TILE), 1)
    table = jnp.zeros((8, TILE), f32)
    for h in range(heads):
        sums = {}
        for k in range(5):
            least, most = TILE * (k - 2) - TILE + 1, TILE * (k - 2) + TILE - 1
            tile = tiles.ref[(5 * h + k) * TILE : (5 * h + k + 1) * TILE, :]
            if k in (0, 4):
                b = bucket_of(least if k == 0 else most)
                sums[b] = sums.get(b, 0.0) + folded(tile, jnp.sum)
                continue
            offset = TILE * (k - 2) + iota((TILE, TILE), 0) - iota((TILE, TILE), 1)
            runs = bucket_runs(least, most)
            for n, (first, b) in enumerate(runs):
                held = offset >= first
                if n + 1 < len(runs):
                    held = held & (offset < runs[n + 1][0])
                sums[b] = sums.get(b, 0.0) + folded(jnp.where(held, tile, 0.0), jnp.sum)
        for b, part in sums.items():
            total = jnp.sum(jnp.sum(part, axis=0, keepdims=True), axis=1, keepdims=True)
            table = jnp.where((bucket == b) & (head == h), total, table)
    table_out.ref[...] = table


def joint_grads(spot, n1, dqa, dqb, dkv, lows, mixes, tiles, peers, after):
    width, own = n1.shape[1], dqa.shape[1]
    return run(
        functools.partial(joint_grads_body, own // DH),
        [(spot, "smem"), *held(n1, dqa, dqb, dkv, *lows, *mixes, tiles)],
        [((8, TILE), f32), *sums_outs(width, 4 * own, peers)],
        us=6,
        scratch=[VMEM((width, 4 * own), f32)],
        after=after,
    )


def near_sum_body(ins, outs):
    keep, received = ins
    (total,) = outs
    total.ref[...] = (keep.ref[...].astype(f32) + received.ref[...].astype(f32)).astype(bf16)


def near_sum(keep, received, after=()):
    (total,) = run(near_sum_body, held(keep, received), [(keep.shape, bf16)], us=1, mib=4, after=after)
    return total


def pair_sum(mine, other, after=()):
    (total,) = run(near_sum_body, held(mine, other), [(mine.shape, bf16)], us=1, mib=4, after=after)
    return total


def out_split_body(ins, outs):
    spot_ref, keep, received = ins
    mine, far = outs
    side = lax.div(spot_ref[PLACE], 2)
    mine.ref[...] = keep.ref[side] + received.ref[side].astype(f32)
    far.ref[...] = (keep.ref[1 - side] + received.ref[1 - side].astype(f32)).astype(bf16)


def out_split(spot, keep, received, after=()):
    shape = keep.shape[1:]
    ins = [(spot, "smem"), *held(keep, received)]
    return run(out_split_body, ins, [(shape, f32), (shape, bf16)], us=1, mib=4, after=after)


def out_rows_body(ins, outs, rows_ref):
    spot_ref, h1a, h1b, mine, received = ins
    (out,) = outs
    quarter = mine.ref.shape[0]
    side, core = lax.div(spot_ref[PLACE], 2), lax.rem(spot_ref[PLACE], 2)
    for n, h1 in enumerate((h1a, h1b)):

        @pl.when(side == n)
        def taken():
            rows_ref[...] = h1.ref[rows_at(core, quarter), :]

    out.ref[...] = (rows_ref[...] + (mine.ref[...] + received.ref[...].astype(f32))).astype(bf16)


def finished_rows(spot, h1s, mine, received, after=()):
    (rows,) = run(
        out_rows_body,
        [(spot, "smem"), *held(*h1s, mine, received)],
        [(mine.shape, bf16, "hbm")],
        us=1.5,
        scratch=[VMEM(mine.shape, f32)],
        mib=6,
        after=after,
    )
    return rows


def halve_body(distances, ins, outs):
    spot_ref, *ins = ins
    for n, distance in enumerate(distances):
        keep, received = ins[2 * n : 2 * n + 2]
        kept, sent = outs[2 * n : 2 * n + 2]
        bit = bit_of(spot_ref, distance)
        for u in range(kept.ref.shape[0]):
            far = 2 * u + 1 - bit
            sent.ref[u] = (keep.ref[far] + received.ref[far].astype(f32)).astype(bf16)
        sent.send()
        for u in range(kept.ref.shape[0]):
            near = 2 * u + bit
            kept.ref[u] = keep.ref[near] + received.ref[near].astype(f32)
        kept.send()


def halve(spot, distances, sums, after):
    outs = []
    for keep in sums[::2]:
        shape = (keep.shape[0] // 2, *keep.shape[1:])
        outs += [(shape, f32, "hbm"), (shape, bf16, "hbm")]
    return run(
        functools.partial(halve_body, distances),
        [(spot, "smem"), *[(array, 1) for array in sums]],
        outs,
        us=2.5,
        mib=12,
        after=after,
    )


def last_sums_body(plan, ins, outs, total_ref):
    columns = ins[0].target.shape[2]
    for n in range(2):
        keep, received = ins[2 * n : 2 * n + 2]
        total_ref[:, n * columns : (n + 1) * columns] = keep.ref[0] + received.ref[0].astype(f32)
    for out, (first, last, turned) in zip(outs, plan):
        part = total_ref[:, first:last]
        out.ref[...] = part.T if turned else part
        out.send()


def last_sums(plan, sums, after):
    block, columns = sums[0].shape[1:]
    shapes = [(last - first, block) if turned else (block, last - first) for first, last, turned in plan]
    return run(
        functools.partial(last_sums_body, plan),
        [(array, 1) for array in sums],
        [(shape, f32, "hbm") for shape in shapes],
        us=2,
        scratch=[VMEM((block, 2 * columns), f32)],
        mib=6,
        after=after,
    )


def swapped(shard, axis, distance):
    peers = lax.axis_size(axis)
    return lax.ppermute(shard, axis, [(i, i ^ distance) for i in range(peers)])


def gathered(shard):
    far = swapped(shard, "mp", 2)
    near = swapped(shard, "mp", 1)
    return shard, near, far, swapped(far, "mp", 1)


def summed_over(value, axis):
    peers = lax.axis_size(axis)
    if peers <= 4:
        parts = [value] + [swapped(value, axis, d) for d in range(1, peers)]
        while len(parts) > 1:
            parts = [one + two for one, two in zip(parts[::2], parts[1::2])]
        return parts[0]
    distance = 1
    while distance < lax.axis_size(axis):
        value = value + swapped(value, axis, distance)
        distance *= 2
    return value


def scattered(sums):
    peers = lax.axis_size("dp")
    me = lax.axis_index("dp")
    distances = [2**n for n in range(peers.bit_length() - 1)]
    parts = []
    for n, first in enumerate(STREAMS):
        order = sorted(distances, key=lambda d: (d != first, d))
        left = distances[::-1]
        if len(sums) == 4:
            keep, send = sums[2 * n : 2 * n + 2]
            blocks = keep + swapped(send, "dp", first).astype(f32)
            order.pop(0)
            left.remove(first)
        else:
            columns = sums[0].shape[1] // 2
            blocks = sums[0][:, n * columns : (n + 1) * columns]
            blocks = blocks.reshape(peers, -1, columns)
        block, columns = blocks.shape[1:]
        blocks = blocks.reshape(*[2] * len(left), block, columns)
        for distance in order:
            axis = left.index(distance)
            left.remove(distance)
            bit = lax.rem(lax.div(me, distance), 2)
            kept = lax.dynamic_index_in_dim(blocks, bit, axis, keepdims=False)
            sent = lax.dynamic_index_in_dim(blocks, 1 - bit, axis, keepdims=False)
            blocks = kept + swapped(sent.astype(bf16), "dp", distance).astype(f32)
        parts.append(blocks)
    return jnp.concatenate(parts, axis=1)


def body(
    byte_embeds,
    lengths,
    score_weight,
    norm1_gain,
    w_query,
    w_key,
    w_value,
    rel_table,
    w_out,
    norm2_gain,
    w_gate,
    w_up,
    w_down,
    cotangent,
):
    width = byte_embeds.shape[1]
    assert lengths.shape[0] == 1 and lax.axis_size("mp") == 4
    quarter = cotangent.shape[0]
    half = 2 * quarter
    heads = w_query.shape[1] // DH
    units = w_gate.shape[1]
    own = heads * DH
    peers = lax.axis_size("dp")
    spot = jnp.stack([lax.axis_index("mp"), lax.axis_index("dp"), lengths[0]])

    cots = gathered(cotangent)
    projections = gathered(w_out)
    h0, n1, q, k, v, weights, masses, mixing, near, *fetched = pool_forward(
        spot,
        rel_table.T,
        byte_embeds,
        score_weight,
        norm1_gain,
        w_query.T,
        w_key.T,
        w_value.T,
        norm2_gain,
        w_gate,
        w_up,
        w_down,
        w_out,
        cotangent,
    )
    score_vector, gain_one, wq, wk, wv, gain_two, wg, wu, wd, wo, own_rows = fetched
    cots = (own_rows, *cots[1:])
    projections = (wo, *projections[1:])

    mixes, sums = [], []
    order = cots[1:3]
    for chunk in range(2):
        mix, log_sums = attend(near, q, k, v, chunk * half, half, order)
        mixes.append(mix)
        sums.append(log_sums)
        order = [mix, *projections[1:3]]
    order = [mixes[1]]
    fed, second = [], []
    for chunk in range(2):
        mixed = gathered(mixes[chunk])
        *kept, keep, send = feed(
            spot, h0, cots, gain_two, wg, wu, wd, mixed, projections, chunk, order
        )
        mine = near_sum(keep, swapped(send, "mp", 1))
        fed.append(kept)
        second.append((mine, swapped(mine, "mp", 2)))
        order = [mine]
    h1s, n2s, hiddens, backs = zip(*fed)
    out_keep, out_send, *feed_sums = feed_grads(spot, n2s, hiddens, backs, wd, cots, peers, order)
    out_near = swapped(out_send, "mp", 1)

    def received(sums, distances):
        return [
            swapped(sums[k], "dp", distances[k // 2]) if k % 2 else sums[k] for k in range(len(sums))
        ]

    def both(pair, after):
        total = pair_sum(*pair, after)
        return total, swapped(total, "mp", 1)

    def back(chunk, pieces, *more):
        return attend_back(
            spot, gain_two, h1s[chunk], q, k, near, sums[chunk], v, wo, pieces, cots, chunk, *more
        )

    halving = len(feed_sums) == 4 and peers == 8
    lowa, backa, gain_two_sum, dqa, tiles, dk, dv = back(0, both(second[0], [feed_sums[0]]))
    pieces = both(second[1], [lowa])
    out_mine, out_far = out_split(spot, out_keep, out_near, [pieces[0]])
    lowb, backb, gain_two_sum, dqb, tiles, first_keep, first_send, dkv = back(
        1, pieces, (dk, dv, tiles, gain_two_sum, dqa, wq, wk, wv), [out_mine]
    )
    order = [lowb]
    if halving:
        feed_sums = halve(spot, STREAMS[::-1], received(feed_sums, STREAMS), order)
        order = [feed_sums[0]]
    first = near_sum(first_keep, swapped(first_send, "mp", 1), order)
    table_sum, *joint_sums = joint_grads(
        spot, n1, dqa, dqb, dkv, (lowa, lowb), mixes, tiles, peers, [first]
    )
    order = [table_sum]
    feed_plan = ((0, units, False), (units, 2 * units, False), (2 * units, 3 * units, True))
    joint_plan = tuple((n * own, (n + 1) * own, n == 3) for n in range(4))
    if halving:
        feed_sums = halve(spot, (4, 4), received(feed_sums, STREAMS[::-1]), order)
        joint_sums = halve(spot, STREAMS[::-1], received(joint_sums, STREAMS), [feed_sums[0]])
        order = [joint_sums[0]]
    factors, small, grad_rows = pool_scores(
        spot,
        byte_embeds,
        h0,
        (backa, backb),
        gain_one,
        weights,
        gain_two_sum,
        table_sum,
        masses,
        both((first, swapped(first, "mp", 2)), order),
        order,
    )
    order = [small]
    if halving:
        joint_sums = halve(spot, (4, 4), received(joint_sums, STREAMS[::-1]), order)
        order = [joint_sums[0]]
    (byte_grad,) = pool_bytes(score_vector, mixing, factors, grad_rows, order)
    order = [byte_grad]
    if halving:
        feed_parts = last_sums(feed_plan, received(feed_sums, (4, 4)), order)
        order = [feed_parts[0]]
    out_rows = finished_rows(spot, h1s, out_mine, swapped(out_far, "mp", 2), order)
    if halving:
        joint_parts = last_sums(joint_plan, received(joint_sums, (4, 4)), [out_rows])
    else:
        parts = []
        for sums, plan in ((feed_sums, feed_plan), (joint_sums, joint_plan)):
            total = scattered(sums)
            parts.append([total[:, a:b].T if turned else total[:, a:b] for a, b, turned in plan])
        feed_parts, joint_parts = parts
    small = summed_over(small, "dp")
    table_part = small[4 : 4 + heads, :BUCKETS].T
    size_dist = small[3, :4] / small[3, 4]
    share = width // peers
    score_part = lax.dynamic_slice_in_dim(small[0], lax.axis_index("dp") * share, share, 0)
    return (
        out_rows,
        byte_grad,
        score_part,
        small[1],
        *joint_parts[:3],
        table_part,
        joint_parts[3],
        small[2],
        *feed_parts,
        size_dist,
    )


def solution(mesh):
    placed = (
        P("dp", None),
        P("dp"),
        P(),
        P(),
        P(None, "mp"),
        P(None, "mp"),
        P(None, "mp"),
        P(None, "mp"),
        P("mp", None),
        P(),
        P(None, "mp"),
        P(None, "mp"),
        P("mp", None),
        P(("dp", "mp"), None),
    )
    return jax.shard_map(
        body,
        mesh=mesh,
        in_specs=placed,
        out_specs=(
            P(("dp", "mp"), None),
            P("dp", None),
            P("dp"),
            P(),
            P("dp", "mp"),
            P("dp", "mp"),
            P("dp", "mp"),
            P(None, "mp"),
            P("mp", "dp"),
            P(),
            P("dp", "mp"),
            P("dp", "mp"),
            P("mp", "dp"),
            P(),
        ),
        check_vma=False,
    )
```

```python
import functools

import jax
import jax.numpy as jnp
from jax import lax
from jax.experimental import pallas as pl
from jax.experimental.pallas import tpu as pltpu
from jax.sharding import PartitionSpec as P

DH = 64
BUCKETS = 32
TILE = 128
POOL_BYTES = 192
QUERY_ROWS = 256

epsilon = 1e-06
bucket_edges = (12, 16, 23, 32, 46, 64, 91)
highest = lax.Precision.HIGHEST
f32 = jnp.float32
bf16 = jnp.bfloat16
SMEM = pltpu.SMEM
VMEM = pltpu.VMEM


def bucket_of(offset):
    distance = abs(offset)
    near = distance if distance < 8 else 8 + sum(distance >= edge for edge in bucket_edges)
    return near + (16 if offset > 0 else 0)


def bucket_runs(least, most):
    runs = [(least, bucket_of(least))]
    for offset in range(least + 1, most + 1):
        if bucket_of(offset) != runs[-1][1]:
            runs.append((offset, bucket_of(offset)))
    return runs


def iota(shape, dim):
    return lax.broadcasted_iota(jnp.int32, shape, dim)


def dot(left, right, left_dim=1, right_dim=0, precision=None):
    return lax.dot_general(
        left,
        right,
        (((left_dim,), (right_dim,)), ((), ())),
        precision=precision,
        preferred_element_type=f32,
    )


def two_parts(value):
    high = value.astype(bf16)
    return high, (value - high.astype(f32)).astype(bf16)


class Held:
    def __init__(self, ref):
        self.ref = self.target = ref

    def upto(self, row):
        return self.ref

    def send(self, *at):
        pass


class Loaded:
    def __init__(self, source, target, semaphores):
        rows = source.shape[0] // len(semaphores)
        self.rows, self.target, self.waited = rows, target, set()
        if len(semaphores) == 1:
            self.copies = [pltpu.make_async_copy(source, target, semaphores[0])]
            return
        self.copies = [
            pltpu.make_async_copy(
                source.at[pl.ds(k * rows, rows)], target.at[pl.ds(k * rows, rows)], semaphore
            )
            for k, semaphore in enumerate(semaphores)
        ]

    def start(self):
        for copy in self.copies:
            copy.start()

    def upto(self, row):
        for k, copy in enumerate(self.copies):
            if k * self.rows < row and k not in self.waited:
                copy.wait()
                self.waited.add(k)
        return self.target

    @property
    def ref(self):
        return self.upto(self.target.shape[0])


class Stored:
    def __init__(self, source, target, semaphores):
        self.ref, self.target, self.semaphores, self.copies = source, target, semaphores, []

    def send(self, *at):
        source, target = (self.ref.at[at], self.target.at[at]) if at else (self.ref, self.target)
        copy = pltpu.make_async_copy(source, target, self.semaphores[len(self.copies)])
        copy.start()
        self.copies.append(copy)


SENDS = 4


def run(body, ins, outs, us, scratch=(), mib=24, after=()):
    loaded = [(array, how) for array, how in ins if isinstance(how, int)]
    copied = [len(out) == 3 for out in outs]
    count, more = len(ins), len(after)

    def kernel(*refs):
        sources = refs[:count]
        targets = refs[count + more : count + more + len(outs)]
        rest = list(refs[count + more + len(outs) :])
        stages = [rest.pop(0) for _ in loaded]
        results = [rest.pop(0) if moved else None for moved in copied]
        load_semaphores, store_semaphores = rest.pop(0), rest.pop(0)
        given, used = [], 0
        for source, (_, how) in zip(sources, ins):
            if how == "vmem":
                given.append(Held(source))
            elif not isinstance(how, int):
                given.append(source)
            else:
                semaphores = [load_semaphores.at[used + k] for k in range(how)]
                given.append(Loaded(source, stages.pop(0), semaphores))
                given[-1].start()
                used += how
        stored = [
            Stored(result, target, [store_semaphores.at[SENDS * k + n] for n in range(SENDS)])
            if moved
            else Held(target)
            for k, (result, target, moved) in enumerate(zip(results, targets, copied))
        ]
        body(given, stored, *rest)
        for array in given:
            if isinstance(array, Loaded):
                array.ref
        for result in stored:
            if isinstance(result, Stored):
                if not result.copies:
                    result.send()
                for copy in result.copies:
                    copy.wait()

    spaces = {"smem": SMEM, "vmem": VMEM, "any": pl.ANY}
    arrays = [
        pltpu.with_memory_space_constraint(array, pltpu.HBM)
        if how == "hbm" or isinstance(how, int)
        else array
        for array, how in ins
    ]
    return pl.pallas_call(
        kernel,
        out_shape=[
            pltpu.HBM(*out[:2]) if moved else jax.ShapeDtypeStruct(*out)
            for out, moved in zip(outs, copied)
        ],
        in_specs=[
            *[pl.BlockSpec(memory_space=spaces.get(how, pltpu.HBM)) for _, how in ins],
            *[pl.BlockSpec(memory_space=pl.ANY)] * more,
        ],
        out_specs=[pl.BlockSpec(memory_space=pltpu.HBM if moved else VMEM) for moved in copied],
        scratch_shapes=[
            *[VMEM(array.shape, array.dtype) for array, _ in loaded],
            *[VMEM(*out[:2]) for out, moved in zip(outs, copied) if moved],
            pltpu.SemaphoreType.DMA((max(1, sum(how for _, how in loaded)),)),
            pltpu.SemaphoreType.DMA((SENDS * len(outs),)),
            *scratch,
        ],
        cost_estimate=pl.CostEstimate(flops=1, transcendentals=0, bytes_accessed=1),
        compiler_params=pltpu.CompilerParams(vmem_limit_bytes=mib * 2**20),
    )(*arrays, *[pltpu.with_memory_space_constraint(*a) if isinstance(a, tuple) else a for a in after])


def held(*arrays):
    return [(array, "vmem") for array in arrays]


def started(*copies):
    for copy in copies:
        copy.start()
    return copies


def fetch_owned(pieces, owners, place, target, semaphores):
    waits = []
    for n, owner in enumerate(owners):
        for d, piece in enumerate(pieces):
            pl.when(lax.bitwise_xor(place, d) == owner)(
                pltpu.make_async_copy(piece, target.at[n], semaphores.at[n]).start
            )
        waits.append(pltpu.make_async_copy(pieces[0], target.at[n], semaphores.at[n]))
    return waits


def fetch_pair(core, mine, others, target, at, semaphores):
    rows = others[0].shape[0]
    return started(
        pltpu.make_async_copy(mine, target.at[at + core], semaphores.at[0]),
        *[
            pltpu.make_async_copy(
                piece, target.at[at + 1 - core, pl.ds(n * rows, rows)], semaphores.at[1 + n]
            )
            for n, piece in enumerate(others)
        ],
    )


PIECES = 2


def in_pieces(shape):
    return [(shape[0] // PIECES, *shape[1:])] * PIECES


def scatter_pieces(value, pieces):
    rows = pieces[0].ref.shape[0]
    for n, piece in enumerate(pieces):
        piece.ref[...] = value[n * rows : (n + 1) * rows].astype(piece.ref.dtype)


def near_pieces(pieces):
    return [swapped(piece, "mp", 1) for piece in pieces]


def rows_at(index, count):
    return pl.ds(pl.multiple_of(index * count, count), count)


def pair_sums(even, odd):
    count = even.shape[1]
    lane = iota(even.shape, 1)

    def after(value, k):
        return jnp.where(lane < count - k, pltpu.roll(value, count - k, 1), 0.0)

    def before(value, k):
        return pltpu.roll(value, k, 1)

    two = even + odd
    first = lax.rem(lane, 2) == 0
    four = two + after(two, 1)
    four = jnp.where(first, four, before(four, 1))
    place = lax.rem(lane, 3)
    early = two + after(even, 1)
    late = after(odd, 1) + after(two, 2)
    far = before(late, 2)
    three_even = jnp.where(place == 0, early, jnp.where(place == 1, before(early, 1), far))
    three_odd = jnp.where(place == 0, early, jnp.where(place == 1, before(late, 1), far))
    return [(even, odd), (two, two), (three_even, three_odd), (four, four)]


def by_row(rows):
    shape = (8, rows[0].shape[1])
    place = iota(shape, 0)
    result = jnp.zeros(shape, f32)
    for k, row in enumerate(rows):
        result = jnp.where(place == k, row, result)
    return result


def pool_masks(byte_count, lanes):
    byte = iota((byte_count, 1), 0)
    row = iota((1, lanes), 1)
    return [
        (0, True, False, byte == 2 * row),
        (0, False, True, byte == 2 * row + 1),
        (1, True, True, lax.div(byte, 2) == row),
        (2, True, False, lax.div(byte, 3) == lax.div(2 * row, 3)),
        (2, False, True, lax.div(byte, 3) == lax.div(2 * row + 1, 3)),
        (3, True, True, lax.div(byte, 4) == lax.div(row, 2)),
    ]


def pool_chunks(byte_total):
    return [(at, min(POOL_BYTES, byte_total - at)) for at in range(0, byte_total, POOL_BYTES)]


def near_bias(table, heads, near_ref):
    runs = bucket_runs(-2 * TILE, 2 * TILE)
    values = [[table[h : h + 1, bucket : bucket + 1] for _, bucket in runs] for h in range(heads)]
    for k in range(5):
        offset = TILE * (k - 2) + iota((TILE, TILE), 0) - iota((TILE, TILE), 1)
        tiles = [jnp.broadcast_to(values[h][0], (TILE, TILE)) for h in range(heads)]
        for n in range(1, len(runs)):
            past = offset >= runs[n][0]
            tiles = [jnp.where(past, values[h][n], tiles[h]) for h in range(heads)]
        for h in range(heads):
            near_ref[(5 * h + k) * TILE : (5 * h + k + 1) * TILE, :] = tiles[h]


def as_row(vector_ref):
    return vector_ref[...].astype(f32).reshape(1, -1)


def byte_scores(parts, vector, scores_ref):
    columns = jnp.broadcast_to(vector, (TILE, vector.shape[1])).T.astype(bf16)
    for part in parts:
        at, x = part()
        scores_ref[at, :] = dot(x, columns)
    half = scores_ref.shape[0] // 2
    return [scores_ref[pl.ds(k, half, stride=2), :].T[:8] for k in range(2)]


X_PARTS = 4
PLACE, GROUP, LENGTH = 0, 1, 2


def pool_body(ins, outs, scores_ref, semaphores):
    spot_ref, table, x, *sources = ins
    h0, n1, q, k, v, weights, masses, mixing, near, *fetched = outs
    copies = started(
        *[
            pltpu.make_async_copy(source, target.ref, semaphores.at[n])
            for n, (source, target) in enumerate(zip(sources, fetched))
        ]
    )
    score_row, gain_row, wq, wk, wv = fetched[:5]
    byte_total, width = x.target.shape
    share = byte_total // X_PARTS
    heads = table.target.shape[0]
    own = heads * DH
    length = spot_ref[LENGTH]
    valid = lax.div(length + 1, 2)
    near_bias(table.ref[...].astype(f32), heads, near.ref)
    for copy in copies[:2]:
        copy.wait()

    def part(n):
        x.upto((n + 1) * share)
        return pl.ds(n * share, share), x.target[n * share : (n + 1) * share, :]

    row = iota((8, byte_total // 2), 1)
    inside = (2 * row < length, 2 * row + 1 < length)
    parts = [functools.partial(part, n) for n in range(X_PARTS)]
    scores = byte_scores(parts, as_row(score_row.ref), scores_ref)
    scores = [jnp.where(known, score, 0.0) for known, score in zip(inside, scores)]
    sums = pair_sums(*scores)
    sized = []
    for odd in range(2):
        logits = [pair[odd] / (b + 1) for b, pair in enumerate(sums)]
        peak = functools.reduce(jnp.maximum, logits)
        shifted = [jnp.exp(logit - peak) for logit in logits]
        mass = functools.reduce(jnp.add, shifted)
        sized.append(by_row([one / mass for one in shifted]))
    weights.ref[:8] = sized[0]
    weights.ref[8:] = sized[1]
    total = sum(
        jnp.sum(jnp.where(known, one, 0.0), axis=1, keepdims=True) for known, one in zip(inside, sized)
    )
    masses.ref[...] = jnp.broadcast_to(total, masses.ref.shape)
    gain = as_row(gain_row.ref)
    for at, count in pool_chunks(byte_total):
        rows = count // 2
        start = at // 2
        blank = jnp.zeros((8, TILE - rows), f32)
        even, odd = [jnp.concatenate((one[:, start : start + rows], blank), axis=1) for one in sized]
        part = jnp.zeros((count, TILE), f32)
        for b, for_even, for_odd, mask in pool_masks(count, TILE):
            line = even if not for_odd else odd if not for_even else even + odd
            part = part + jnp.where(mask, line[b : b + 1] / (2 * b + 2), 0.0)
        part = jnp.where(iota((count, 1), 0) + at < length, part, 0.0)
        both = jnp.concatenate(two_parts(part), axis=1)
        mixing.ref[at : at + count, :] = both
        pooled = dot(both, x.ref[at : at + count, :], 0, 0)
        pooled = pooled[:rows] + pooled[TILE : TILE + rows]
        h0.ref[start : start + rows, :] = pooled
        scale = lax.rsqrt(jnp.mean(pooled * pooled, axis=1, keepdims=True) + epsilon)
        n1.ref[start : start + rows, :] = (pooled * scale * gain).astype(bf16)
    for copy in copies[2:]:
        copy.wait()
    normed = n1.ref[...]
    rows, padding = normed.shape[0], q.ref.shape[1] - own
    first = iota((rows, padding), 1) == 0
    masked = iota((rows, padding), 0) >= valid
    q.ref[:, own:] = jnp.where(first, 1.0, 0.0).astype(bf16)
    k.ref[:, own:] = jnp.where(first & masked, -1e30, 0.0).astype(bf16)
    v.ref[:, own:] = jnp.zeros((rows, padding), bf16)
    for out, weight in ((q, wq), (k, wk), (v, wv)):
        out.ref[:, :own] = dot(normed, weight.ref[...], 1, 1).astype(bf16)
        out.send()


def pool_forward(spot, table, x, *fetched):
    byte_total, width = x.shape
    rows = byte_total // 2
    heads = table.shape[0]
    padded = heads * DH + DH
    return run(
        pool_body,
        [(spot, "smem"), (table, 1), (x, X_PARTS), *[(array, "hbm") for array in fetched]],
        [
            ((rows, width), f32),
            ((rows, width), bf16),
            ((rows, padded), bf16),
            ((rows, padded), bf16),
            ((rows, padded), bf16),
            ((16, rows), f32),
            ((8, TILE), f32),
            ((byte_total, 2 * TILE), bf16),
            ((5 * heads * TILE, TILE), f32),
            *[(array.shape, array.dtype) for array in fetched],
        ],
        us=10,
        scratch=[
            VMEM((byte_total, TILE), f32),
            pltpu.SemaphoreType.DMA((len(fetched),)),
        ],
    )


def pool_scores_body(ins, outs, back_ref, rows_ref, semaphores):
    spot_ref, x, h0, backa, backb, gain, weights, gain_grad, table, masses, *pieces = ins
    factors, small, rows_out = outs
    core = lax.rem(spot_ref[PLACE], 2)
    each = 1 + PIECES
    waits = [
        fetch_pair(
            core,
            pieces[each * n],
            pieces[each * n + 1 : each * n + each],
            rows_ref,
            2 * n,
            semaphores.at[pl.ds(each * n, each)],
        )
        for n in range(2)
    ]
    byte_total, width = x.target.shape
    rows_total = byte_total // 2
    quarter = rows_ref.shape[1]
    length = spot_ref[LENGTH]
    gain = as_row(gain.ref)
    grad_rows = rows_out.ref
    gain_sum = jnp.zeros((1, width), f32)
    for chunk, back in enumerate((backa, backb)):
        for copy in waits[chunk]:
            copy.wait()
        for half in range(2):
            n = 2 * chunk + half
            at = slice(n * quarter, (n + 1) * quarter)
            total, added = norm_back(h0.ref[at, :], gain, rows_ref[n])
            gain_sum = gain_sum + added
            total = total + back.ref[half * quarter : (half + 1) * quarter, :]
            grad_rows[at, :] = total.astype(bf16)
    rows_out.send()
    for at, count in pool_chunks(byte_total):
        rows = count // 2
        start = at // 2
        product = dot(x.upto(at + count)[at : at + count, :], grad_rows[start : start + rows, :], 1, 1)
        product = jnp.where(iota((count, 1), 0) + at < length, product, 0.0)
        even, odd = [None] * 4, [None] * 4
        for b, for_even, for_odd, mask in pool_masks(count, rows):
            total = jnp.sum(jnp.where(mask, product, 0.0), axis=0, keepdims=True) / (2 * b + 2)
            if for_even:
                even[b] = total
            if for_odd:
                odd[b] = total
        back_ref[:8, start : start + rows] = by_row(even)
        back_ref[8:, start : start + rows] = by_row(odd)
    logit_back = []
    for odd in range(2):
        weight = weights.ref[8 * odd : 8 * odd + 8, :]
        back = back_ref[8 * odd : 8 * odd + 8, :]
        logit_back.append(weight * (back - jnp.sum(weight * back, axis=0, keepdims=True)))
    place = iota((8, rows_total), 0)
    row = iota((1, rows_total), 1)
    sums = pair_sums(*logit_back)
    lines = []
    for odd in range(2):
        picked = jnp.zeros((8, rows_total), f32)
        for b, pair in enumerate(sums):
            picked = picked + jnp.where(place == b, pair[odd] / (b + 1), 0.0)
        total = jnp.sum(picked, axis=0, keepdims=True)
        lines += two_parts(jnp.where(2 * row + odd < length, total, 0.0))
    place = iota((16, rows_total), 0)
    stacked = jnp.zeros((16, rows_total), f32)
    for k, line in enumerate(lines):
        stacked = jnp.where(place == k, line.astype(f32), stacked)
    stacked = stacked.astype(bf16)
    total = jnp.zeros((16, width), f32)
    for at, count in pool_chunks(byte_total):
        rows = count // 2
        part = stacked[:, at // 2 : at // 2 + rows]
        byte = iota((rows, count), 1)
        row = iota((rows, count), 0)
        picks = [jnp.where(byte == 2 * row + odd, 1.0, 0.0).astype(bf16) for odd in range(2)]
        upper = iota((16, rows), 0) < 2
        zero = jnp.zeros_like(part)
        spread = dot(jnp.where(upper, part.astype(f32), 0.0).astype(bf16), picks[0]) + dot(
            jnp.where(upper, 0.0, part.astype(f32)).astype(bf16), picks[1]
        )
        spread = spread.astype(bf16)
        factors.ref[:, at : at + count] = spread
        total = total + dot(spread, x.ref[at : at + count, :])
    small.ref[0:1, :] = jnp.sum(total, axis=0, keepdims=True)
    small.ref[1:2, :] = gain_sum
    small.ref[2:3, :] = gain_grad.ref[...]
    small.ref[3:, :] = jnp.zeros((5, width), f32)
    lane = iota((1, TILE), 1)
    sizes = jnp.where(lane == 4, length.astype(f32), 0.0)
    for b in range(4):
        sizes = sizes + jnp.where(lane == b, masses.ref[b : b + 1, :], 0.0)
    small.ref[3:4, :TILE] = sizes
    small.ref[4:8, :TILE] = table.ref[:4, :]


def pool_scores(spot, x, h0, backs, gain, weights, gain_grad, table, masses, pieces, after):
    byte_total, width = x.shape
    quarter = pieces[0].shape[0]
    return run(
        pool_scores_body,
        [
            (spot, "smem"),
            (x, X_PARTS),
            *held(h0, *backs, gain, weights, gain_grad, table, masses),
            *[(piece, "any") for piece in pieces],
        ],
        [
            ((16, byte_total), bf16),
            ((8, width), f32),
            ((byte_total // 2, width), bf16),
        ],
        us=6,
        scratch=[
            VMEM((16, byte_total // 2), f32),
            VMEM((4, quarter, width), bf16),
            pltpu.SemaphoreType.DMA((2 + 2 * PIECES,)),
        ],
        after=after,
    )


def pool_bytes_body(ins, outs):
    score_row, mixing, factors, grad_rows = [one.ref for one in ins]
    (byte_grad,) = outs
    byte_total, width = byte_grad.ref.shape
    vector = jnp.broadcast_to(as_row(score_row), (16, width)).astype(bf16)
    chunks = pool_chunks(byte_total)
    sent = 0
    for n, (at, count) in enumerate(chunks):
        rows = count // 2
        g = grad_rows[at // 2 : at // 2 + rows, :]
        both = mixing[at : at + count, :]
        back = dot(both[:, :rows], g) + dot(both[:, TILE : TILE + rows], g)
        back = back + dot(factors[:, at : at + count], vector, 0, 0)
        byte_grad.ref[at : at + count, :] = back.astype(bf16)
        if n % 4 == 3 or n + 1 == len(chunks):
            byte_grad.send(pl.ds(sent, at + count - sent))
            sent = at + count


def pool_bytes(score_weight, mixing, factors, grad_rows, after):
    byte_total, width = mixing.shape[0], grad_rows.shape[1]
    return run(
        pool_bytes_body,
        held(score_weight, mixing, factors, grad_rows),
        [((byte_total, width), bf16, "hbm")],
        us=5,
        after=after,
    )


def norm_back(value, gain, incoming):
    incoming = incoming.astype(f32)
    scale = lax.rsqrt(jnp.mean(value * value, axis=1, keepdims=True) + epsilon)
    unit = value * scale
    product = incoming * unit
    inner = jnp.mean(product * gain, axis=1, keepdims=True)
    return scale * (incoming * gain - unit * inner), jnp.sum(product, axis=0, keepdims=True)


def head_lanes(width, first, last, more=None):
    lane = iota((1, width), 1)
    keep = (lane >= first) & (lane < last)
    if more is not None:
        keep = keep | (lane == more)
    return jnp.where(keep, 1.0, 0.0).astype(bf16)


def bias_rows(head, distance):
    place = 5 * head + min(max(distance + 2, 0), 4)
    return slice(place * TILE, (place + 1) * TILE)


def folded(value, op):
    return op(value.reshape(-1, 8, value.shape[1]), axis=0)


def attend_body(heads, first_block, ins, outs, vt_ref, semaphores):
    q, k, near, v, *passed = ins
    mix, sums, *copied = outs
    copies = started(
        *[
            pltpu.make_async_copy(source, target.ref, semaphores.at[n])
            for n, (source, target) in enumerate(zip(passed, copied))
        ]
    )
    own = heads * DH
    key_rows, width = k.target.shape
    halves = QUERY_ROWS // TILE
    keys = k.ref[...]
    for step in range(mix.ref.shape[0] // QUERY_ROWS):
        first = (first_block + step) * QUERY_ROWS
        queries = q.ref[first : first + QUERY_ROWS, :]
        columns = slice(step * QUERY_ROWS, (step + 1) * QUERY_ROWS)
        mixed = []
        for h in range(heads):
            scores = dot(keys, queries * head_lanes(width, h * DH, h * DH + DH, own), 1, 1)
            probs, log_sums, masses = [], [], []
            for half in range(halves):
                query_tile = first // TILE + half
                tiles, peak = [], None
                for j in range(key_rows // TILE):
                    tile = scores[j * TILE : (j + 1) * TILE, half * TILE : (half + 1) * TILE]
                    tile = tile + near.ref[bias_rows(h, j - query_tile), :]
                    top = folded(tile, jnp.max)
                    peak = top if peak is None else jnp.maximum(peak, top)
                    tiles.append(tile)
                peak = jnp.max(peak, axis=0, keepdims=True)
                mass, column = None, []
                for tile in tiles:
                    shifted = jnp.exp(tile - peak)
                    part = folded(shifted, jnp.sum)
                    mass = part if mass is None else mass + part
                    column.append(shifted.astype(bf16))
                mass = jnp.sum(mass, axis=0, keepdims=True)
                probs.append(jnp.concatenate(column, axis=0))
                masses.append(mass)
                log_sums.append(peak + jnp.log(mass))
            prob = jnp.concatenate(probs, axis=1)
            if step == 0 and h == 0:
                vt_ref[...] = v.ref[...].T
            out = dot(vt_ref[h * DH : (h + 1) * DH, :], prob)
            mixed.append(out / jnp.concatenate(masses, axis=1))
            sums.ref[h : h + 1, columns] = jnp.concatenate(log_sums, axis=1)
        mixed.append(jnp.zeros((width - own, QUERY_ROWS), f32))
        mix.ref[columns, :] = jnp.concatenate(mixed, axis=0).T[:, :own].astype(bf16)
    for copy in copies:
        copy.wait()


def attend(near, q, k, v, first_row, row_count, after, passed=()):
    key_rows, width = k.shape
    heads = (width - DH) // DH
    return run(
        functools.partial(attend_body, heads, first_row // QUERY_ROWS),
        [*held(q, k, near, v), *[(array, "any") for array in passed]],
        [
            ((row_count, heads * DH), bf16),
            ((8, row_count), f32),
            *[(array.shape, array.dtype) for array in passed],
        ],
        us=4,
        scratch=[
            VMEM((width, key_rows), bf16),
            pltpu.SemaphoreType.DMA((max(1, len(passed)),)),
        ],
        mib=16,
        after=after,
    )


def attend_back_body(chunk, last, ins, outs, rows_ref, dy_ref, kt_ref, mb_ref, *scratch):
    spot_ref, gain, h1, q, k, near, sums, v, wo, *ins = ins
    if last:
        dk_in, dv_in, tiles_in, gain_in, dqa, wq, wk, wv, *ins = ins
        low, back, gain_out, dq, tiles_out, keepa, keepb, dkv, *sends = outs
        dk_ref, dv_ref, *scratch = scratch
    else:
        low, back, gain_out, dq, tiles_out, dk_out, dv_out = outs
        dk_ref, dv_ref = dk_out.ref, dv_out.ref
    (semaphores,) = scratch
    place = spot_ref[PLACE]
    core = lax.rem(place, 2)
    waits = [
        *fetch_pair(core, ins[0], ins[1 : 1 + PIECES], rows_ref, 0, semaphores.at[pl.ds(2, 1 + PIECES)]),
        *fetch_owned(
            ins[1 + PIECES :], (2 * chunk, 2 * chunk + 1), place, dy_ref, semaphores.at[pl.ds(0, 2)]
        ),
    ]
    for copy in waits:
        copy.wait()
    quarter, model = dy_ref.shape[1:]
    gain = as_row(gain.ref)
    gain_sum = gain_in.ref[...] if last else jnp.zeros((1, model), f32)
    for half in range(2):
        at = slice(half * quarter, (half + 1) * quarter)
        total, added = norm_back(h1.ref[at, :], gain, rows_ref[half])
        gain_sum = gain_sum + added
        total = total + dy_ref[half].astype(f32)
        back.ref[at, :] = total
        low.ref[at, :] = total.astype(bf16)
    gain_out.ref[...] = gain_sum
    gain_out.send()
    back.send()
    low.send()

    key_rows, width = k.target.shape
    own = wo.target.shape[0]
    heads = own // DH
    halves = QUERY_ROWS // TILE
    kt_ref[...] = k.ref[...].T
    if last:
        dk_ref, dv_ref = dk_in.ref, dv_in.ref
        tiles_out.ref[...] = tiles_in.ref[...]
    else:
        tiles_out.ref[...] = jnp.zeros_like(tiles_out.ref)
    keys, values = k.ref[...], v.ref[...]
    for step in range(2 * quarter // QUERY_ROWS):
        columns = slice(step * QUERY_ROWS, (step + 1) * QUERY_ROWS)
        first = chunk * 2 * quarter + step * QUERY_ROWS
        queries = q.ref[first : first + QUERY_ROWS, :]
        mb_ref[:, :own] = dot(low.ref[columns, :], wo.ref[...], 1, 1).astype(bf16)
        mb_ref[:, own:] = jnp.zeros((QUERY_ROWS, width - own), bf16)
        mb = mb_ref[...]
        all_probs, all_backs, all_mb, all_q, query_back = [], [], [], [], []
        for h in range(heads):
            only = head_lanes(width, h * DH, h * DH + DH)
            scores = dot(keys, queries * head_lanes(width, h * DH, h * DH + DH, own), 1, 1)
            own_mb = mb * only
            prob_back = dot(values, own_mb, 1, 1)
            low_columns, back_columns = [], []
            for half in range(halves):
                query_tile = first // TILE + half
                lanes = slice(half * TILE, (half + 1) * TILE)
                at = step * QUERY_ROWS + half * TILE
                log_sum = sums.ref[h : h + 1, at : at + TILE]
                probs, inner = [], None
                for j in range(key_rows // TILE):
                    rows = slice(j * TILE, (j + 1) * TILE)
                    tile = scores[rows, lanes] + near.ref[bias_rows(h, j - query_tile), :]
                    prob = jnp.exp(tile - log_sum)
                    part = folded(prob * prob_back[rows, lanes], jnp.sum)
                    inner = part if inner is None else inner + part
                    probs.append(prob)
                inner = jnp.sum(inner, axis=0, keepdims=True)
                column = []
                for j, prob in enumerate(probs):
                    rows = slice(j * TILE, (j + 1) * TILE)
                    score_back = (prob * (prob_back[rows, lanes] - inner)).astype(bf16)
                    table_rows = bias_rows(h, j - query_tile)
                    tiles_out.ref[table_rows, :] += score_back.astype(f32)
                    column.append(score_back)
                low_columns.append(jnp.concatenate([p.astype(bf16) for p in probs], axis=0))
                back_columns.append(jnp.concatenate(column, axis=0))
            score_back = jnp.concatenate(back_columns, axis=1)
            all_probs.append(jnp.concatenate(low_columns, axis=1))
            all_backs.append(score_back)
            all_mb.append(own_mb)
            all_q.append(queries * only)
            query_back.append(dot(kt_ref[h * DH : (h + 1) * DH, :], score_back))
        value_back = dot(jnp.concatenate(all_probs, axis=1), jnp.concatenate(all_mb, axis=0))
        key_back = dot(jnp.concatenate(all_backs, axis=1), jnp.concatenate(all_q, axis=0))
        if last or step:
            dv_ref[...] += value_back
            dk_ref[...] += key_back
        else:
            dv_ref[...] = value_back
            dk_ref[...] = key_back
        query_back.append(jnp.zeros((width - own, QUERY_ROWS), f32))
        dq.ref[columns, :] = jnp.concatenate(query_back, axis=0).T[:, :own].astype(bf16)
    tiles_out.send()
    dq.send()
    if not last:
        return
    dkv.ref[:, :own] = dk_ref[:, :own].astype(bf16)
    dkv.ref[:, own:] = dv_ref[:, :own].astype(bf16)
    dkv.send()
    for place, sent in ((1 - core, True), (core, False)):
        local = rows_at(place, quarter)
        for chunk, query_back in enumerate((dqa, dq)):
            rows = rows_at(2 * chunk + place, quarter)
            total = dot(query_back.ref[local, :], wq.ref[...])
            total = total + dot(dkv.ref[rows, :own], wk.ref[...])
            total = total + dot(dkv.ref[rows, own:], wv.ref[...])
            if sent:
                scatter_pieces(total, sends[PIECES * chunk : PIECES * (chunk + 1)])
            else:
                (keepa, keepb)[chunk].ref[...] = total


def attend_back(spot, gain, h1, q, k, near, sums, v, wo, pieces, cots, chunk, kept=None, after=()):
    key_rows, width = k.shape
    rows, model = h1.shape
    own = wo.shape[0]
    quarter = rows // 2
    last = kept is not None
    outs = [
        ((rows, model), bf16),
        ((rows, model), f32),
        ((1, model), f32),
        ((rows, own), bf16),
        (near.shape, f32),
    ]
    sums_shape = ((key_rows, width), f32)
    if last:
        outs += [
            ((quarter, model), f32),
            ((quarter, model), f32),
            ((key_rows, 2 * own), bf16),
            *[(shape, bf16) for shape in 2 * in_pieces((quarter, model))],
        ]
    else:
        outs += [sums_shape, sums_shape]
    return run(
        functools.partial(attend_back_body, chunk, last),
        [
            (spot, "smem"),
            *held(gain, h1, q, k, near, sums, v, wo, *(kept or ())),
            *[(array, "any") for array in (*pieces, *cots)],
        ],
        outs,
        us=12 if last else 10,
        scratch=[
            VMEM((2, quarter, model), bf16),
            VMEM((2, quarter, model), bf16),
            VMEM((width, key_rows), bf16),
            VMEM((QUERY_ROWS, width), bf16),
            *([VMEM(*sums_shape), VMEM(*sums_shape)] if last else []),
            pltpu.SemaphoreType.DMA((3 + PIECES,)),
        ],
        mib=20,
        after=after,
    )


def gelu_parts(gate):
    factor = (2.0 / jnp.pi) ** 0.5
    square = gate * gate
    bent = jnp.tanh(factor * gate * (1.0 + 0.044715 * square))
    value = 0.5 * gate * (1.0 + bent)
    slope = 0.5 * (1.0 + bent) + 0.5 * gate * (1.0 - bent * bent) * (
        factor * (1.0 + 3 * 0.044715 * square)
    )
    return value, slope


def feed_body(chunk, ins, outs, dy_ref, mix_ref, out_ref, semaphores):
    spot_ref, h0, gain, wg, wu, wd, *pieces = ins
    cots, mixes, projections = pieces[:4], pieces[4:8], pieces[8:12]
    h1, n2, hidden, backs, keep = [one.ref for one in outs[:5]]
    send = outs[5:]
    place = spot_ref[PLACE]
    core = lax.rem(place, 2)
    quarter = keep.shape[0]
    rows = 2 * quarter
    units = wg.ref.shape[1]
    copies = []
    for d in range(4):
        owner = lax.bitwise_xor(place, d)
        copies += started(
            pltpu.make_async_copy(mixes[d], mix_ref.at[owner], semaphores.at[2 * d]),
            pltpu.make_async_copy(projections[d], out_ref.at[owner], semaphores.at[1 + 2 * d]),
        )
    owners = (2 * chunk, 2 * chunk + 1)
    more = fetch_owned(cots, owners, place, dy_ref, semaphores.at[pl.ds(8, 2)])
    for copy in copies:
        copy.wait()
    gain = as_row(gain.ref)
    for half in range(2):
        at = slice(half * quarter, (half + 1) * quarter)
        after = h0.ref[chunk * rows + half * quarter : chunk * rows + (half + 1) * quarter, :]
        for owner in range(4):
            after = after + dot(mix_ref[owner, at, :], out_ref[owner])
        h1[at, :] = after
        scale = lax.rsqrt(jnp.mean(after * after, axis=1, keepdims=True) + epsilon)
        n2[at, :] = (after * scale * gain).astype(bf16)
    for copy in more:
        copy.wait()
    for half, target in ((1 - core, send), (core, keep)):
        at = rows_at(half, quarter)
        normed = n2[at, :]
        gate = dot(normed, wg.ref[...])
        up = dot(normed, wu.ref[...])
        value, slope = gelu_parts(gate)
        hidden[at, :] = (value * up).astype(bf16)
        hidden_back = dot(dy_ref[half], wd.ref[...], 1, 1)
        gate_back = (hidden_back * up * slope).astype(bf16)
        up_back = (hidden_back * value).astype(bf16)
        backs[at, :units] = gate_back
        backs[at, units:] = up_back
        total = dot(gate_back, wg.ref[...], 1, 1) + dot(up_back, wu.ref[...], 1, 1)
        if target is send:
            scatter_pieces(total, send)
        else:
            keep[...] = total


def feed(spot, h0, cots, gain, wg, wu, wd, mixes, projections, chunk, after):
    rows, width = mixes[0].shape[0], h0.shape[1]
    units = wg.shape[1]
    quarter = rows // 2
    return run(
        functools.partial(feed_body, chunk),
        [
            (spot, "smem"),
            *held(h0, gain, wg, wu, wd),
            *[(array, "any") for array in (*cots, *mixes, *projections)],
        ],
        [
            ((rows, width), f32),
            ((rows, width), bf16),
            ((rows, units), bf16),
            ((rows, 2 * units), bf16),
            ((quarter, width), f32),
            *[(shape, bf16) for shape in in_pieces((quarter, width))],
        ],
        us=6,
        scratch=[
            VMEM((2, quarter, width), bf16),
            VMEM((4, *mixes[0].shape), bf16),
            VMEM((4, *projections[0].shape), bf16),
            pltpu.SemaphoreType.DMA((10,)),
        ],
        after=after,
    )


STREAMS = (1, 2)


def bit_of(spot_ref, distance):
    return lax.rem(lax.div(spot_ref[GROUP], distance), 2)


def split_sums(spot_ref, total_ref, outs):
    if len(outs) == 1:
        outs[0].ref[...] = total_ref[...]
        outs[0].send()
        return
    for n, distance in enumerate(STREAMS):
        keep, send = outs[2 * n : 2 * n + 2]
        pairs, block, columns = keep.ref.shape
        lanes = slice(n * columns, (n + 1) * columns)
        bit = bit_of(spot_ref, distance)
        for t in range(pairs):
            first = t // distance * 2 * distance + t % distance
            send.ref[t] = total_ref[
                rows_at(first + (1 - bit) * distance, block), lanes
            ].astype(bf16)
            keep.ref[t] = total_ref[rows_at(first + bit * distance, block), lanes]
        send.send()
        keep.send()


def sums_outs(width, columns, peers):
    block = width // peers
    if peers >= 4 and block % 16 == 0:
        shape = (peers // 2, block, columns // 2)
        return [(shape, f32), (shape, bf16)] * 2
    return [((width, columns), f32, "hbm")]


def feed_grads_body(ins, outs, total_ref):
    spot_ref, n2a, n2b, hiddena, hiddenb, backsa, backsb, wd, *cots = ins
    keep, send = outs[:2]
    place = spot_ref[PLACE]
    core = lax.rem(place, 2)
    quarter = cots[0].target.shape[0]
    units = hiddena.target.shape[1]
    total_ref[:, : 2 * units] = dot(n2a.ref[...], backsa.ref[...], 0, 0) + dot(
        n2b.ref[...], backsb.ref[...], 0, 0
    )
    here = lax.div(place, 2) == 0
    arrays = [one.ref for one in (hiddena, hiddenb, *cots)]
    hiddena, hiddenb, cots = arrays[0], arrays[1], arrays[2:]
    for one, two in ((hiddena, hiddenb), (hiddenb, hiddena)):

        @pl.when(here if one is hiddena else jnp.logical_not(here))
        def summed():
            total = None
            for d, hidden in zip(range(4), (one, one, two, two)):
                at = rows_at(lax.bitwise_xor(core, d % 2), quarter)
                part = dot(cots[d][...], hidden[at, :], 0, 0)
                total = part if total is None else total + part
            total_ref[:, 2 * units :] = total

    split_sums(spot_ref, total_ref, outs[2:])
    for half, target in ((1 - core, send), (core, keep)):
        for chunk, hidden in enumerate((hiddena, hiddenb)):
            target.ref[chunk] = dot(hidden[rows_at(half, quarter), :], wd.ref[...]).astype(
                target.ref.dtype
            )


def feed_grads(spot, n2s, hiddens, backs, wd, cots, peers, after):
    units, width = wd.shape
    quarter = cots[0].shape[0]
    return run(
        feed_grads_body,
        [(spot, "smem"), *held(*n2s, *hiddens, *backs, wd, *cots)],
        [
            ((2, quarter, width), f32),
            ((2, quarter, width), bf16),
            *sums_outs(width, 3 * units, peers),
        ],
        us=6,
        scratch=[VMEM((width, 3 * units), f32)],
        mib=20,
        after=after,
    )


def joint_grads_body(heads, ins, outs, total_ref):
    spot_ref, n1, dqa, dqb, dkv, lowa, lowb, mixa, mixb, tiles = ins
    table_out = outs[0]
    rows, own = dqa.target.shape
    total_ref[:, :own] = dot(n1.ref[:rows, :], dqa.ref[...], 0, 0) + dot(
        n1.ref[rows:, :], dqb.ref[...], 0, 0
    )
    total_ref[:, own : 3 * own] = dot(n1.ref[...], dkv.ref[...], 0, 0)
    total_ref[:, 3 * own :] = dot(lowa.ref[...], mixa.ref[...], 0, 0) + dot(
        lowb.ref[...], mixb.ref[...], 0, 0
    )
    split_sums(spot_ref, total_ref, outs[1:])
    head = iota((8, TILE), 0)
    bucket = iota((8, TILE), 1)
    table = jnp.zeros((8, TILE), f32)
    for h in range(heads):
        sums = {}
        for k in range(5):
            least, most = TILE * (k - 2) - TILE + 1, TILE * (k - 2) + TILE - 1
            tile = tiles.ref[(5 * h + k) * TILE : (5 * h + k + 1) * TILE, :]
            if k in (0, 4):
                b = bucket_of(least if k == 0 else most)
                sums[b] = sums.get(b, 0.0) + folded(tile, jnp.sum)
                continue
            offset = TILE * (k - 2) + iota((TILE, TILE), 0) - iota((TILE, TILE), 1)
            runs = bucket_runs(least, most)
            for n, (first, b) in enumerate(runs):
                held = offset >= first
                if n + 1 < len(runs):
                    held = held & (offset < runs[n + 1][0])
                sums[b] = sums.get(b, 0.0) + folded(jnp.where(held, tile, 0.0), jnp.sum)
        for b, part in sums.items():
            total = jnp.sum(jnp.sum(part, axis=0, keepdims=True), axis=1, keepdims=True)
            table = jnp.where((bucket == b) & (head == h), total, table)
    table_out.ref[...] = table


def joint_grads(spot, n1, dqa, dqb, dkv, lows, mixes, tiles, peers, after):
    width, own = n1.shape[1], dqa.shape[1]
    return run(
        functools.partial(joint_grads_body, own // DH),
        [(spot, "smem"), *held(n1, dqa, dqb, dkv, *lows, *mixes, tiles)],
        [((8, TILE), f32), *sums_outs(width, 4 * own, peers)],
        us=6,
        scratch=[VMEM((width, 4 * own), f32)],
        mib=16,
        after=after,
    )


def sum_body(counts, ins, outs):
    one, *ins = ins
    two, passed = ins[: counts[0]], ins[counts[0] :]
    total, *outs = outs
    pieces, copied = outs[: counts[1]], outs[counts[1] :]
    rows = two[0].ref.shape[0]
    for n, piece in enumerate(two):
        at = slice(n * rows, (n + 1) * rows)
        total.ref[at] = (one.ref[at].astype(f32) + piece.ref[...].astype(f32)).astype(total.ref.dtype)
    if pieces:
        scatter_pieces(total.ref[...], pieces)
    for source, target in zip(passed, copied):
        target.ref[...] = source.ref[...]


def added(one, two, after=(), passed=(), kind=bf16, cut=False):
    pieces = in_pieces(one.shape) if cut else []
    return run(
        functools.partial(sum_body, (len(two), len(pieces))),
        held(one, *two, *passed),
        [
            (one.shape, kind),
            *[(shape, kind) for shape in pieces],
            *[(array.shape, array.dtype) for array in passed],
        ],
        us=1,
        mib=4,
        after=after,
    )


def copy_body(ins, outs):
    outs[0].ref[...] = ins[0].ref[...]


def copied(array, after):
    return run(copy_body, held(array), [(array.shape, array.dtype)], us=1, mib=4, after=after)[0]


def out_split_body(ins, outs):
    spot_ref, keep, received = ins
    mine, far = outs
    side = lax.div(spot_ref[PLACE], 2)
    mine.ref[...] = keep.ref[side] + received.ref[side].astype(f32)
    far.ref[...] = (keep.ref[1 - side] + received.ref[1 - side].astype(f32)).astype(bf16)


def out_split(spot, keep, received, after=()):
    shape = keep.shape[1:]
    ins = [(spot, "smem"), *held(keep, received)]
    return run(out_split_body, ins, [(shape, f32), (shape, bf16)], us=1, mib=4, after=after)


def out_rows_body(ins, outs, rows_ref):
    spot_ref, h1a, h1b, mine, received = ins
    (out,) = outs
    quarter = mine.ref.shape[0]
    side, core = lax.div(spot_ref[PLACE], 2), lax.rem(spot_ref[PLACE], 2)
    for n, h1 in enumerate((h1a, h1b)):

        @pl.when(side == n)
        def taken():
            rows_ref[...] = h1.ref[rows_at(core, quarter), :]

    out.ref[...] = (rows_ref[...] + (mine.ref[...] + received.ref[...].astype(f32))).astype(bf16)


def finished_rows(spot, h1s, mine, received, after=()):
    (rows,) = run(
        out_rows_body,
        [(spot, "smem"), *held(*h1s, mine, received)],
        [(mine.shape, bf16, "hbm")],
        us=1.5,
        scratch=[VMEM(mine.shape, f32)],
        mib=6,
        after=after,
    )
    return rows


def halve_body(distances, ins, outs):
    spot_ref, *ins = ins
    for n, distance in enumerate(distances):
        keep, received = ins[2 * n : 2 * n + 2]
        kept, sent = outs[2 * n : 2 * n + 2]
        bit = bit_of(spot_ref, distance)
        for u in range(kept.ref.shape[0]):
            far = 2 * u + 1 - bit
            sent.ref[u] = (keep.ref[far] + received.ref[far].astype(f32)).astype(bf16)
        sent.send()
        for u in range(kept.ref.shape[0]):
            near = 2 * u + bit
            kept.ref[u] = keep.ref[near] + received.ref[near].astype(f32)
        kept.send()


def halve(spot, distances, sums, after):
    outs = []
    for keep in sums[::2]:
        shape = (keep.shape[0] // 2, *keep.shape[1:])
        outs += [(shape, f32), (shape, bf16)]
    return run(
        functools.partial(halve_body, distances),
        [(spot, "smem"), *held(*sums)],
        outs,
        us=2.5,
        mib=4,
        after=after,
    )


def last_sums_body(plan, ins, outs, total_ref):
    columns = ins[0].target.shape[2]
    for n in range(2):
        keep, received = ins[2 * n : 2 * n + 2]
        total_ref[:, n * columns : (n + 1) * columns] = keep.ref[0] + received.ref[0].astype(f32)
    for out, (first, last, turned) in zip(outs, plan):
        part = total_ref[:, first:last]
        out.ref[...] = part.T if turned else part
        out.send()


def last_sums(plan, sums, after):
    block, columns = sums[0].shape[1:]
    shapes = [(last - first, block) if turned else (block, last - first) for first, last, turned in plan]
    return run(
        functools.partial(last_sums_body, plan),
        held(*sums),
        [(shape, f32, "hbm") for shape in shapes],
        us=2,
        scratch=[VMEM((block, 2 * columns), f32)],
        mib=6,
        after=after,
    )


def finish_body(heads, ins, outs):
    spot_ref, one, two = ins
    score, gain_one, gain_two, table, sizes = [out.ref for out in outs]
    total = one.ref[...] + two.ref[...]
    share, width = score.shape[0], total.shape[1]
    moved = pltpu.roll(total, lax.rem(width - spot_ref[GROUP] * share, width), 1)
    score[...] = moved[0, :share]
    gain_one[...] = total[1]
    gain_two[...] = total[2]
    table[...] = total[4 : 4 + heads, :BUCKETS]
    sizes[...] = (total[3:4, :4] / total[3:4, 4:5])[0]


def finished(spot, one, two, heads, share, after=()):
    width = one.shape[1]
    shapes = [(share,), (width,), (width,), (heads, BUCKETS), (4,)]
    return run(
        functools.partial(finish_body, heads),
        [(spot, "smem"), *held(one, two)],
        [(shape, f32, "hbm") for shape in shapes],
        us=1,
        mib=4,
        after=after,
    )


def swapped(shard, axis, distance):
    peers = lax.axis_size(axis)
    return lax.ppermute(shard, axis, [(i, i ^ distance) for i in range(peers)])


def summed_but_last(value, axis, order):
    distance, pair = 1, (value, jnp.zeros_like(value))
    while distance < lax.axis_size(axis):
        if distance > 1:
            value, order = added(pair[0], pair[1:], order, kind=f32)[0], ()
        pair = value, swapped(value, axis, distance)
        distance *= 2
    return pair


def scattered(sums):
    peers = lax.axis_size("dp")
    me = lax.axis_index("dp")
    distances = [2**n for n in range(peers.bit_length() - 1)]
    parts = []
    for n, first in enumerate(STREAMS):
        order = sorted(distances, key=lambda d: (d != first, d))
        left = distances[::-1]
        if len(sums) == 4:
            keep, send = sums[2 * n : 2 * n + 2]
            blocks = keep + swapped(send, "dp", first).astype(f32)
            order.pop(0)
            left.remove(first)
        else:
            columns = sums[0].shape[1] // 2
            blocks = sums[0][:, n * columns : (n + 1) * columns]
            blocks = blocks.reshape(peers, -1, columns)
        block, columns = blocks.shape[1:]
        blocks = blocks.reshape(*[2] * len(left), block, columns)
        for distance in order:
            axis = left.index(distance)
            left.remove(distance)
            bit = lax.rem(lax.div(me, distance), 2)
            kept = lax.dynamic_index_in_dim(blocks, bit, axis, keepdims=False)
            sent = lax.dynamic_index_in_dim(blocks, 1 - bit, axis, keepdims=False)
            blocks = kept + swapped(sent.astype(bf16), "dp", distance).astype(f32)
        parts.append(blocks)
    return jnp.concatenate(parts, axis=1)


def body(
    byte_embeds,
    lengths,
    score_weight,
    norm1_gain,
    w_query,
    w_key,
    w_value,
    rel_table,
    w_out,
    norm2_gain,
    w_gate,
    w_up,
    w_down,
    cotangent,
):
    width = byte_embeds.shape[1]
    assert lengths.shape[0] == 1 and lax.axis_size("mp") == 4
    quarter = cotangent.shape[0]
    half = 2 * quarter
    heads = w_query.shape[1] // DH
    units = w_gate.shape[1]
    own = heads * DH
    peers = lax.axis_size("dp")
    spot = jnp.stack([lax.axis_index("mp"), lax.axis_index("dp"), lengths[0]])

    cots = [cotangent, swapped(cotangent, "mp", 1), swapped(cotangent, "mp", 2)]
    projections = [w_out, swapped(w_out, "mp", 1), swapped(w_out, "mp", 2)]
    h0, n1, q, k, v, weights, masses, mixing, near, *fetched = pool_forward(
        spot,
        rel_table.T,
        byte_embeds,
        score_weight,
        norm1_gain,
        w_query.T,
        w_key.T,
        w_value.T,
        norm2_gain,
        w_gate,
        w_up,
        w_down,
        w_out,
        cotangent,
    )
    score_vector, gain_one, wq, wk, wv, gain_two, wg, wu, wd, wo, own_rows = fetched
    mixes, sums = [None, None], [None, None]
    mixes[0], sums[0] = attend(near, q, k, v, 0, half, [])
    mixes[1], sums[1], *passed = attend(
        near, q, k, v, half, half, [mixes[0]], (cots[2], projections[2])
    )
    cots = (own_rows, cots[1], passed[0], swapped(passed[0], "mp", 1))
    projections = (wo, projections[1], passed[1], swapped(passed[1], "mp", 1))
    far = [swapped(mix, "mp", 2) for mix in mixes]
    next_far = copied(far[0], [mixes[1]])
    order = []
    fed, second = [], []
    for chunk in range(2):
        mixed = (mixes[chunk], swapped(mixes[chunk], "mp", 1), far[chunk], swapped(next_far, "mp", 1))
        h1, n2, hidden, backs, keep, *sends = feed(
            spot, h0, cots, gain_two, wg, wu, wd, mixed, projections, chunk, order
        )
        passed = [far[1]] if chunk == 0 else []
        mine, *passed = added(keep, near_pieces(sends), [], passed)
        if passed:
            next_far = passed[0]
        fed.append((h1, n2, hidden, backs))
        second.append((mine, swapped(mine, "mp", 2)))
        order = [mine]
    h1s, n2s, hiddens, backs = zip(*fed)
    out_keep, out_send, *feed_sums = feed_grads(spot, n2s, hiddens, backs, wd, cots, peers, order)
    out_near = swapped(out_send, "mp", 1)

    def received(sums, distances):
        return [
            swapped(sums[k], "dp", distances[k // 2]) if k % 2 else sums[k] for k in range(len(sums))
        ]

    def both(pair, after):
        total, *pieces = added(pair[0], pair[1:], after, cut=True)
        return total, *near_pieces(pieces)

    def back(chunk, pieces, *more):
        return attend_back(
            spot, gain_two, h1s[chunk], q, k, near, sums[chunk], v, wo, pieces, cots, chunk, *more
        )

    halving = len(feed_sums) == 4 and peers == 8
    lowa, backa, gain_two_sum, dqa, tiles, dk, dv = back(0, both(second[0], [feed_sums[0]]))
    pieces = both(second[1], [lowa])
    out_mine, out_far = out_split(spot, out_keep, out_near, [pieces[0]])
    lowb, backb, gain_two_sum, dqb, tiles, keepa, keepb, dkv, *sends = back(
        1, pieces, (dk, dv, tiles, gain_two_sum, dqa, wq, wk, wv), [out_mine]
    )
    order = [lowb]
    if halving:
        feed_sums = halve(spot, STREAMS[::-1], received(feed_sums, STREAMS), order)
        order = [feed_sums[0]]
    (firsta,) = added(keepa, near_pieces(sends[:PIECES]), order)
    (firstb,) = added(keepb, near_pieces(sends[PIECES:]), [firsta])
    first = [(one, swapped(one, "mp", 2)) for one in (firsta, firstb)]
    table_sum, *joint_sums = joint_grads(
        spot, n1, dqa, dqb, dkv, (lowa, lowb), mixes, tiles, peers, [firstb]
    )
    order = [table_sum]
    feed_plan = ((0, units, False), (units, 2 * units, False), (2 * units, 3 * units, True))
    joint_plan = tuple((n * own, (n + 1) * own, n == 3) for n in range(4))
    if halving:
        feed_sums = halve(spot, (4, 4), received(feed_sums, STREAMS[::-1]), order)
        joint_sums = halve(spot, STREAMS[::-1], received(joint_sums, STREAMS), [feed_sums[0]])
        order = [joint_sums[0]]
    firsts = both(first[0], order)
    firsts = [*firsts, *both(first[1], [firsts[0]])]
    factors, small, grad_rows = pool_scores(
        spot,
        byte_embeds,
        h0,
        (backa, backb),
        gain_one,
        weights,
        gain_two_sum,
        table_sum,
        masses,
        firsts,
        order,
    )
    order = [small]
    if halving:
        joint_sums = halve(spot, (4, 4), received(joint_sums, STREAMS[::-1]), order)
        order = [joint_sums[0]]
    (byte_grad,) = pool_bytes(score_vector, mixing, factors, grad_rows, order)
    order = [(byte_grad, pltpu.HBM)]
    if halving:
        feed_parts = last_sums(feed_plan, received(feed_sums, (4, 4)), order)
        order = [(feed_parts[0], pltpu.HBM)]
    out_rows = finished_rows(spot, h1s, out_mine, swapped(out_far, "mp", 2), order)
    if halving:
        joint_parts = last_sums(joint_plan, received(joint_sums, (4, 4)), [(out_rows, pltpu.HBM)])
    else:
        parts = []
        for sums, plan in ((feed_sums, feed_plan), (joint_sums, joint_plan)):
            total = scattered(sums)
            parts.append([total[:, a:b].T if turned else total[:, a:b] for a, b, turned in plan])
        feed_parts, joint_parts = parts
    score_part, gain_one_part, gain_two_part, table_part, size_dist = finished(
        spot,
        *summed_but_last(small, "dp", [(byte_grad, pltpu.HBM)]),
        heads,
        width // peers,
        [(joint_parts[0], pltpu.HBM)] if halving else [],
    )
    return (
        out_rows,
        byte_grad,
        score_part,
        gain_one_part,
        *joint_parts[:3],
        table_part.T,
        joint_parts[3],
        gain_two_part,
        *feed_parts,
        size_dist,
    )


def solution(mesh):
    placed = (
        P("dp", None),
        P("dp"),
        P(),
        P(),
        P(None, "mp"),
        P(None, "mp"),
        P(None, "mp"),
        P(None, "mp"),
        P("mp", None),
        P(),
        P(None, "mp"),
        P(None, "mp"),
        P("mp", None),
        P(("dp", "mp"), None),
    )
    return jax.shard_map(
        body,
        mesh=mesh,
        in_specs=placed,
        out_specs=(
            P(("dp", "mp"), None),
            P("dp", None),
            P("dp"),
            P(),
            P("dp", "mp"),
            P("dp", "mp"),
            P("dp", "mp"),
            P(None, "mp"),
            P("mp", "dp"),
            P(),
            P("dp", "mp"),
            P("dp", "mp"),
            P("mp", "dp"),
            P(),
        ),
        check_vma=False,
    )
```

```python
import functools

import jax
import jax.numpy as jnp
from jax import lax
from jax.experimental import pallas as pl
from jax.experimental.pallas import tpu as pltpu
from jax.sharding import PartitionSpec as P

DH = 64
BUCKETS = 32
TILE = 128
POOL_BYTES = 192
QUERY_ROWS = 256

epsilon = 1e-06
bucket_edges = (12, 16, 23, 32, 46, 64, 91)
highest = lax.Precision.HIGHEST
f32 = jnp.float32
bf16 = jnp.bfloat16
SMEM = pltpu.SMEM
VMEM = pltpu.VMEM


def bucket_of(offset):
    distance = abs(offset)
    near = distance if distance < 8 else 8 + sum(distance >= edge for edge in bucket_edges)
    return near + (16 if offset > 0 else 0)


def bucket_runs(least, most):
    runs = [(least, bucket_of(least))]
    for offset in range(least + 1, most + 1):
        if bucket_of(offset) != runs[-1][1]:
            runs.append((offset, bucket_of(offset)))
    return runs


def iota(shape, dim):
    return lax.broadcasted_iota(jnp.int32, shape, dim)


def dot(left, right, left_dim=1, right_dim=0, precision=None):
    return lax.dot_general(
        left,
        right,
        (((left_dim,), (right_dim,)), ((), ())),
        precision=precision,
        preferred_element_type=f32,
    )


def two_parts(value):
    high = value.astype(bf16)
    return high, (value - high.astype(f32)).astype(bf16)


class Held:
    def __init__(self, ref):
        self.ref = self.target = ref

    def upto(self, row):
        return self.ref

    def send(self, *at):
        pass


class Loaded:
    def __init__(self, source, target, semaphores):
        rows = source.shape[0] // len(semaphores)
        self.rows, self.target, self.waited = rows, target, set()
        if len(semaphores) == 1:
            self.copies = [pltpu.make_async_copy(source, target, semaphores[0])]
            return
        self.copies = [
            pltpu.make_async_copy(
                source.at[pl.ds(k * rows, rows)], target.at[pl.ds(k * rows, rows)], semaphore
            )
            for k, semaphore in enumerate(semaphores)
        ]

    def start(self):
        for copy in self.copies:
            copy.start()

    def upto(self, row):
        for k, copy in enumerate(self.copies):
            if k * self.rows < row and k not in self.waited:
                copy.wait()
                self.waited.add(k)
        return self.target

    @property
    def ref(self):
        return self.upto(self.target.shape[0])


class Stored:
    def __init__(self, source, target, semaphores):
        self.ref, self.target, self.semaphores, self.copies = source, target, semaphores, []

    def send(self, *at):
        source, target = (self.ref.at[at], self.target.at[at]) if at else (self.ref, self.target)
        copy = pltpu.make_async_copy(source, target, self.semaphores[len(self.copies)])
        copy.start()
        self.copies.append(copy)


def run(body, ins, outs, us, scratch=(), mib=24, after=()):
    loaded = [(array, how) for array, how in ins if isinstance(how, int)]
    copied = [out[2] if len(out) == 3 else 0 for out in outs]
    count, more = len(ins), len(after)

    def kernel(*refs):
        sources = refs[:count]
        targets = refs[count + more : count + more + len(outs)]
        rest = list(refs[count + more + len(outs) :])
        stages = [rest.pop(0) for _ in loaded]
        results = [rest.pop(0) if moved else None for moved in copied]
        load_semaphores = rest.pop(0) if loaded else None
        store_semaphores = rest.pop(0) if sum(copied) else None
        given, used, stored, first = [], 0, [], 0
        for source, (_, how) in zip(sources, ins):
            if how == "vmem":
                given.append(Held(source))
            elif not isinstance(how, int):
                given.append(source)
            else:
                semaphores = [load_semaphores.at[used + k] for k in range(how)]
                given.append(Loaded(source, stages.pop(0), semaphores))
                given[-1].start()
                used += how
        for result, target, moved in zip(results, targets, copied):
            if not moved:
                stored.append(Held(target))
                continue
            semaphores = [store_semaphores.at[first + n] for n in range(moved)]
            stored.append(Stored(result, target, semaphores))
            first += moved
        body(given, stored, *rest)
        for array in given:
            if isinstance(array, Loaded):
                array.ref
        sent = [result for result in stored if isinstance(result, Stored)]
        for result in sent:
            if not result.copies:
                result.send()
        for result in sent:
            for copy in result.copies:
                copy.wait()

    spaces = {"smem": SMEM, "vmem": VMEM, "any": pl.ANY}
    arrays = [
        pltpu.with_memory_space_constraint(array, pltpu.HBM)
        if how == "hbm" or isinstance(how, int)
        else array
        for array, how in ins
    ]
    return pl.pallas_call(
        kernel,
        out_shape=[
            pltpu.HBM(*out[:2]) if moved else jax.ShapeDtypeStruct(*out)
            for out, moved in zip(outs, copied)
        ],
        in_specs=[
            *[pl.BlockSpec(memory_space=spaces.get(how, pltpu.HBM)) for _, how in ins],
            *[pl.BlockSpec(memory_space=pl.ANY)] * more,
        ],
        out_specs=[pl.BlockSpec(memory_space=pltpu.HBM if moved else VMEM) for moved in copied],
        scratch_shapes=[
            *[VMEM(array.shape, array.dtype) for array, _ in loaded],
            *[VMEM(*out[:2]) for out, moved in zip(outs, copied) if moved],
            *([pltpu.SemaphoreType.DMA((sum(how for _, how in loaded),))] if loaded else []),
            *([pltpu.SemaphoreType.DMA((sum(copied),))] if sum(copied) else []),
            *scratch,
        ],
        cost_estimate=pl.CostEstimate(flops=1, transcendentals=0, bytes_accessed=1),
        compiler_params=pltpu.CompilerParams(vmem_limit_bytes=mib * 2**20),
    )(*arrays, *[pltpu.with_memory_space_constraint(*a) if isinstance(a, tuple) else a for a in after])


def held(*arrays):
    return [(array, "vmem") for array in arrays]


def started(*copies):
    for copy in copies:
        copy.start()
    return copies


def fetch_owned(pieces, owners, place, target, semaphores):
    waits = []
    for n, owner in enumerate(owners):
        for d, piece in enumerate(pieces):
            pl.when(lax.bitwise_xor(place, d) == owner)(
                pltpu.make_async_copy(piece, target.at[n], semaphores.at[n]).start
            )
        waits.append(pltpu.make_async_copy(pieces[0], target.at[n], semaphores.at[n]))
    return waits


def fetch_pair(core, mine, others, target, at, semaphores):
    rows = others[0].shape[0]
    return started(
        pltpu.make_async_copy(mine, target.at[at + core], semaphores.at[0]),
        *[
            pltpu.make_async_copy(
                piece, target.at[at + 1 - core, pl.ds(n * rows, rows)], semaphores.at[1 + n]
            )
            for n, piece in enumerate(others)
        ],
    )


PIECES = 2


def in_pieces(shape):
    return [(shape[0] // PIECES, *shape[1:])] * PIECES


def scatter_pieces(value, pieces):
    rows = pieces[0].ref.shape[0]
    for n, piece in enumerate(pieces):
        piece.ref[...] = value[n * rows : (n + 1) * rows].astype(piece.ref.dtype)


def near_pieces(pieces):
    return [swapped(piece, "mp", 1) for piece in pieces]


def rows_at(index, count):
    return pl.ds(pl.multiple_of(index * count, count), count)


def pair_sums(even, odd):
    count = even.shape[1]
    lane = iota(even.shape, 1)

    def after(value, k):
        return jnp.where(lane < count - k, pltpu.roll(value, count - k, 1), 0.0)

    def before(value, k):
        return pltpu.roll(value, k, 1)

    two = even + odd
    first = lax.rem(lane, 2) == 0
    four = two + after(two, 1)
    four = jnp.where(first, four, before(four, 1))
    place = lax.rem(lane, 3)
    early = two + after(even, 1)
    late = after(odd, 1) + after(two, 2)
    far = before(late, 2)
    three_even = jnp.where(place == 0, early, jnp.where(place == 1, before(early, 1), far))
    three_odd = jnp.where(place == 0, early, jnp.where(place == 1, before(late, 1), far))
    return [(even, odd), (two, two), (three_even, three_odd), (four, four)]


def by_row(rows):
    shape = (8, rows[0].shape[1])
    place = iota(shape, 0)
    result = jnp.zeros(shape, f32)
    for k, row in enumerate(rows):
        result = jnp.where(place == k, row, result)
    return result


def pool_masks(byte_count, lanes):
    byte = iota((byte_count, 1), 0)
    row = iota((1, lanes), 1)
    return [
        (0, True, False, byte == 2 * row),
        (0, False, True, byte == 2 * row + 1),
        (1, True, True, lax.div(byte, 2) == row),
        (2, True, False, lax.div(byte, 3) == lax.div(2 * row, 3)),
        (2, False, True, lax.div(byte, 3) == lax.div(2 * row + 1, 3)),
        (3, True, True, lax.div(byte, 4) == lax.div(row, 2)),
    ]


def pool_chunks(byte_total):
    return [(at, min(POOL_BYTES, byte_total - at)) for at in range(0, byte_total, POOL_BYTES)]


def near_bias(table, heads, near_ref):
    for k in range(5):
        middle = TILE * (k - 2)
        if k in (0, 4):
            runs = [(middle, bucket_of(middle))]
        else:
            runs = bucket_runs(middle - TILE + 1, middle + TILE - 1)
        offset = middle + iota((TILE, TILE), 0) - iota((TILE, TILE), 1)
        values = [[table[h : h + 1, bucket : bucket + 1] for _, bucket in runs] for h in range(heads)]
        tiles = [jnp.broadcast_to(values[h][0], (TILE, TILE)) for h in range(heads)]
        for n in range(1, len(runs)):
            past = offset >= runs[n][0]
            tiles = [jnp.where(past, values[h][n], tiles[h]) for h in range(heads)]
        for h in range(heads):
            near_ref[(5 * h + k) * TILE : (5 * h + k + 1) * TILE, :] = tiles[h]


def as_row(vector_ref):
    return vector_ref[...].astype(f32).reshape(1, -1)


def byte_scores(parts, vector, scores_ref):
    columns = jnp.broadcast_to(vector, (TILE, vector.shape[1])).T.astype(bf16)
    for part in parts:
        at, x = part()
        scores_ref[at, :] = dot(x, columns)
    half = scores_ref.shape[0] // 2
    return [scores_ref[pl.ds(k, half, stride=2), :].T[:8] for k in range(2)]


X_PARTS = 4


def pool_body(ins, outs, scores_ref, semaphores):
    length_ref, table, x, *sources = ins
    h0, n1, q, k, v, weights, masses, mixing, near, *fetched = outs
    copies = started(
        *[
            pltpu.make_async_copy(source, target.ref, semaphores.at[n])
            for n, (source, target) in enumerate(zip(sources, fetched))
        ]
    )
    score_row, gain_row, wq, wk, wv = fetched[:5]
    byte_total, width = x.target.shape
    share = byte_total // X_PARTS
    heads = table.target.shape[0]
    own = heads * DH
    length = length_ref[0]
    valid = lax.div(length + 1, 2)
    near_bias(table.ref[...].astype(f32), heads, near.ref)
    for copy in copies[:2]:
        copy.wait()

    def part(n):
        x.upto((n + 1) * share)
        return pl.ds(n * share, share), x.target[n * share : (n + 1) * share, :]

    row = iota((8, byte_total // 2), 1)
    inside = (2 * row < length, 2 * row + 1 < length)
    parts = [functools.partial(part, n) for n in range(X_PARTS)]
    scores = byte_scores(parts, as_row(score_row.ref), scores_ref)
    scores = [jnp.where(known, score, 0.0) for known, score in zip(inside, scores)]
    sums = pair_sums(*scores)
    sized = []
    for odd in range(2):
        logits = [pair[odd] / (b + 1) for b, pair in enumerate(sums)]
        peak = functools.reduce(jnp.maximum, logits)
        shifted = [jnp.exp(logit - peak) for logit in logits]
        mass = functools.reduce(jnp.add, shifted)
        sized.append(by_row([one / mass for one in shifted]))
    weights.ref[:8] = sized[0]
    weights.ref[8:] = sized[1]
    total = sum(
        jnp.sum(jnp.where(known, one, 0.0), axis=1, keepdims=True) for known, one in zip(inside, sized)
    )
    masses.ref[...] = jnp.broadcast_to(total, masses.ref.shape)
    gain = as_row(gain_row.ref)
    for at, count in pool_chunks(byte_total):
        rows = count // 2
        start = at // 2
        blank = jnp.zeros((8, TILE - rows), f32)
        even, odd = [jnp.concatenate((one[:, start : start + rows], blank), axis=1) for one in sized]
        part = jnp.zeros((count, TILE), f32)
        for b, for_even, for_odd, mask in pool_masks(count, TILE):
            line = even if not for_odd else odd if not for_even else even + odd
            part = part + jnp.where(mask, line[b : b + 1] / (2 * b + 2), 0.0)
        part = jnp.where(iota((count, 1), 0) + at < length, part, 0.0)
        both = jnp.concatenate(two_parts(part), axis=1)
        mixing.ref[at : at + count, :] = both
        pooled = dot(both, x.ref[at : at + count, :], 0, 0)
        pooled = pooled[:rows] + pooled[TILE : TILE + rows]
        h0.ref[start : start + rows, :] = pooled
        scale = lax.rsqrt(jnp.mean(pooled * pooled, axis=1, keepdims=True) + epsilon)
        n1.ref[start : start + rows, :] = (pooled * scale * gain).astype(bf16)
    for copy in copies[2:]:
        copy.wait()
    normed = n1.ref[...]
    rows, padding = normed.shape[0], q.ref.shape[1] - own
    first = iota((rows, padding), 1) == 0
    masked = iota((rows, padding), 0) >= valid
    q.ref[:, own:] = jnp.where(first, 1.0, 0.0).astype(bf16)
    k.ref[:, own:] = jnp.where(first & masked, -1e30, 0.0).astype(bf16)
    v.ref[:, own:] = jnp.zeros((rows, padding), bf16)
    for out, weight in ((q, wq), (k, wk), (v, wv)):
        out.ref[:, :own] = dot(normed, weight.ref[...], 1, 1).astype(bf16)
        out.send()


def pool_forward(length, table, x, *fetched):
    byte_total, width = x.shape
    rows = byte_total // 2
    heads = table.shape[0]
    padded = heads * DH + DH
    return run(
        pool_body,
        [(length, "smem"), (table, 1), (x, X_PARTS), *[(array, "hbm") for array in fetched]],
        [
            ((rows, width), f32),
            ((rows, width), bf16),
            ((rows, padded), bf16),
            ((rows, padded), bf16),
            ((rows, padded), bf16),
            ((16, rows), f32),
            ((8, TILE), f32),
            ((byte_total, 2 * TILE), bf16),
            ((5 * heads * TILE, TILE), f32),
            *[(array.shape, array.dtype) for array in fetched],
        ],
        us=10,
        scratch=[
            VMEM((byte_total, TILE), f32),
            pltpu.SemaphoreType.DMA((len(fetched),)),
        ],
    )


def pool_scores_body(ins, outs, back_ref, rows_ref, semaphores):
    length_ref, x, h0, backa, backb, gain, weights, gain_grad, table, masses, *pieces = ins
    factors, small, rows_out = outs
    core = lax.rem(lax.axis_index("mp"), 2)
    each = 1 + PIECES
    waits = [
        fetch_pair(
            core,
            pieces[each * n],
            pieces[each * n + 1 : each * n + each],
            rows_ref,
            2 * n,
            semaphores.at[pl.ds(each * n, each)],
        )
        for n in range(2)
    ]
    byte_total, width = x.target.shape
    rows_total = byte_total // 2
    quarter = rows_ref.shape[1]
    length = length_ref[0]
    gain = as_row(gain.ref)
    grad_rows = rows_out.ref
    gain_sum = jnp.zeros((1, width), f32)
    for chunk, back in enumerate((backa, backb)):
        for copy in waits[chunk]:
            copy.wait()
        for half in range(2):
            n = 2 * chunk + half
            at = slice(n * quarter, (n + 1) * quarter)
            total, added = norm_back(h0.ref[at, :], gain, rows_ref[n])
            gain_sum = gain_sum + added
            total = total + back.ref[half * quarter : (half + 1) * quarter, :]
            grad_rows[at, :] = total.astype(bf16)
    rows_out.send()
    for at, count in pool_chunks(byte_total):
        rows = count // 2
        start = at // 2
        product = dot(x.upto(at + count)[at : at + count, :], grad_rows[start : start + rows, :], 1, 1)
        product = jnp.where(iota((count, 1), 0) + at < length, product, 0.0)
        even, odd = [None] * 4, [None] * 4
        for b, for_even, for_odd, mask in pool_masks(count, rows):
            total = jnp.sum(jnp.where(mask, product, 0.0), axis=0, keepdims=True) / (2 * b + 2)
            if for_even:
                even[b] = total
            if for_odd:
                odd[b] = total
        back_ref[:8, start : start + rows] = by_row(even)
        back_ref[8:, start : start + rows] = by_row(odd)
    logit_back = []
    for odd in range(2):
        weight = weights.ref[8 * odd : 8 * odd + 8, :]
        back = back_ref[8 * odd : 8 * odd + 8, :]
        logit_back.append(weight * (back - jnp.sum(weight * back, axis=0, keepdims=True)))
    place = iota((8, rows_total), 0)
    row = iota((1, rows_total), 1)
    sums = pair_sums(*logit_back)
    lines = []
    for odd in range(2):
        picked = jnp.zeros((8, rows_total), f32)
        for b, pair in enumerate(sums):
            picked = picked + jnp.where(place == b, pair[odd] / (b + 1), 0.0)
        total = jnp.sum(picked, axis=0, keepdims=True)
        lines += two_parts(jnp.where(2 * row + odd < length, total, 0.0))
    place = iota((16, rows_total), 0)
    stacked = jnp.zeros((16, rows_total), f32)
    for k, line in enumerate(lines):
        stacked = jnp.where(place == k, line.astype(f32), stacked)
    stacked = stacked.astype(bf16)
    total = jnp.zeros((16, width), f32)
    for at, count in pool_chunks(byte_total):
        rows = count // 2
        part = stacked[:, at // 2 : at // 2 + rows]
        byte = iota((rows, count), 1)
        row = iota((rows, count), 0)
        picks = [jnp.where(byte == 2 * row + odd, 1.0, 0.0).astype(bf16) for odd in range(2)]
        upper = iota((16, rows), 0) < 2
        zero = jnp.zeros_like(part)
        spread = dot(jnp.where(upper, part.astype(f32), 0.0).astype(bf16), picks[0]) + dot(
            jnp.where(upper, 0.0, part.astype(f32)).astype(bf16), picks[1]
        )
        spread = spread.astype(bf16)
        factors.ref[:, at : at + count] = spread
        total = total + dot(spread, x.ref[at : at + count, :])
    small.ref[0:1, :] = jnp.sum(total, axis=0, keepdims=True)
    small.ref[1:2, :] = gain_sum
    small.ref[2:3, :] = gain_grad.ref[...]
    small.ref[3:, :] = jnp.zeros((5, width), f32)
    lane = iota((1, TILE), 1)
    sizes = jnp.where(lane == 4, length.astype(f32), 0.0)
    for b in range(4):
        sizes = sizes + jnp.where(lane == b, masses.ref[b : b + 1, :], 0.0)
    small.ref[3:4, :TILE] = sizes
    small.ref[4:8, :TILE] = table.ref[:4, :]


def pool_scores(length, x, h0, backs, gain, weights, gain_grad, table, masses, pieces, after):
    byte_total, width = x.shape
    quarter = pieces[0].shape[0]
    return run(
        pool_scores_body,
        [
            (length, "smem"),
            (x, X_PARTS),
            *held(h0, *backs, gain, weights, gain_grad, table, masses),
            *[(piece, "any") for piece in pieces],
        ],
        [
            ((16, byte_total), bf16),
            ((8, width), f32),
            ((byte_total // 2, width), bf16),
        ],
        us=6,
        scratch=[
            VMEM((16, byte_total // 2), f32),
            VMEM((4, quarter, width), bf16),
            pltpu.SemaphoreType.DMA((2 + 2 * PIECES,)),
        ],
        after=after,
    )


def pool_bytes_body(ins, outs):
    score_row, mixing, factors, grad_rows = [one.ref for one in ins]
    (byte_grad,) = outs
    byte_total, width = byte_grad.ref.shape
    vector = jnp.broadcast_to(as_row(score_row), (16, width)).astype(bf16)
    chunks = pool_chunks(byte_total)
    sent = 0
    for n, (at, count) in enumerate(chunks):
        rows = count // 2
        g = grad_rows[at // 2 : at // 2 + rows, :]
        both = mixing[at : at + count, :]
        back = dot(both[:, :rows], g) + dot(both[:, TILE : TILE + rows], g)
        back = back + dot(factors[:, at : at + count], vector, 0, 0)
        byte_grad.ref[at : at + count, :] = back.astype(bf16)
        if n % 4 == 3 or n + 1 == len(chunks):
            byte_grad.send(pl.ds(sent, at + count - sent))
            sent = at + count


def pool_bytes(score_weight, mixing, factors, grad_rows, after):
    byte_total, width = mixing.shape[0], grad_rows.shape[1]
    return run(
        pool_bytes_body,
        held(score_weight, mixing, factors, grad_rows),
        [((byte_total, width), bf16, 4)],
        us=5,
        after=after,
    )


def norm_back(value, gain, incoming):
    incoming = incoming.astype(f32)
    scale = lax.rsqrt(jnp.mean(value * value, axis=1, keepdims=True) + epsilon)
    unit = value * scale
    product = incoming * unit
    inner = jnp.mean(product * gain, axis=1, keepdims=True)
    return scale * (incoming * gain - unit * inner), jnp.sum(product, axis=0, keepdims=True)


def head_lanes(width, first, last, more=None):
    lane = iota((1, width), 1)
    keep = (lane >= first) & (lane < last)
    if more is not None:
        keep = keep | (lane == more)
    return jnp.where(keep, 1.0, 0.0).astype(bf16)


def bias_rows(head, distance):
    place = 5 * head + min(max(distance + 2, 0), 4)
    return slice(place * TILE, (place + 1) * TILE)


def folded(value, op):
    return op(value.reshape(-1, 8, value.shape[1]), axis=0)


def attend_body(heads, first_block, ins, outs, vt_ref, *semaphores):
    q, k, near, v, *passed = ins
    mix, sums, out_t, *copied = outs
    copies = started(
        *[
            pltpu.make_async_copy(source, target.ref, semaphores[0].at[n])
            for n, (source, target) in enumerate(zip(passed, copied))
        ]
    )
    own = heads * DH
    key_rows, width = k.target.shape
    halves = QUERY_ROWS // TILE
    keys = k.ref[...]
    for step in range(mix.ref.shape[0] // QUERY_ROWS):
        first = (first_block + step) * QUERY_ROWS
        queries = q.ref[first : first + QUERY_ROWS, :]
        columns = slice(step * QUERY_ROWS, (step + 1) * QUERY_ROWS)
        mixed = []
        for h in range(heads):
            scores = dot(keys, queries * head_lanes(width, h * DH, h * DH + DH, own), 1, 1)
            probs, log_sums, masses = [], [], []
            for half in range(halves):
                query_tile = first // TILE + half
                tiles, peak = [], None
                for j in range(key_rows // TILE):
                    tile = scores[j * TILE : (j + 1) * TILE, half * TILE : (half + 1) * TILE]
                    tile = tile + near.ref[bias_rows(h, j - query_tile), :]
                    top = folded(tile, jnp.max)
                    peak = top if peak is None else jnp.maximum(peak, top)
                    tiles.append(tile)
                peak = jnp.max(peak, axis=0, keepdims=True)
                mass, column = None, []
                for tile in tiles:
                    shifted = jnp.exp(tile - peak)
                    part = folded(shifted, jnp.sum)
                    mass = part if mass is None else mass + part
                    column.append(shifted.astype(bf16))
                mass = jnp.sum(mass, axis=0, keepdims=True)
                probs.append(jnp.concatenate(column, axis=0))
                masses.append(mass)
                log_sums.append(peak + jnp.log(mass))
            prob = jnp.concatenate(probs, axis=1)
            if step == 0 and h == 0:
                vt_ref[...] = v.ref[...].T
            out = dot(vt_ref[h * DH : (h + 1) * DH, :], prob)
            out = out / jnp.concatenate(masses, axis=1)
            out_t.ref[h * DH : (h + 1) * DH, columns] = out
            mixed.append(out)
            sums.ref[h : h + 1, columns] = jnp.concatenate(log_sums, axis=1)
        mixed.append(jnp.zeros((width - own, QUERY_ROWS), f32))
        mix.ref[columns, :] = jnp.concatenate(mixed, axis=0).T[:, :own].astype(bf16)
    for copy in copies:
        copy.wait()


def attend(near, q, k, v, first_row, row_count, after, passed=()):
    key_rows, width = k.shape
    heads = (width - DH) // DH
    return run(
        functools.partial(attend_body, heads, first_row // QUERY_ROWS),
        [*held(q, k, near, v), *[(array, "any") for array in passed]],
        [
            ((row_count, heads * DH), bf16),
            ((8, row_count), f32),
            ((heads * DH, row_count), f32),
            *[(array.shape, array.dtype) for array in passed],
        ],
        us=4,
        scratch=[
            VMEM((width, key_rows), bf16),
            *([pltpu.SemaphoreType.DMA((len(passed),))] if passed else []),
        ],
        mib=16,
        after=after,
    )


def attend_back_body(chunk, last, ins, outs, rows_ref, dy_ref, kt_ref, mb_ref, *scratch):
    gain, h1, q, k, near, sums, turned, v, wo, *ins = ins
    if last:
        dk_in, dv_in, tiles_in, gain_in, dqa, wq, wk, wv, *ins = ins
        low, back, gain_out, dq, tiles_out, keepa, keepb, dkv, *sends = outs
        dk_ref, dv_ref, *scratch = scratch
    else:
        low, back, gain_out, dq, tiles_out, dk_out, dv_out = outs
        dk_ref, dv_ref = dk_out.ref, dv_out.ref
    (semaphores,) = scratch
    place = lax.axis_index("mp")
    core = lax.rem(place, 2)
    waits = [
        *fetch_pair(core, ins[0], ins[1 : 1 + PIECES], rows_ref, 0, semaphores.at[pl.ds(2, 1 + PIECES)]),
        *fetch_owned(
            ins[1 + PIECES :], (2 * chunk, 2 * chunk + 1), place, dy_ref, semaphores.at[pl.ds(0, 2)]
        ),
    ]
    for copy in waits:
        copy.wait()
    quarter, model = dy_ref.shape[1:]
    gain = as_row(gain.ref)
    gain_sum = gain_in.ref[...] if last else jnp.zeros((1, model), f32)
    for half in range(2):
        at = slice(half * quarter, (half + 1) * quarter)
        total, added = norm_back(h1.ref[at, :], gain, rows_ref[half])
        gain_sum = gain_sum + added
        total = total + dy_ref[half].astype(f32)
        back.ref[at, :] = total
        low.ref[at, :] = total.astype(bf16)
    gain_out.ref[...] = gain_sum
    gain_out.send()
    back.send()
    low.send()

    key_rows, width = k.target.shape
    own = wo.target.shape[0]
    heads = own // DH
    halves = QUERY_ROWS // TILE
    kt_ref[...] = k.ref[...].T
    if last:
        dk_ref, dv_ref = dk_in.ref, dv_in.ref
        tiles_out.ref[...] = tiles_in.ref[...]
    else:
        tiles_out.ref[...] = jnp.zeros_like(tiles_out.ref)
    keys, values = k.ref[...], v.ref[...]
    for step in range(2 * quarter // QUERY_ROWS):
        columns = slice(step * QUERY_ROWS, (step + 1) * QUERY_ROWS)
        first = chunk * 2 * quarter + step * QUERY_ROWS
        queries = q.ref[first : first + QUERY_ROWS, :]
        mb_ref[:, :own] = dot(low.ref[columns, :], wo.ref[...], 1, 1).astype(bf16)
        mb_ref[:, own:] = jnp.zeros((QUERY_ROWS, width - own), bf16)
        mb = mb_ref[...]
        weighted = mb.astype(f32).T[:own] * turned.ref[:, columns]
        all_probs, all_backs, all_mb, all_q, query_back = [], [], [], [], []
        for h in range(heads):
            only = head_lanes(width, h * DH, h * DH + DH)
            scores = dot(keys, queries * head_lanes(width, h * DH, h * DH + DH, own), 1, 1)
            own_mb = mb * only
            prob_back = dot(values, own_mb, 1, 1)
            inner = jnp.sum(weighted[h * DH : (h + 1) * DH], axis=0, keepdims=True)
            low_columns, back_columns = [], []
            for half in range(halves):
                query_tile = first // TILE + half
                lanes = slice(half * TILE, (half + 1) * TILE)
                at = step * QUERY_ROWS + half * TILE
                log_sum = sums.ref[h : h + 1, at : at + TILE]
                low_column, back_column = [], []
                for j in range(key_rows // TILE):
                    rows = slice(j * TILE, (j + 1) * TILE)
                    table_rows = bias_rows(h, j - query_tile)
                    prob = jnp.exp(scores[rows, lanes] + (near.ref[table_rows, :] - log_sum))
                    score_back = prob * (prob_back[rows, lanes] - inner[:, lanes])
                    low_column.append(prob.astype(bf16))
                    back_column.append(score_back.astype(bf16))
                    tiles_out.ref[table_rows, :] += back_column[-1].astype(f32)
                low_columns.append(jnp.concatenate(low_column, axis=0))
                back_columns.append(jnp.concatenate(back_column, axis=0))
            score_back = jnp.concatenate(back_columns, axis=1)
            all_probs.append(jnp.concatenate(low_columns, axis=1))
            all_backs.append(score_back)
            all_mb.append(own_mb)
            all_q.append(queries * only)
            query_back.append(dot(kt_ref[h * DH : (h + 1) * DH, :], score_back))
        value_back = dot(jnp.concatenate(all_probs, axis=1), jnp.concatenate(all_mb, axis=0))
        key_back = dot(jnp.concatenate(all_backs, axis=1), jnp.concatenate(all_q, axis=0))
        if last or step:
            dv_ref[...] += value_back
            dk_ref[...] += key_back
        else:
            dv_ref[...] = value_back
            dk_ref[...] = key_back
        query_back.append(jnp.zeros((width - own, QUERY_ROWS), f32))
        dq.ref[columns, :] = jnp.concatenate(query_back, axis=0).T[:, :own].astype(bf16)
    tiles_out.send()
    dq.send()
    if not last:
        return
    dkv.ref[:, :own] = dk_ref[:, :own].astype(bf16)
    dkv.ref[:, own:] = dv_ref[:, :own].astype(bf16)
    dkv.send()
    for place, sent in ((1 - core, True), (core, False)):
        local = rows_at(place, quarter)
        for chunk, query_back in enumerate((dqa, dq)):
            rows = rows_at(2 * chunk + place, quarter)
            total = dot(query_back.ref[local, :], wq.ref[...])
            total = total + dot(dkv.ref[rows, :own], wk.ref[...])
            total = total + dot(dkv.ref[rows, own:], wv.ref[...])
            if sent:
                scatter_pieces(total, sends[PIECES * chunk : PIECES * (chunk + 1)])
            else:
                (keepa, keepb)[chunk].ref[...] = total


def attend_back(gain, h1, q, k, near, sums, turned, v, wo, pieces, cots, chunk, kept=None, after=()):
    key_rows, width = k.shape
    rows, model = h1.shape
    own = wo.shape[0]
    quarter = rows // 2
    last = kept is not None
    outs = [
        ((rows, model), bf16),
        ((rows, model), f32),
        ((1, model), f32),
        ((rows, own), bf16),
        (near.shape, f32),
    ]
    sums_shape = ((key_rows, width), f32)
    if last:
        outs += [
            ((quarter, model), f32),
            ((quarter, model), f32),
            ((key_rows, 2 * own), bf16),
            *[(shape, bf16) for shape in 2 * in_pieces((quarter, model))],
        ]
    else:
        outs += [sums_shape, sums_shape]
    return run(
        functools.partial(attend_back_body, chunk, last),
        [
            *held(gain, h1, q, k, near, sums, turned, v, wo, *(kept or ())),
            *[(array, "any") for array in (*pieces, *cots)],
        ],
        outs,
        us=12 if last else 10,
        scratch=[
            VMEM((2, quarter, model), bf16),
            VMEM((2, quarter, model), bf16),
            VMEM((width, key_rows), bf16),
            VMEM((QUERY_ROWS, width), bf16),
            *([VMEM(*sums_shape), VMEM(*sums_shape)] if last else []),
            pltpu.SemaphoreType.DMA((3 + PIECES,)),
        ],
        mib=20,
        after=after,
    )


def gelu_parts(gate):
    factor = (2.0 / jnp.pi) ** 0.5
    square = gate * gate
    bent = jnp.tanh(factor * gate * (1.0 + 0.044715 * square))
    value = 0.5 * gate * (1.0 + bent)
    slope = 0.5 * (1.0 + bent) + 0.5 * gate * (1.0 - bent * bent) * (
        factor * (1.0 + 3 * 0.044715 * square)
    )
    return value, slope


def feed_body(chunk, ins, outs, dy_ref, mix_ref, out_ref, semaphores):
    h0, gain, wg, wu, wd, *pieces = ins
    cots, mixes, projections = pieces[:4], pieces[4:8], pieces[8:12]
    h1, n2, hidden, backs, keep = [one.ref for one in outs[:5]]
    send = outs[5:]
    place = lax.axis_index("mp")
    core = lax.rem(place, 2)
    quarter = keep.shape[0]
    rows = 2 * quarter
    units = wg.ref.shape[1]
    copies = []
    for d in range(4):
        owner = lax.bitwise_xor(place, d)
        copies += started(
            pltpu.make_async_copy(mixes[d], mix_ref.at[owner], semaphores.at[2 * d]),
            pltpu.make_async_copy(projections[d], out_ref.at[owner], semaphores.at[1 + 2 * d]),
        )
    owners = (2 * chunk, 2 * chunk + 1)
    more = fetch_owned(cots, owners, place, dy_ref, semaphores.at[pl.ds(8, 2)])
    for copy in copies:
        copy.wait()
    gain = as_row(gain.ref)
    for half in range(2):
        at = slice(half * quarter, (half + 1) * quarter)
        after = h0.ref[chunk * rows + half * quarter : chunk * rows + (half + 1) * quarter, :]
        for owner in range(4):
            after = after + dot(mix_ref[owner, at, :], out_ref[owner])
        h1[at, :] = after
        scale = lax.rsqrt(jnp.mean(after * after, axis=1, keepdims=True) + epsilon)
        n2[at, :] = (after * scale * gain).astype(bf16)
    for copy in more:
        copy.wait()
    for half, target in ((1 - core, send), (core, keep)):
        at = rows_at(half, quarter)
        normed = n2[at, :]
        gate = dot(normed, wg.ref[...])
        up = dot(normed, wu.ref[...])
        value, slope = gelu_parts(gate)
        hidden[at, :] = (value * up).astype(bf16)
        hidden_back = dot(dy_ref[half], wd.ref[...], 1, 1)
        gate_back = (hidden_back * up * slope).astype(bf16)
        up_back = (hidden_back * value).astype(bf16)
        backs[at, :units] = gate_back
        backs[at, units:] = up_back
        total = dot(gate_back, wg.ref[...], 1, 1) + dot(up_back, wu.ref[...], 1, 1)
        if target is send:
            scatter_pieces(total, send)
        else:
            keep[...] = total


def feed(h0, cots, gain, wg, wu, wd, mixes, projections, chunk, after):
    rows, width = mixes[0].shape[0], h0.shape[1]
    units = wg.shape[1]
    quarter = rows // 2
    return run(
        functools.partial(feed_body, chunk),
        [
            *held(h0, gain, wg, wu, wd),
            *[(array, "any") for array in (*cots, *mixes, *projections)],
        ],
        [
            ((rows, width), f32),
            ((rows, width), bf16),
            ((rows, units), bf16),
            ((rows, 2 * units), bf16),
            ((quarter, width), f32),
            *[(shape, bf16) for shape in in_pieces((quarter, width))],
        ],
        us=6,
        scratch=[
            VMEM((2, quarter, width), bf16),
            VMEM((4, *mixes[0].shape), bf16),
            VMEM((4, *projections[0].shape), bf16),
            pltpu.SemaphoreType.DMA((10,)),
        ],
        after=after,
    )


STREAMS = (1, 2)


def bit_of(distance):
    return lax.rem(lax.div(lax.axis_index("dp"), distance), 2)


def split_sums(total_ref, outs):
    if len(outs) == 1:
        outs[0].ref[...] = total_ref[...]
        outs[0].send()
        return
    for n, distance in enumerate(STREAMS):
        keep, send = outs[2 * n : 2 * n + 2]
        pairs, block, columns = keep.ref.shape
        lanes = slice(n * columns, (n + 1) * columns)
        bit = bit_of(distance)
        for t in range(pairs):
            first = t // distance * 2 * distance + t % distance
            send.ref[t] = total_ref[
                rows_at(first + (1 - bit) * distance, block), lanes
            ].astype(bf16)
            keep.ref[t] = total_ref[rows_at(first + bit * distance, block), lanes]
        send.send()
        keep.send()


def sums_outs(width, columns, peers):
    block = width // peers
    if peers >= 4 and block % 16 == 0:
        shape = (peers // 2, block, columns // 2)
        return [(shape, f32), (shape, bf16)] * 2
    return [((width, columns), f32, 1)]


def feed_grads_body(ins, outs, total_ref):
    n2a, n2b, hiddena, hiddenb, backsa, backsb, wd, *cots = ins
    keep, send = outs[:2]
    place = lax.axis_index("mp")
    core = lax.rem(place, 2)
    quarter = cots[0].target.shape[0]
    units = hiddena.target.shape[1]
    total_ref[:, : 2 * units] = dot(n2a.ref[...], backsa.ref[...], 0, 0) + dot(
        n2b.ref[...], backsb.ref[...], 0, 0
    )
    here = lax.div(place, 2) == 0
    arrays = [one.ref for one in (hiddena, hiddenb, *cots)]
    hiddena, hiddenb, cots = arrays[0], arrays[1], arrays[2:]
    for one, two in ((hiddena, hiddenb), (hiddenb, hiddena)):

        @pl.when(here if one is hiddena else jnp.logical_not(here))
        def summed():
            total = None
            for d, hidden in zip(range(4), (one, one, two, two)):
                at = rows_at(lax.bitwise_xor(core, d % 2), quarter)
                part = dot(cots[d][...], hidden[at, :], 0, 0)
                total = part if total is None else total + part
            total_ref[:, 2 * units :] = total

    split_sums(total_ref, outs[2:])
    for half, target in ((1 - core, send), (core, keep)):
        for chunk, hidden in enumerate((hiddena, hiddenb)):
            target.ref[chunk] = dot(hidden[rows_at(half, quarter), :], wd.ref[...]).astype(
                target.ref.dtype
            )


def feed_grads(n2s, hiddens, backs, wd, cots, peers, after):
    units, width = wd.shape
    quarter = cots[0].shape[0]
    return run(
        feed_grads_body,
        [*held(*n2s, *hiddens, *backs, wd, *cots)],
        [
            ((2, quarter, width), f32),
            ((2, quarter, width), bf16),
            *sums_outs(width, 3 * units, peers),
        ],
        us=6,
        scratch=[VMEM((width, 3 * units), f32)],
        mib=20,
        after=after,
    )


def joint_grads_body(heads, ins, outs, total_ref):
    n1, dqa, dqb, dkv, lowa, lowb, mixa, mixb, tiles = ins
    table_out = outs[0]
    rows, own = dqa.target.shape
    total_ref[:, :own] = dot(n1.ref[:rows, :], dqa.ref[...], 0, 0) + dot(
        n1.ref[rows:, :], dqb.ref[...], 0, 0
    )
    total_ref[:, own : 3 * own] = dot(n1.ref[...], dkv.ref[...], 0, 0)
    total_ref[:, 3 * own :] = dot(lowa.ref[...], mixa.ref[...], 0, 0) + dot(
        lowb.ref[...], mixb.ref[...], 0, 0
    )
    split_sums(total_ref, outs[1:])
    head = iota((8, TILE), 0)
    bucket = iota((8, TILE), 1)
    table = jnp.zeros((8, TILE), f32)
    for h in range(heads):
        sums = {}
        for k in range(5):
            least, most = TILE * (k - 2) - TILE + 1, TILE * (k - 2) + TILE - 1
            tile = tiles.ref[(5 * h + k) * TILE : (5 * h + k + 1) * TILE, :]
            if k in (0, 4):
                b = bucket_of(least if k == 0 else most)
                sums[b] = sums.get(b, 0.0) + folded(tile, jnp.sum)
                continue
            offset = TILE * (k - 2) + iota((TILE, TILE), 0) - iota((TILE, TILE), 1)
            runs = bucket_runs(least, most)
            for n, (first, b) in enumerate(runs):
                held = offset >= first
                if n + 1 < len(runs):
                    held = held & (offset < runs[n + 1][0])
                sums[b] = sums.get(b, 0.0) + folded(jnp.where(held, tile, 0.0), jnp.sum)
        for b, part in sums.items():
            total = jnp.sum(jnp.sum(part, axis=0, keepdims=True), axis=1, keepdims=True)
            table = jnp.where((bucket == b) & (head == h), total, table)
    table_out.ref[...] = table


def joint_grads(n1, dqa, dqb, dkv, lows, mixes, tiles, peers, after):
    width, own = n1.shape[1], dqa.shape[1]
    return run(
        functools.partial(joint_grads_body, own // DH),
        [*held(n1, dqa, dqb, dkv, *lows, *mixes, tiles)],
        [((8, TILE), f32), *sums_outs(width, 4 * own, peers)],
        us=6,
        scratch=[VMEM((width, 4 * own), f32)],
        mib=16,
        after=after,
    )


def sum_body(counts, ins, outs):
    one, *ins = ins
    two, passed = ins[: counts[0]], ins[counts[0] :]
    total, *outs = outs
    pieces, copied = outs[: counts[1]], outs[counts[1] :]
    rows = two[0].ref.shape[0]
    for n, piece in enumerate(two):
        at = slice(n * rows, (n + 1) * rows)
        total.ref[at] = (one.ref[at].astype(f32) + piece.ref[...].astype(f32)).astype(total.ref.dtype)
    if pieces:
        scatter_pieces(total.ref[...], pieces)
    for source, target in zip(passed, copied):
        target.ref[...] = source.ref[...]


def added(one, two, after=(), passed=(), kind=bf16, cut=False):
    pieces = in_pieces(one.shape) if cut else []
    return run(
        functools.partial(sum_body, (len(two), len(pieces))),
        held(one, *two, *passed),
        [
            (one.shape, kind),
            *[(shape, kind) for shape in pieces],
            *[(array.shape, array.dtype) for array in passed],
        ],
        us=1,
        mib=4,
        after=after,
    )


def copy_body(ins, outs):
    outs[0].ref[...] = ins[0].ref[...]


def copied(array, after):
    return run(copy_body, held(array), [(array.shape, array.dtype)], us=1, mib=4, after=after)[0]


def out_split_body(ins, outs):
    keep, received = ins
    mine, far = outs
    side = lax.div(lax.axis_index("mp"), 2)
    mine.ref[...] = keep.ref[side] + received.ref[side].astype(f32)
    far.ref[...] = (keep.ref[1 - side] + received.ref[1 - side].astype(f32)).astype(bf16)


def out_split(keep, received, after=()):
    shape = keep.shape[1:]
    ins = held(keep, received)
    return run(out_split_body, ins, [(shape, f32), (shape, bf16)], us=1, mib=4, after=after)


def out_rows_body(ins, outs, rows_ref):
    h1a, h1b, mine, received = ins
    (out,) = outs
    quarter = mine.ref.shape[0]
    side, core = lax.div(lax.axis_index("mp"), 2), lax.rem(lax.axis_index("mp"), 2)
    for n, h1 in enumerate((h1a, h1b)):

        @pl.when(side == n)
        def taken():
            rows_ref[...] = h1.ref[rows_at(core, quarter), :]

    out.ref[...] = (rows_ref[...] + (mine.ref[...] + received.ref[...].astype(f32))).astype(bf16)


def finished_rows(h1s, mine, received, after=()):
    (rows,) = run(
        out_rows_body,
        [*held(*h1s, mine, received)],
        [(mine.shape, bf16, 1)],
        us=1.5,
        scratch=[VMEM(mine.shape, f32)],
        mib=6,
        after=after,
    )
    return rows


def halve_body(distances, ins, outs):
    for n, distance in enumerate(distances):
        keep, received = ins[2 * n : 2 * n + 2]
        kept, sent = outs[2 * n : 2 * n + 2]
        bit = bit_of(distance)
        for u in range(kept.ref.shape[0]):
            far = 2 * u + 1 - bit
            sent.ref[u] = (keep.ref[far] + received.ref[far].astype(f32)).astype(bf16)
        sent.send()
        for u in range(kept.ref.shape[0]):
            near = 2 * u + bit
            kept.ref[u] = keep.ref[near] + received.ref[near].astype(f32)
        kept.send()


def halve(distances, sums, after):
    outs = []
    for keep in sums[::2]:
        shape = (keep.shape[0] // 2, *keep.shape[1:])
        outs += [(shape, f32), (shape, bf16)]
    return run(
        functools.partial(halve_body, distances),
        [*held(*sums)],
        outs,
        us=2.5,
        mib=4,
        after=after,
    )


def last_sums_body(plan, ins, outs, total_ref):
    columns = ins[0].target.shape[2]
    for n in range(2):
        keep, received = ins[2 * n : 2 * n + 2]
        total_ref[:, n * columns : (n + 1) * columns] = keep.ref[0] + received.ref[0].astype(f32)
    for out, (first, last, turned) in zip(outs, plan):
        part = total_ref[:, first:last]
        out.ref[...] = part.T if turned else part
        out.send()


def last_sums(plan, sums, after):
    block, columns = sums[0].shape[1:]
    shapes = [(last - first, block) if turned else (block, last - first) for first, last, turned in plan]
    return run(
        functools.partial(last_sums_body, plan),
        held(*sums),
        [(shape, f32, 1) for shape in shapes],
        us=2,
        scratch=[VMEM((block, 2 * columns), f32)],
        mib=6,
        after=after,
    )


def finish_body(heads, ins, outs):
    one, two = ins
    score, gain_one, gain_two, table, sizes = [out.ref for out in outs]
    total = one.ref[...] + two.ref[...]
    share, width = score.shape[0], total.shape[1]
    moved = pltpu.roll(total, lax.rem(width - lax.axis_index("dp") * share, width), 1)
    score[...] = moved[0, :share]
    gain_one[...] = total[1]
    gain_two[...] = total[2]
    table[...] = total[4 : 4 + heads, :BUCKETS]
    sizes[...] = (total[3:4, :4] / total[3:4, 4:5])[0]


def finished(one, two, heads, share, after=()):
    width = one.shape[1]
    shapes = [(share,), (width,), (width,), (heads, BUCKETS), (4,)]
    return run(
        functools.partial(finish_body, heads),
        [*held(one, two)],
        [(shape, f32, 1) for shape in shapes],
        us=1,
        mib=4,
        after=after,
    )


def swapped(shard, axis, distance):
    peers = lax.axis_size(axis)
    return lax.ppermute(shard, axis, [(i, i ^ distance) for i in range(peers)])


def summed_but_last(value, axis, order):
    distance, pair = 1, (value, jnp.zeros_like(value))
    while distance < lax.axis_size(axis):
        if distance > 1:
            value, order = added(pair[0], pair[1:], order, kind=f32)[0], ()
        pair = value, swapped(value, axis, distance)
        distance *= 2
    return pair


def scattered(sums):
    peers = lax.axis_size("dp")
    me = lax.axis_index("dp")
    distances = [2**n for n in range(peers.bit_length() - 1)]
    parts = []
    for n, first in enumerate(STREAMS):
        order = sorted(distances, key=lambda d: (d != first, d))
        left = distances[::-1]
        if len(sums) == 4:
            keep, send = sums[2 * n : 2 * n + 2]
            blocks = keep + swapped(send, "dp", first).astype(f32)
            order.pop(0)
            left.remove(first)
        else:
            columns = sums[0].shape[1] // 2
            blocks = sums[0][:, n * columns : (n + 1) * columns]
            blocks = blocks.reshape(peers, -1, columns)
        block, columns = blocks.shape[1:]
        blocks = blocks.reshape(*[2] * len(left), block, columns)
        for distance in order:
            axis = left.index(distance)
            left.remove(distance)
            bit = lax.rem(lax.div(me, distance), 2)
            kept = lax.dynamic_index_in_dim(blocks, bit, axis, keepdims=False)
            sent = lax.dynamic_index_in_dim(blocks, 1 - bit, axis, keepdims=False)
            blocks = kept + swapped(sent.astype(bf16), "dp", distance).astype(f32)
        parts.append(blocks)
    return jnp.concatenate(parts, axis=1)


def body(
    byte_embeds,
    lengths,
    score_weight,
    norm1_gain,
    w_query,
    w_key,
    w_value,
    rel_table,
    w_out,
    norm2_gain,
    w_gate,
    w_up,
    w_down,
    cotangent,
):
    width = byte_embeds.shape[1]
    assert lengths.shape[0] == 1 and lax.axis_size("mp") == 4
    quarter = cotangent.shape[0]
    half = 2 * quarter
    heads = w_query.shape[1] // DH
    units = w_gate.shape[1]
    own = heads * DH
    peers = lax.axis_size("dp")

    cots = [cotangent, swapped(cotangent, "mp", 1), swapped(cotangent, "mp", 2)]
    projections = [w_out, swapped(w_out, "mp", 1), swapped(w_out, "mp", 2)]
    h0, n1, q, k, v, weights, masses, mixing, near, *fetched = pool_forward(
        lengths,
        rel_table.T,
        byte_embeds,
        score_weight,
        norm1_gain,
        w_query.T,
        w_key.T,
        w_value.T,
        norm2_gain,
        w_gate,
        w_up,
        w_down,
        w_out,
        cotangent,
    )
    score_vector, gain_one, wq, wk, wv, gain_two, wg, wu, wd, wo, own_rows = fetched
    mixes, sums, turned = [None, None], [None, None], [None, None]
    mixes[0], sums[0], turned[0] = attend(near, q, k, v, 0, half, [])
    mixes[1], sums[1], turned[1], *passed = attend(
        near, q, k, v, half, half, [mixes[0]], (cots[2], projections[2])
    )
    cots = (own_rows, cots[1], passed[0], swapped(passed[0], "mp", 1))
    projections = (wo, projections[1], passed[1], swapped(passed[1], "mp", 1))
    far = [swapped(mix, "mp", 2) for mix in mixes]
    next_far = copied(far[0], [mixes[1]])
    order = []
    fed, second = [], []
    for chunk in range(2):
        mixed = (mixes[chunk], swapped(mixes[chunk], "mp", 1), far[chunk], swapped(next_far, "mp", 1))
        h1, n2, hidden, backs, keep, *sends = feed(
            h0, cots, gain_two, wg, wu, wd, mixed, projections, chunk, order
        )
        passed = [far[1]] if chunk == 0 else []
        mine, *passed = added(keep, near_pieces(sends), [], passed)
        if passed:
            next_far = passed[0]
        fed.append((h1, n2, hidden, backs))
        second.append((mine, swapped(mine, "mp", 2)))
        order = [mine]
    h1s, n2s, hiddens, backs = zip(*fed)
    out_keep, out_send, *feed_sums = feed_grads(n2s, hiddens, backs, wd, cots, peers, order)
    out_near = swapped(out_send, "mp", 1)

    def received(sums, distances):
        return [
            swapped(sums[k], "dp", distances[k // 2]) if k % 2 else sums[k] for k in range(len(sums))
        ]

    def both(pair, after):
        total, *pieces = added(pair[0], pair[1:], after, cut=True)
        return total, *near_pieces(pieces)

    def back(chunk, pieces, *more):
        return attend_back(
            gain_two, h1s[chunk], q, k, near, sums[chunk], turned[chunk], v, wo, pieces, cots, chunk, *more
        )

    halving = len(feed_sums) == 4 and peers == 8
    lowa, backa, gain_two_sum, dqa, tiles, dk, dv = back(0, both(second[0], [feed_sums[0]]))
    pieces = both(second[1], [lowa])
    out_mine, out_far = out_split(out_keep, out_near, [pieces[0]])
    lowb, backb, gain_two_sum, dqb, tiles, keepa, keepb, dkv, *sends = back(
        1, pieces, (dk, dv, tiles, gain_two_sum, dqa, wq, wk, wv), [out_mine]
    )
    order = [lowb]
    if halving:
        feed_sums = halve(STREAMS[::-1], received(feed_sums, STREAMS), order)
        order = [feed_sums[0]]
    (firsta,) = added(keepa, near_pieces(sends[:PIECES]), order)
    (firstb,) = added(keepb, near_pieces(sends[PIECES:]), [firsta])
    first = [(one, swapped(one, "mp", 2)) for one in (firsta, firstb)]
    table_sum, *joint_sums = joint_grads(
        n1, dqa, dqb, dkv, (lowa, lowb), mixes, tiles, peers, [firstb]
    )
    order = [table_sum]
    feed_plan = ((0, units, False), (units, 2 * units, False), (2 * units, 3 * units, True))
    joint_plan = tuple((n * own, (n + 1) * own, n == 3) for n in range(4))
    if halving:
        feed_sums = halve((4, 4), received(feed_sums, STREAMS[::-1]), order)
        joint_sums = halve(STREAMS[::-1], received(joint_sums, STREAMS), [feed_sums[0]])
        order = [joint_sums[0]]
    firsts = both(first[0], order)
    firsts = [*firsts, *both(first[1], [firsts[0]])]
    factors, small, grad_rows = pool_scores(
        lengths,
        byte_embeds,
        h0,
        (backa, backb),
        gain_one,
        weights,
        gain_two_sum,
        table_sum,
        masses,
        firsts,
        order,
    )
    order = [small]
    if halving:
        joint_sums = halve((4, 4), received(joint_sums, STREAMS[::-1]), order)
        order = [joint_sums[0]]
    (byte_grad,) = pool_bytes(score_vector, mixing, factors, grad_rows, order)
    order = [(byte_grad, pltpu.HBM)]
    if halving:
        feed_parts = last_sums(feed_plan, received(feed_sums, (4, 4)), order)
        order = [(feed_parts[0], pltpu.HBM)]
    out_rows = finished_rows(h1s, out_mine, swapped(out_far, "mp", 2), order)
    if halving:
        joint_parts = last_sums(joint_plan, received(joint_sums, (4, 4)), [(out_rows, pltpu.HBM)])
    else:
        parts = []
        for sums, plan in ((feed_sums, feed_plan), (joint_sums, joint_plan)):
            total = scattered(sums)
            parts.append([total[:, a:b].T if turned else total[:, a:b] for a, b, turned in plan])
        feed_parts, joint_parts = parts
    score_part, gain_one_part, gain_two_part, table_part, size_dist = finished(
        *summed_but_last(small, "dp", [(byte_grad, pltpu.HBM)]),
        heads,
        width // peers,
        [(joint_parts[0], pltpu.HBM)] if halving else [],
    )
    return (
        out_rows,
        byte_grad,
        score_part,
        gain_one_part,
        *joint_parts[:3],
        table_part.T,
        joint_parts[3],
        gain_two_part,
        *feed_parts,
        size_dist,
    )


def solution(mesh):
    placed = (
        P("dp", None),
        P("dp"),
        P(),
        P(),
        P(None, "mp"),
        P(None, "mp"),
        P(None, "mp"),
        P(None, "mp"),
        P("mp", None),
        P(),
        P(None, "mp"),
        P(None, "mp"),
        P("mp", None),
        P(("dp", "mp"), None),
    )
    return jax.shard_map(
        body,
        mesh=mesh,
        in_specs=placed,
        out_specs=(
            P(("dp", "mp"), None),
            P("dp", None),
            P("dp"),
            P(),
            P("dp", "mp"),
            P("dp", "mp"),
            P("dp", "mp"),
            P(None, "mp"),
            P("mp", "dp"),
            P(),
            P("dp", "mp"),
            P("dp", "mp"),
            P("mp", "dp"),
            P(),
        ),
        check_vma=False,
    )
```

```python
import functools

import jax
import jax.numpy as jnp
from jax import lax
from jax.experimental import pallas as pl
from jax.experimental.pallas import tpu as pltpu
from jax.sharding import PartitionSpec as P

DH = 64
BUCKETS = 32
TILE = 128
POOL_BYTES = 192
QUERY_ROWS = 256

epsilon = 1e-06
bucket_edges = (12, 16, 23, 32, 46, 64, 91)
highest = lax.Precision.HIGHEST
f32 = jnp.float32
bf16 = jnp.bfloat16
SMEM = pltpu.SMEM
VMEM = pltpu.VMEM


def bucket_of(offset):
    distance = abs(offset)
    near = distance if distance < 8 else 8 + sum(distance >= edge for edge in bucket_edges)
    return near + (16 if offset > 0 else 0)


def bucket_runs(least, most):
    runs = [(least, bucket_of(least))]
    for offset in range(least + 1, most + 1):
        if bucket_of(offset) != runs[-1][1]:
            runs.append((offset, bucket_of(offset)))
    return runs


def iota(shape, dim):
    return lax.broadcasted_iota(jnp.int32, shape, dim)


def dot(left, right, left_dim=1, right_dim=0, precision=None):
    return lax.dot_general(
        left,
        right,
        (((left_dim,), (right_dim,)), ((), ())),
        precision=precision,
        preferred_element_type=f32,
    )


def two_parts(value):
    high = value.astype(bf16)
    return high, (value - high.astype(f32)).astype(bf16)


class Held:
    def __init__(self, ref):
        self.ref = self.target = ref

    def upto(self, row):
        return self.ref

    def send(self, *at):
        pass


class Loaded:
    def __init__(self, source, target, semaphores):
        rows = source.shape[0] // len(semaphores)
        self.rows, self.target, self.waited = rows, target, set()
        if len(semaphores) == 1:
            self.copies = [pltpu.make_async_copy(source, target, semaphores[0])]
            return
        self.copies = [
            pltpu.make_async_copy(
                source.at[pl.ds(k * rows, rows)], target.at[pl.ds(k * rows, rows)], semaphore
            )
            for k, semaphore in enumerate(semaphores)
        ]

    def start(self):
        for copy in self.copies:
            copy.start()

    def upto(self, row):
        for k, copy in enumerate(self.copies):
            if k * self.rows < row and k not in self.waited:
                copy.wait()
                self.waited.add(k)
        return self.target

    @property
    def ref(self):
        return self.upto(self.target.shape[0])


class Stored:
    def __init__(self, source, target, semaphores):
        self.ref, self.target, self.semaphores, self.copies = source, target, semaphores, []

    def send(self, *at):
        source, target = (self.ref.at[at], self.target.at[at]) if at else (self.ref, self.target)
        copy = pltpu.make_async_copy(source, target, self.semaphores[len(self.copies)])
        copy.start()
        self.copies.append(copy)


def run(body, ins, outs, us, scratch=(), mib=24, after=()):
    loaded = [(array, how) for array, how in ins if isinstance(how, int)]
    copied = [out[2] if len(out) == 3 else 0 for out in outs]
    count, more = len(ins), len(after)

    def kernel(*refs):
        sources = refs[:count]
        targets = refs[count + more : count + more + len(outs)]
        rest = list(refs[count + more + len(outs) :])
        stages = [rest.pop(0) for _ in loaded]
        results = [rest.pop(0) if moved else None for moved in copied]
        load_semaphores = rest.pop(0) if loaded else None
        store_semaphores = rest.pop(0) if sum(copied) else None
        given, used, stored, first = [], 0, [], 0
        for source, (_, how) in zip(sources, ins):
            if how == "vmem":
                given.append(Held(source))
            elif not isinstance(how, int):
                given.append(source)
            else:
                semaphores = [load_semaphores.at[used + k] for k in range(how)]
                given.append(Loaded(source, stages.pop(0), semaphores))
                given[-1].start()
                used += how
        for result, target, moved in zip(results, targets, copied):
            if not moved:
                stored.append(Held(target))
                continue
            semaphores = [store_semaphores.at[first + n] for n in range(moved)]
            stored.append(Stored(result, target, semaphores))
            first += moved
        body(given, stored, *rest)
        for array in given:
            if isinstance(array, Loaded):
                array.ref
        sent = [result for result in stored if isinstance(result, Stored)]
        for result in sent:
            if not result.copies:
                result.send()
        for result in sent:
            for copy in result.copies:
                copy.wait()

    spaces = {"smem": SMEM, "vmem": VMEM, "any": pl.ANY}
    arrays = [
        pltpu.with_memory_space_constraint(array, pltpu.HBM)
        if how == "hbm" or isinstance(how, int)
        else array
        for array, how in ins
    ]
    return pl.pallas_call(
        kernel,
        out_shape=[
            pltpu.HBM(*out[:2]) if moved else jax.ShapeDtypeStruct(*out)
            for out, moved in zip(outs, copied)
        ],
        in_specs=[
            *[pl.BlockSpec(memory_space=spaces.get(how, pltpu.HBM)) for _, how in ins],
            *[pl.BlockSpec(memory_space=pl.ANY)] * more,
        ],
        out_specs=[pl.BlockSpec(memory_space=pltpu.HBM if moved else VMEM) for moved in copied],
        scratch_shapes=[
            *[VMEM(array.shape, array.dtype) for array, _ in loaded],
            *[VMEM(*out[:2]) for out, moved in zip(outs, copied) if moved],
            *([pltpu.SemaphoreType.DMA((sum(how for _, how in loaded),))] if loaded else []),
            *([pltpu.SemaphoreType.DMA((sum(copied),))] if sum(copied) else []),
            *scratch,
        ],
        cost_estimate=pl.CostEstimate(flops=1, transcendentals=0, bytes_accessed=1),
        compiler_params=pltpu.CompilerParams(vmem_limit_bytes=mib * 2**20),
    )(*arrays, *[pltpu.with_memory_space_constraint(*a) if isinstance(a, tuple) else a for a in after])


def held(*arrays):
    return [(array, "vmem") for array in arrays]


def started(*copies):
    for copy in copies:
        copy.start()
    return copies


def fetch_owned(pieces, owners, place, target):
    for n, owner in enumerate(owners):
        for d, piece in enumerate(pieces):

            @pl.when(lax.bitwise_xor(place, d) == owner)
            def taken():
                target[n] = piece.ref[...]


def fetch_pair(core, mine, others, target, at):
    rows = others[0].ref.shape[0]
    target[at + core] = mine.ref[...]
    for n, piece in enumerate(others):
        target[at + 1 - core, n * rows : (n + 1) * rows] = piece.ref[...]


PIECES = 2


def in_pieces(shape):
    return [(shape[0] // PIECES, *shape[1:])] * PIECES


def scatter_pieces(value, pieces):
    rows = pieces[0].ref.shape[0]
    for n, piece in enumerate(pieces):
        piece.ref[...] = value[n * rows : (n + 1) * rows].astype(piece.ref.dtype)


def near_pieces(pieces):
    return [swapped(piece, "mp", 1) for piece in pieces]


def rows_at(index, count):
    return pl.ds(pl.multiple_of(index * count, count), count)


def pair_sums(even, odd):
    count = even.shape[1]
    lane = iota(even.shape, 1)

    def after(value, k):
        return jnp.where(lane < count - k, pltpu.roll(value, count - k, 1), 0.0)

    def before(value, k):
        return pltpu.roll(value, k, 1)

    two = even + odd
    first = lax.rem(lane, 2) == 0
    four = two + after(two, 1)
    four = jnp.where(first, four, before(four, 1))
    place = lax.rem(lane, 3)
    early = two + after(even, 1)
    late = after(odd, 1) + after(two, 2)
    far = before(late, 2)
    three_even = jnp.where(place == 0, early, jnp.where(place == 1, before(early, 1), far))
    three_odd = jnp.where(place == 0, early, jnp.where(place == 1, before(late, 1), far))
    return [(even, odd), (two, two), (three_even, three_odd), (four, four)]


def by_row(rows):
    shape = (8, rows[0].shape[1])
    place = iota(shape, 0)
    result = jnp.zeros(shape, f32)
    for k, row in enumerate(rows):
        result = jnp.where(place == k, row, result)
    return result


def pool_masks(byte_count, lanes):
    byte = iota((byte_count, 1), 0)
    row = iota((1, lanes), 1)
    return [
        (0, True, False, byte == 2 * row),
        (0, False, True, byte == 2 * row + 1),
        (1, True, True, lax.div(byte, 2) == row),
        (2, True, False, lax.div(byte, 3) == lax.div(2 * row, 3)),
        (2, False, True, lax.div(byte, 3) == lax.div(2 * row + 1, 3)),
        (3, True, True, lax.div(byte, 4) == lax.div(row, 2)),
    ]


def pool_chunks(byte_total):
    return [(at, min(POOL_BYTES, byte_total - at)) for at in range(0, byte_total, POOL_BYTES)]


def near_bias(table, heads, near_ref):
    for k in range(5):
        middle = TILE * (k - 2)
        if k in (0, 4):
            runs = [(middle, bucket_of(middle))]
        else:
            runs = bucket_runs(middle - TILE + 1, middle + TILE - 1)
        offset = middle + iota((TILE, TILE), 0) - iota((TILE, TILE), 1)
        values = [[table[h : h + 1, bucket : bucket + 1] for _, bucket in runs] for h in range(heads)]
        tiles = [jnp.broadcast_to(values[h][0], (TILE, TILE)) for h in range(heads)]
        for n in range(1, len(runs)):
            past = offset >= runs[n][0]
            tiles = [jnp.where(past, values[h][n], tiles[h]) for h in range(heads)]
        for h in range(heads):
            near_ref[(5 * h + k) * TILE : (5 * h + k + 1) * TILE, :] = tiles[h]


def as_row(vector_ref):
    return vector_ref[...].astype(f32).reshape(1, -1)


def byte_scores(parts, vector, scores_ref):
    columns = jnp.broadcast_to(vector, (TILE, vector.shape[1])).T.astype(bf16)
    for part in parts:
        at, x = part()
        scores_ref[at, :] = dot(x, columns)
    half = scores_ref.shape[0] // 2
    return [scores_ref[pl.ds(k, half, stride=2), :].T[:8] for k in range(2)]


X_PARTS = 4


def pool_body(ins, outs, scores_ref, semaphores):
    length_ref, table, x, *sources = ins
    h0, n1, q, k, v, weights, masses, mixing, near, *fetched = outs
    copies = started(
        *[
            pltpu.make_async_copy(source, target.ref, semaphores.at[n])
            for n, (source, target) in enumerate(zip(sources, fetched))
        ]
    )
    score_row, gain_row, wq, wk, wv = fetched[:5]
    byte_total, width = x.target.shape
    share = byte_total // X_PARTS
    heads = table.target.shape[0]
    own = heads * DH
    length = length_ref[0]
    valid = lax.div(length + 1, 2)
    near_bias(table.ref[...].astype(f32), heads, near.ref)
    for copy in copies[:2]:
        copy.wait()

    def part(n):
        x.upto((n + 1) * share)
        return pl.ds(n * share, share), x.target[n * share : (n + 1) * share, :]

    row = iota((8, byte_total // 2), 1)
    inside = (2 * row < length, 2 * row + 1 < length)
    parts = [functools.partial(part, n) for n in range(X_PARTS)]
    scores = byte_scores(parts, as_row(score_row.ref), scores_ref)
    scores = [jnp.where(known, score, 0.0) for known, score in zip(inside, scores)]
    sums = pair_sums(*scores)
    sized = []
    for odd in range(2):
        logits = [pair[odd] / (b + 1) for b, pair in enumerate(sums)]
        peak = functools.reduce(jnp.maximum, logits)
        shifted = [jnp.exp(logit - peak) for logit in logits]
        mass = functools.reduce(jnp.add, shifted)
        sized.append(by_row([one / mass for one in shifted]))
    weights.ref[:8] = sized[0]
    weights.ref[8:] = sized[1]
    total = sum(
        jnp.sum(jnp.where(known, one, 0.0), axis=1, keepdims=True) for known, one in zip(inside, sized)
    )
    masses.ref[...] = jnp.broadcast_to(total, masses.ref.shape)
    gain = as_row(gain_row.ref)
    for at, count in pool_chunks(byte_total):
        rows = count // 2
        start = at // 2
        blank = jnp.zeros((8, TILE - rows), f32)
        even, odd = [jnp.concatenate((one[:, start : start + rows], blank), axis=1) for one in sized]
        part = jnp.zeros((count, TILE), f32)
        for b, for_even, for_odd, mask in pool_masks(count, TILE):
            line = even if not for_odd else odd if not for_even else even + odd
            part = part + jnp.where(mask, line[b : b + 1] / (2 * b + 2), 0.0)
        part = jnp.where(iota((count, 1), 0) + at < length, part, 0.0)
        both = jnp.concatenate(two_parts(part), axis=1)
        mixing.ref[at : at + count, :] = both
        pooled = dot(both, x.ref[at : at + count, :], 0, 0)
        pooled = pooled[:rows] + pooled[TILE : TILE + rows]
        h0.ref[start : start + rows, :] = pooled
        scale = lax.rsqrt(jnp.mean(pooled * pooled, axis=1, keepdims=True) + epsilon)
        n1.ref[start : start + rows, :] = (pooled * scale * gain).astype(bf16)
    for copy in copies[2:]:
        copy.wait()
    normed = n1.ref[...]
    rows, padding = normed.shape[0], q.ref.shape[1] - own
    first = iota((rows, padding), 1) == 0
    masked = iota((rows, padding), 0) >= valid
    q.ref[:, own:] = jnp.where(first, 1.0, 0.0).astype(bf16)
    k.ref[:, own:] = jnp.where(first & masked, -1e30, 0.0).astype(bf16)
    v.ref[:, own:] = jnp.zeros((rows, padding), bf16)
    for out, weight in ((q, wq), (k, wk), (v, wv)):
        out.ref[:, :own] = dot(normed, weight.ref[...], 1, 1).astype(bf16)
        out.send()


def pool_forward(length, table, x, *fetched):
    byte_total, width = x.shape
    rows = byte_total // 2
    heads = table.shape[0]
    padded = heads * DH + DH
    return run(
        pool_body,
        [(length, "smem"), (table, 1), (x, X_PARTS), *[(array, "hbm") for array in fetched]],
        [
            ((rows, width), f32),
            ((rows, width), bf16),
            ((rows, padded), bf16),
            ((rows, padded), bf16),
            ((rows, padded), bf16),
            ((16, rows), f32),
            ((8, TILE), f32),
            ((byte_total, 2 * TILE), bf16),
            ((5 * heads * TILE, TILE), f32),
            *[(array.shape, array.dtype) for array in fetched],
        ],
        us=10,
        scratch=[
            VMEM((byte_total, TILE), f32),
            pltpu.SemaphoreType.DMA((len(fetched),)),
        ],
    )


def pool_scores_body(ins, outs, back_ref, rows_ref):
    length_ref, x, h0, backa, backb, gain, weights, gain_grad, table, masses, *pieces = ins
    factors, small, rows_out = outs
    core = lax.rem(lax.axis_index("mp"), 2)
    each = 1 + PIECES
    for n in range(2):
        fetch_pair(
            core, pieces[each * n], pieces[each * n + 1 : each * n + each], rows_ref, 2 * n
        )
    byte_total, width = x.target.shape
    rows_total = byte_total // 2
    quarter = rows_ref.shape[1]
    length = length_ref[0]
    gain = as_row(gain.ref)
    grad_rows = rows_out.ref
    gain_sum = jnp.zeros((1, width), f32)
    for chunk, back in enumerate((backa, backb)):
        for half in range(2):
            n = 2 * chunk + half
            at = slice(n * quarter, (n + 1) * quarter)
            total, added = norm_back(h0.ref[at, :], gain, rows_ref[n])
            gain_sum = gain_sum + added
            total = total + back.ref[half * quarter : (half + 1) * quarter, :]
            grad_rows[at, :] = total.astype(bf16)
    rows_out.send()
    for at, count in pool_chunks(byte_total):
        rows = count // 2
        start = at // 2
        product = dot(x.upto(at + count)[at : at + count, :], grad_rows[start : start + rows, :], 1, 1)
        product = jnp.where(iota((count, 1), 0) + at < length, product, 0.0)
        even, odd = [None] * 4, [None] * 4
        for b, for_even, for_odd, mask in pool_masks(count, rows):
            total = jnp.sum(jnp.where(mask, product, 0.0), axis=0, keepdims=True) / (2 * b + 2)
            if for_even:
                even[b] = total
            if for_odd:
                odd[b] = total
        back_ref[:8, start : start + rows] = by_row(even)
        back_ref[8:, start : start + rows] = by_row(odd)
    logit_back = []
    for odd in range(2):
        weight = weights.ref[8 * odd : 8 * odd + 8, :]
        back = back_ref[8 * odd : 8 * odd + 8, :]
        logit_back.append(weight * (back - jnp.sum(weight * back, axis=0, keepdims=True)))
    place = iota((8, rows_total), 0)
    row = iota((1, rows_total), 1)
    sums = pair_sums(*logit_back)
    lines = []
    for odd in range(2):
        picked = jnp.zeros((8, rows_total), f32)
        for b, pair in enumerate(sums):
            picked = picked + jnp.where(place == b, pair[odd] / (b + 1), 0.0)
        total = jnp.sum(picked, axis=0, keepdims=True)
        lines += two_parts(jnp.where(2 * row + odd < length, total, 0.0))
    place = iota((16, rows_total), 0)
    stacked = jnp.zeros((16, rows_total), f32)
    for k, line in enumerate(lines):
        stacked = jnp.where(place == k, line.astype(f32), stacked)
    stacked = stacked.astype(bf16)
    total = jnp.zeros((16, width), f32)
    for at, count in pool_chunks(byte_total):
        rows = count // 2
        part = stacked[:, at // 2 : at // 2 + rows]
        byte = iota((rows, count), 1)
        row = iota((rows, count), 0)
        picks = [jnp.where(byte == 2 * row + odd, 1.0, 0.0).astype(bf16) for odd in range(2)]
        upper = iota((16, rows), 0) < 2
        zero = jnp.zeros_like(part)
        spread = dot(jnp.where(upper, part.astype(f32), 0.0).astype(bf16), picks[0]) + dot(
            jnp.where(upper, 0.0, part.astype(f32)).astype(bf16), picks[1]
        )
        spread = spread.astype(bf16)
        factors.ref[:, at : at + count] = spread
        total = total + dot(spread, x.ref[at : at + count, :])
    small.ref[0:1, :] = jnp.sum(total, axis=0, keepdims=True)
    small.ref[1:2, :] = gain_sum
    small.ref[2:3, :] = gain_grad.ref[...]
    small.ref[3:, :] = jnp.zeros((5, width), f32)
    lane = iota((1, TILE), 1)
    sizes = jnp.where(lane == 4, length.astype(f32), 0.0)
    for b in range(4):
        sizes = sizes + jnp.where(lane == b, masses.ref[b : b + 1, :], 0.0)
    small.ref[3:4, :TILE] = sizes
    small.ref[4:8, :TILE] = table.ref[:4, :]


def pool_scores(length, x, h0, backs, gain, weights, gain_grad, table, masses, pieces, after):
    byte_total, width = x.shape
    quarter = pieces[0].shape[0]
    return run(
        pool_scores_body,
        [
            (length, "smem"),
            (x, X_PARTS),
            *held(h0, *backs, gain, weights, gain_grad, table, masses),
            *held(*pieces),
        ],
        [
            ((16, byte_total), bf16),
            ((8, width), f32),
            ((byte_total // 2, width), bf16),
        ],
        us=6,
        scratch=[
            VMEM((16, byte_total // 2), f32),
            VMEM((4, quarter, width), bf16),
        ],
        after=after,
    )


def pool_bytes_body(ins, outs, twice_ref):
    score_row, mixing, factors, grad_rows = [one.ref for one in ins]
    (byte_grad,) = outs
    byte_total, width = byte_grad.ref.shape
    vector = jnp.broadcast_to(as_row(score_row), (16, width)).astype(bf16)
    chunks = pool_chunks(byte_total)
    sent, known = 0, None
    for n, (at, count) in enumerate(chunks):
        rows = count // 2
        g = grad_rows[at // 2 : at // 2 + rows, :]
        both = mixing[at : at + count, :]
        if rows != known:
            twice_ref[...] = jnp.zeros_like(twice_ref)
            known = rows
        twice_ref[:rows, :] = g
        twice_ref[TILE : TILE + rows, :] = g
        back = dot(both, twice_ref[...]) + dot(factors[:, at : at + count], vector, 0, 0)
        byte_grad.ref[at : at + count, :] = back.astype(bf16)
        if n % 4 == 3 or n + 1 == len(chunks):
            byte_grad.send(pl.ds(sent, at + count - sent))
            sent = at + count


def pool_bytes(score_weight, mixing, factors, grad_rows, after):
    byte_total, width = mixing.shape[0], grad_rows.shape[1]
    return run(
        pool_bytes_body,
        held(score_weight, mixing, factors, grad_rows),
        [((byte_total, width), bf16, 4)],
        us=5,
        scratch=[VMEM((2 * TILE, width), bf16)],
        after=after,
    )


def norm_back(value, gain, incoming):
    incoming = incoming.astype(f32)
    scale = lax.rsqrt(jnp.mean(value * value, axis=1, keepdims=True) + epsilon)
    unit = value * scale
    product = incoming * unit
    inner = jnp.mean(product * gain, axis=1, keepdims=True)
    return scale * (incoming * gain - unit * inner), jnp.sum(product, axis=0, keepdims=True)


def head_lanes(width, first, last, more=None):
    lane = iota((1, width), 1)
    keep = (lane >= first) & (lane < last)
    if more is not None:
        keep = keep | (lane == more)
    return jnp.where(keep, 1.0, 0.0).astype(bf16)


def bias_rows(head, distance):
    place = 5 * head + min(max(distance + 2, 0), 4)
    return slice(place * TILE, (place + 1) * TILE)


def folded(value, op):
    return op(value.reshape(-1, 8, value.shape[1]), axis=0)


def attend_body(heads, first_block, ins, outs, vt_ref, *semaphores):
    q, k, near, v, *passed = ins
    mix, sums, out_t, *copied = outs
    copies = started(
        *[
            pltpu.make_async_copy(source, target.ref, semaphores[0].at[n])
            for n, (source, target) in enumerate(zip(passed, copied))
        ]
    )
    own = heads * DH
    key_rows, width = k.target.shape
    halves = QUERY_ROWS // TILE
    keys = k.ref[...]
    for step in range(mix.ref.shape[0] // QUERY_ROWS):
        first = (first_block + step) * QUERY_ROWS
        queries = q.ref[first : first + QUERY_ROWS, :]
        columns = slice(step * QUERY_ROWS, (step + 1) * QUERY_ROWS)
        mixed = []
        for h in range(heads):
            scores = dot(keys, queries * head_lanes(width, h * DH, h * DH + DH, own), 1, 1)
            probs, log_sums, masses = [], [], []
            for half in range(halves):
                query_tile = first // TILE + half
                tiles, peak = [], None
                for j in range(key_rows // TILE):
                    tile = scores[j * TILE : (j + 1) * TILE, half * TILE : (half + 1) * TILE]
                    tile = tile + near.ref[bias_rows(h, j - query_tile), :]
                    top = folded(tile, jnp.max)
                    peak = top if peak is None else jnp.maximum(peak, top)
                    tiles.append(tile)
                peak = jnp.max(peak, axis=0, keepdims=True)
                mass, column = None, []
                for tile in tiles:
                    shifted = jnp.exp(tile - peak)
                    part = folded(shifted, jnp.sum)
                    mass = part if mass is None else mass + part
                    column.append(shifted.astype(bf16))
                mass = jnp.sum(mass, axis=0, keepdims=True)
                probs.append(jnp.concatenate(column, axis=0))
                masses.append(mass)
                log_sums.append(peak + jnp.log(mass))
            prob = jnp.concatenate(probs, axis=1)
            if step == 0 and h == 0:
                vt_ref[...] = v.ref[...].T
            out = dot(vt_ref[h * DH : (h + 1) * DH, :], prob)
            out = out / jnp.concatenate(masses, axis=1)
            out_t.ref[h * DH : (h + 1) * DH, columns] = out
            mixed.append(out)
            sums.ref[h : h + 1, columns] = jnp.concatenate(log_sums, axis=1)
        mixed.append(jnp.zeros((width - own, QUERY_ROWS), f32))
        mix.ref[columns, :] = jnp.concatenate(mixed, axis=0).T[:, :own].astype(bf16)
    for copy in copies:
        copy.wait()


def attend(near, q, k, v, first_row, row_count, after, passed=()):
    key_rows, width = k.shape
    heads = (width - DH) // DH
    return run(
        functools.partial(attend_body, heads, first_row // QUERY_ROWS),
        [*held(q, k, near, v), *[(array, "any") for array in passed]],
        [
            ((row_count, heads * DH), bf16),
            ((8, row_count), f32),
            ((heads * DH, row_count), f32),
            *[(array.shape, array.dtype) for array in passed],
        ],
        us=4,
        scratch=[
            VMEM((width, key_rows), bf16),
            *([pltpu.SemaphoreType.DMA((len(passed),))] if passed else []),
        ],
        mib=16,
        after=after,
    )


def attend_back_body(chunk, last, ins, outs, rows_ref, dy_ref, kt_ref, mb_ref, *scratch):
    gain, h1, q, k, near, sums, turned, v, wo, *ins = ins
    if last:
        dk_in, dv_in, tiles_in, gain_in, dqa, wq, wk, wv, *ins = ins
        low, back, gain_out, dq, tiles_out, keepa, keepb, dkv, *sends = outs
        dk_ref, dv_ref, *scratch = scratch
    else:
        low, back, gain_out, dq, tiles_out, dk_out, dv_out = outs
        dk_ref, dv_ref = dk_out.ref, dv_out.ref
    place = lax.axis_index("mp")
    core = lax.rem(place, 2)
    fetch_pair(core, ins[0], ins[1 : 1 + PIECES], rows_ref, 0)
    fetch_owned(ins[1 + PIECES :], (2 * chunk, 2 * chunk + 1), place, dy_ref)
    quarter, model = dy_ref.shape[1:]
    gain = as_row(gain.ref)
    gain_sum = gain_in.ref[...] if last else jnp.zeros((1, model), f32)
    for half in range(2):
        at = slice(half * quarter, (half + 1) * quarter)
        total, added = norm_back(h1.ref[at, :], gain, rows_ref[half])
        gain_sum = gain_sum + added
        total = total + dy_ref[half].astype(f32)
        back.ref[at, :] = total
        low.ref[at, :] = total.astype(bf16)
    gain_out.ref[...] = gain_sum
    gain_out.send()
    back.send()
    low.send()

    key_rows, width = k.target.shape
    own = wo.target.shape[0]
    heads = own // DH
    halves = QUERY_ROWS // TILE
    kt_ref[...] = k.ref[...].T
    if last:
        dk_ref, dv_ref = dk_in.ref, dv_in.ref
        tiles_out.ref[...] = tiles_in.ref[...]
    else:
        tiles_out.ref[...] = jnp.zeros_like(tiles_out.ref)
    keys, values = k.ref[...], v.ref[...]
    for step in range(2 * quarter // QUERY_ROWS):
        columns = slice(step * QUERY_ROWS, (step + 1) * QUERY_ROWS)
        first = chunk * 2 * quarter + step * QUERY_ROWS
        queries = q.ref[first : first + QUERY_ROWS, :]
        mb_ref[:, :own] = dot(low.ref[columns, :], wo.ref[...], 1, 1).astype(bf16)
        mb_ref[:, own:] = jnp.zeros((QUERY_ROWS, width - own), bf16)
        mb = mb_ref[...]
        weighted = mb.astype(f32).T[:own] * turned.ref[:, columns]
        all_probs, all_backs, all_mb, all_q, query_back = [], [], [], [], []
        for h in range(heads):
            only = head_lanes(width, h * DH, h * DH + DH)
            scores = dot(keys, queries * head_lanes(width, h * DH, h * DH + DH, own), 1, 1)
            own_mb = mb * only
            prob_back = dot(values, own_mb, 1, 1)
            inner = jnp.sum(weighted[h * DH : (h + 1) * DH], axis=0, keepdims=True)
            low_columns, back_columns = [], []
            for half in range(halves):
                query_tile = first // TILE + half
                lanes = slice(half * TILE, (half + 1) * TILE)
                at = step * QUERY_ROWS + half * TILE
                log_sum = sums.ref[h : h + 1, at : at + TILE]
                low_column, back_column = [], []
                for j in range(key_rows // TILE):
                    rows = slice(j * TILE, (j + 1) * TILE)
                    table_rows = bias_rows(h, j - query_tile)
                    prob = jnp.exp(scores[rows, lanes] + (near.ref[table_rows, :] - log_sum))
                    score_back = prob * (prob_back[rows, lanes] - inner[:, lanes])
                    low_column.append(prob.astype(bf16))
                    back_column.append(score_back.astype(bf16))
                    tiles_out.ref[table_rows, :] += back_column[-1].astype(f32)
                low_columns.append(jnp.concatenate(low_column, axis=0))
                back_columns.append(jnp.concatenate(back_column, axis=0))
            score_back = jnp.concatenate(back_columns, axis=1)
            all_probs.append(jnp.concatenate(low_columns, axis=1))
            all_backs.append(score_back)
            all_mb.append(own_mb)
            all_q.append(queries * only)
            query_back.append(dot(kt_ref[h * DH : (h + 1) * DH, :], score_back))
        value_back = dot(jnp.concatenate(all_probs, axis=1), jnp.concatenate(all_mb, axis=0))
        key_back = dot(jnp.concatenate(all_backs, axis=1), jnp.concatenate(all_q, axis=0))
        if last or step:
            dv_ref[...] += value_back
            dk_ref[...] += key_back
        else:
            dv_ref[...] = value_back
            dk_ref[...] = key_back
        query_back.append(jnp.zeros((width - own, QUERY_ROWS), f32))
        dq.ref[columns, :] = jnp.concatenate(query_back, axis=0).T[:, :own].astype(bf16)
    tiles_out.send()
    dq.send()
    if not last:
        return
    dkv.ref[:, :own] = dk_ref[:, :own].astype(bf16)
    dkv.ref[:, own:] = dv_ref[:, :own].astype(bf16)
    dkv.send()
    for place, sent in ((1 - core, True), (core, False)):
        local = rows_at(place, quarter)
        for chunk, query_back in enumerate((dqa, dq)):
            rows = rows_at(2 * chunk + place, quarter)
            total = dot(query_back.ref[local, :], wq.ref[...])
            total = total + dot(dkv.ref[rows, :own], wk.ref[...])
            total = total + dot(dkv.ref[rows, own:], wv.ref[...])
            if sent:
                scatter_pieces(total, sends[PIECES * chunk : PIECES * (chunk + 1)])
            else:
                (keepa, keepb)[chunk].ref[...] = total


def attend_back(gain, h1, q, k, near, sums, turned, v, wo, pieces, cots, chunk, kept=None, after=()):
    key_rows, width = k.shape
    rows, model = h1.shape
    own = wo.shape[0]
    quarter = rows // 2
    last = kept is not None
    outs = [
        ((rows, model), bf16),
        ((rows, model), f32),
        ((1, model), f32),
        ((rows, own), bf16),
        (near.shape, f32),
    ]
    sums_shape = ((key_rows, width), f32)
    if last:
        outs += [
            ((quarter, model), f32),
            ((quarter, model), f32),
            ((key_rows, 2 * own), bf16),
            *[(shape, bf16) for shape in 2 * in_pieces((quarter, model))],
        ]
    else:
        outs += [sums_shape, sums_shape]
    return run(
        functools.partial(attend_back_body, chunk, last),
        [
            *held(gain, h1, q, k, near, sums, turned, v, wo, *(kept or ()), *pieces, *cots),
        ],
        outs,
        us=12 if last else 10,
        scratch=[
            VMEM((2, quarter, model), bf16),
            VMEM((2, quarter, model), bf16),
            VMEM((width, key_rows), bf16),
            VMEM((QUERY_ROWS, width), bf16),
            *([VMEM(*sums_shape), VMEM(*sums_shape)] if last else []),
        ],
        mib=20,
        after=after,
    )


def gelu_parts(gate):
    factor = (2.0 / jnp.pi) ** 0.5
    square = gate * gate
    bent = jnp.tanh(factor * gate * (1.0 + 0.044715 * square))
    value = 0.5 * gate * (1.0 + bent)
    slope = 0.5 * (1.0 + bent) + 0.5 * gate * (1.0 - bent * bent) * (
        factor * (1.0 + 3 * 0.044715 * square)
    )
    return value, slope


def feed_body(chunk, ins, outs, dy_ref, parts_ref):
    h0, gain, wg, wu, wd, *pieces = ins
    cots, mixes, projections = pieces[:4], pieces[4:8], pieces[8:12]
    h1, n2, hidden, backs, keep = [one.ref for one in outs[:5]]
    send = outs[5:]
    place = lax.axis_index("mp")
    core = lax.rem(place, 2)
    quarter = keep.shape[0]
    rows = 2 * quarter
    units = wg.ref.shape[1]
    fetch_owned(cots, (2 * chunk, 2 * chunk + 1), place, dy_ref)
    gain = as_row(gain.ref)
    for half in range(2):
        at = slice(half * quarter, (half + 1) * quarter)
        for d in range(4):
            parts_ref[lax.bitwise_xor(place, d)] = dot(mixes[d].ref[at, :], projections[d].ref[...])
        after = h0.ref[chunk * rows + half * quarter : chunk * rows + (half + 1) * quarter, :]
        for owner in range(4):
            after = after + parts_ref[owner]
        h1[at, :] = after
        scale = lax.rsqrt(jnp.mean(after * after, axis=1, keepdims=True) + epsilon)
        n2[at, :] = (after * scale * gain).astype(bf16)
    for half, target in ((1 - core, send), (core, keep)):
        at = rows_at(half, quarter)
        normed = n2[at, :]
        gate = dot(normed, wg.ref[...])
        up = dot(normed, wu.ref[...])
        value, slope = gelu_parts(gate)
        hidden[at, :] = (value * up).astype(bf16)
        hidden_back = dot(dy_ref[half], wd.ref[...], 1, 1)
        gate_back = (hidden_back * up * slope).astype(bf16)
        up_back = (hidden_back * value).astype(bf16)
        backs[at, :units] = gate_back
        backs[at, units:] = up_back
        total = dot(gate_back, wg.ref[...], 1, 1) + dot(up_back, wu.ref[...], 1, 1)
        if target is send:
            scatter_pieces(total, send)
        else:
            keep[...] = total


def feed(h0, cots, gain, wg, wu, wd, mixes, projections, chunk, after):
    rows, width = mixes[0].shape[0], h0.shape[1]
    units = wg.shape[1]
    quarter = rows // 2
    return run(
        functools.partial(feed_body, chunk),
        [
            *held(h0, gain, wg, wu, wd, *cots, *mixes, *projections),
        ],
        [
            ((rows, width), f32),
            ((rows, width), bf16),
            ((rows, units), bf16),
            ((rows, 2 * units), bf16),
            ((quarter, width), f32),
            *[(shape, bf16) for shape in in_pieces((quarter, width))],
        ],
        us=6,
        scratch=[
            VMEM((2, quarter, width), bf16),
            VMEM((4, quarter, width), f32),
        ],
        after=after,
    )


STREAMS = (1, 2)


def bit_of(distance):
    return lax.rem(lax.div(lax.axis_index("dp"), distance), 2)


def split_sums(total_ref, outs):
    if len(outs) == 1:
        outs[0].ref[...] = total_ref[...]
        outs[0].send()
        return
    for n, distance in enumerate(STREAMS):
        keep, send = outs[2 * n : 2 * n + 2]
        pairs, block, columns = keep.ref.shape
        lanes = slice(n * columns, (n + 1) * columns)
        bit = bit_of(distance)
        for t in range(pairs):
            first = t // distance * 2 * distance + t % distance
            send.ref[t] = total_ref[
                rows_at(first + (1 - bit) * distance, block), lanes
            ].astype(bf16)
            keep.ref[t] = total_ref[rows_at(first + bit * distance, block), lanes]
        send.send()
        keep.send()


def sums_outs(width, columns, peers):
    block = width // peers
    if peers >= 4 and block % 16 == 0:
        shape = (peers // 2, block, columns // 2)
        return [(shape, f32), (shape, bf16)] * 2
    return [((width, columns), f32, 1)]


def feed_grads_body(ins, outs, total_ref):
    n2a, n2b, hiddena, hiddenb, backsa, backsb, wd, *cots = ins
    keep, send = outs[:2]
    place = lax.axis_index("mp")
    core = lax.rem(place, 2)
    quarter = cots[0].target.shape[0]
    units = hiddena.target.shape[1]
    total_ref[:, : 2 * units] = dot(n2a.ref[...], backsa.ref[...], 0, 0) + dot(
        n2b.ref[...], backsb.ref[...], 0, 0
    )
    here = lax.div(place, 2) == 0
    arrays = [one.ref for one in (hiddena, hiddenb, *cots)]
    hiddena, hiddenb, cots = arrays[0], arrays[1], arrays[2:]
    for one, two in ((hiddena, hiddenb), (hiddenb, hiddena)):

        @pl.when(here if one is hiddena else jnp.logical_not(here))
        def summed():
            total = None
            for d, hidden in zip(range(4), (one, one, two, two)):
                at = rows_at(lax.bitwise_xor(core, d % 2), quarter)
                part = dot(cots[d][...], hidden[at, :], 0, 0)
                total = part if total is None else total + part
            total_ref[:, 2 * units :] = total

    split_sums(total_ref, outs[2:])
    for half, target in ((1 - core, send), (core, keep)):
        for chunk, hidden in enumerate((hiddena, hiddenb)):
            target.ref[chunk] = dot(hidden[rows_at(half, quarter), :], wd.ref[...]).astype(
                target.ref.dtype
            )


def feed_grads(n2s, hiddens, backs, wd, cots, peers, after):
    units, width = wd.shape
    quarter = cots[0].shape[0]
    return run(
        feed_grads_body,
        [*held(*n2s, *hiddens, *backs, wd, *cots)],
        [
            ((2, quarter, width), f32),
            ((2, quarter, width), bf16),
            *sums_outs(width, 3 * units, peers),
        ],
        us=6,
        scratch=[VMEM((width, 3 * units), f32)],
        mib=20,
        after=after,
    )


def joint_grads_body(heads, ins, outs, total_ref):
    n1, dqa, dqb, dkv, lowa, lowb, mixa, mixb, tiles = ins
    table_out = outs[0]
    rows, own = dqa.target.shape
    total_ref[:, :own] = dot(n1.ref[:rows, :], dqa.ref[...], 0, 0) + dot(
        n1.ref[rows:, :], dqb.ref[...], 0, 0
    )
    total_ref[:, own : 3 * own] = dot(n1.ref[...], dkv.ref[...], 0, 0)
    total_ref[:, 3 * own :] = dot(lowa.ref[...], mixa.ref[...], 0, 0) + dot(
        lowb.ref[...], mixb.ref[...], 0, 0
    )
    split_sums(total_ref, outs[1:])
    head = iota((8, TILE), 0)
    bucket = iota((8, TILE), 1)
    table = jnp.zeros((8, TILE), f32)
    for h in range(heads):
        sums = {}
        for k in range(5):
            least, most = TILE * (k - 2) - TILE + 1, TILE * (k - 2) + TILE - 1
            tile = tiles.ref[(5 * h + k) * TILE : (5 * h + k + 1) * TILE, :]
            if k in (0, 4):
                b = bucket_of(least if k == 0 else most)
                sums[b] = sums.get(b, 0.0) + folded(tile, jnp.sum)
                continue
            offset = TILE * (k - 2) + iota((TILE, TILE), 0) - iota((TILE, TILE), 1)
            runs = bucket_runs(least, most)
            for n, (first, b) in enumerate(runs):
                held = offset >= first
                if n + 1 < len(runs):
                    held = held & (offset < runs[n + 1][0])
                sums[b] = sums.get(b, 0.0) + folded(jnp.where(held, tile, 0.0), jnp.sum)
        for b, part in sums.items():
            total = jnp.sum(jnp.sum(part, axis=0, keepdims=True), axis=1, keepdims=True)
            table = jnp.where((bucket == b) & (head == h), total, table)
    table_out.ref[...] = table


def joint_grads(n1, dqa, dqb, dkv, lows, mixes, tiles, peers, after):
    width, own = n1.shape[1], dqa.shape[1]
    return run(
        functools.partial(joint_grads_body, own // DH),
        [*held(n1, dqa, dqb, dkv, *lows, *mixes, tiles)],
        [((8, TILE), f32), *sums_outs(width, 4 * own, peers)],
        us=6,
        scratch=[VMEM((width, 4 * own), f32)],
        mib=16,
        after=after,
    )


def sum_body(counts, ins, outs):
    one, *ins = ins
    two, passed = ins[: counts[0]], ins[counts[0] :]
    total, *outs = outs
    pieces, copied = outs[: counts[1]], outs[counts[1] :]
    rows = two[0].ref.shape[0]
    for n, piece in enumerate(two):
        at = slice(n * rows, (n + 1) * rows)
        total.ref[at] = (one.ref[at].astype(f32) + piece.ref[...].astype(f32)).astype(total.ref.dtype)
    if pieces:
        scatter_pieces(total.ref[...], pieces)
    for source, target in zip(passed, copied):
        target.ref[...] = source.ref[...]


def added(one, two, after=(), passed=(), kind=bf16, cut=False):
    pieces = in_pieces(one.shape) if cut else []
    return run(
        functools.partial(sum_body, (len(two), len(pieces))),
        held(one, *two, *passed),
        [
            (one.shape, kind),
            *[(shape, kind) for shape in pieces],
            *[(array.shape, array.dtype) for array in passed],
        ],
        us=1,
        mib=4,
        after=after,
    )


def copy_body(ins, outs):
    outs[0].ref[...] = ins[0].ref[...]


def copied(array, after):
    return run(copy_body, held(array), [(array.shape, array.dtype)], us=1, mib=4, after=after)[0]


def out_split_body(ins, outs):
    keep, received = ins
    mine, far = outs
    side = lax.div(lax.axis_index("mp"), 2)
    mine.ref[...] = keep.ref[side] + received.ref[side].astype(f32)
    far.ref[...] = (keep.ref[1 - side] + received.ref[1 - side].astype(f32)).astype(bf16)


def out_split(keep, received, after=()):
    shape = keep.shape[1:]
    ins = held(keep, received)
    return run(out_split_body, ins, [(shape, f32), (shape, bf16)], us=1, mib=4, after=after)


def out_rows_body(ins, outs, rows_ref):
    h1a, h1b, mine, received = ins
    (out,) = outs
    quarter = mine.ref.shape[0]
    side, core = lax.div(lax.axis_index("mp"), 2), lax.rem(lax.axis_index("mp"), 2)
    for n, h1 in enumerate((h1a, h1b)):

        @pl.when(side == n)
        def taken():
            rows_ref[...] = h1.ref[rows_at(core, quarter), :]

    out.ref[...] = (rows_ref[...] + (mine.ref[...] + received.ref[...].astype(f32))).astype(bf16)


def finished_rows(h1s, mine, received, after=()):
    (rows,) = run(
        out_rows_body,
        [*held(*h1s, mine, received)],
        [(mine.shape, bf16, 1)],
        us=1.5,
        scratch=[VMEM(mine.shape, f32)],
        mib=6,
        after=after,
    )
    return rows


def halve_body(distances, ins, outs):
    for n, distance in enumerate(distances):
        keep, received = ins[2 * n : 2 * n + 2]
        kept, sent = outs[2 * n : 2 * n + 2]
        bit = bit_of(distance)
        for u in range(kept.ref.shape[0]):
            far = 2 * u + 1 - bit
            sent.ref[u] = (keep.ref[far] + received.ref[far].astype(f32)).astype(bf16)
        sent.send()
        for u in range(kept.ref.shape[0]):
            near = 2 * u + bit
            kept.ref[u] = keep.ref[near] + received.ref[near].astype(f32)
        kept.send()


def halve(distances, sums, after):
    outs = []
    for keep in sums[::2]:
        shape = (keep.shape[0] // 2, *keep.shape[1:])
        outs += [(shape, f32), (shape, bf16)]
    return run(
        functools.partial(halve_body, distances),
        [*held(*sums)],
        outs,
        us=2.5,
        mib=4,
        after=after,
    )


def halve_last_body(distance, ins, outs):
    kept, sent = outs
    bit = bit_of(distance)
    for n in range(kept.ref.shape[0]):
        keep, received = ins[2 * n : 2 * n + 2]
        sent.ref[n] = (keep.ref[1 - bit] + received.ref[1 - bit].astype(f32)).astype(bf16)
        kept.ref[n] = keep.ref[bit] + received.ref[bit].astype(f32)


def halve_last(distance, sums, after):
    shape = (len(sums) // 2, *sums[0].shape[1:])
    return run(
        functools.partial(halve_last_body, distance),
        held(*sums),
        [(shape, f32), (shape, bf16)],
        us=2.5,
        mib=4,
        after=after,
    )


def last_sums_body(plan, ins, outs, total_ref):
    keep, received = ins
    streams, _, columns = keep.ref.shape
    for n in range(streams):
        total_ref[:, n * columns : (n + 1) * columns] = keep.ref[n] + received.ref[n].astype(f32)
    for out, (first, last, turned) in zip(outs, plan):
        part = total_ref[:, first:last]
        out.ref[...] = part.T if turned else part
        out.send()


def last_sums(plan, sums, after):
    streams, block, columns = sums[0].shape
    shapes = [(last - first, block) if turned else (block, last - first) for first, last, turned in plan]
    return run(
        functools.partial(last_sums_body, plan),
        held(*sums),
        [(shape, f32, 1) for shape in shapes],
        us=2,
        scratch=[VMEM((block, streams * columns), f32)],
        mib=6,
        after=after,
    )


def finish_body(heads, ins, outs):
    one, two = ins
    score, gain_one, gain_two, table, sizes = [out.ref for out in outs]
    total = one.ref[...] + two.ref[...]
    share, width = score.shape[0], total.shape[1]
    moved = pltpu.roll(total, lax.rem(width - lax.axis_index("dp") * share, width), 1)
    score[...] = moved[0, :share]
    gain_one[...] = total[1]
    gain_two[...] = total[2]
    table[...] = total[4 : 4 + heads, :BUCKETS]
    sizes[...] = (total[3:4, :4] / total[3:4, 4:5])[0]


def finished(one, two, heads, share, after=()):
    width = one.shape[1]
    shapes = [(share,), (width,), (width,), (heads, BUCKETS), (4,)]
    return run(
        functools.partial(finish_body, heads),
        [*held(one, two)],
        [(shape, f32, 1) for shape in shapes],
        us=1,
        mib=4,
        after=after,
    )


def swapped(shard, axis, distance):
    peers = lax.axis_size(axis)
    return lax.ppermute(shard, axis, [(i, i ^ distance) for i in range(peers)])


def summed_over(pair, axis, distances, after):
    for distance in distances:
        (value,) = added(pair[0], pair[1:], after, kind=f32)
        pair, after = (value, swapped(value, axis, distance)), ()
    return pair


def scattered(sums):
    peers = lax.axis_size("dp")
    me = lax.axis_index("dp")
    distances = [2**n for n in range(peers.bit_length() - 1)]
    parts = []
    for n, first in enumerate(STREAMS):
        order = sorted(distances, key=lambda d: (d != first, d))
        left = distances[::-1]
        if len(sums) == 4:
            keep, send = sums[2 * n : 2 * n + 2]
            blocks = keep + swapped(send, "dp", first).astype(f32)
            order.pop(0)
            left.remove(first)
        else:
            columns = sums[0].shape[1] // 2
            blocks = sums[0][:, n * columns : (n + 1) * columns]
            blocks = blocks.reshape(peers, -1, columns)
        block, columns = blocks.shape[1:]
        blocks = blocks.reshape(*[2] * len(left), block, columns)
        for distance in order:
            axis = left.index(distance)
            left.remove(distance)
            bit = lax.rem(lax.div(me, distance), 2)
            kept = lax.dynamic_index_in_dim(blocks, bit, axis, keepdims=False)
            sent = lax.dynamic_index_in_dim(blocks, 1 - bit, axis, keepdims=False)
            blocks = kept + swapped(sent.astype(bf16), "dp", distance).astype(f32)
        parts.append(blocks)
    return jnp.concatenate(parts, axis=1)


def body(
    byte_embeds,
    lengths,
    score_weight,
    norm1_gain,
    w_query,
    w_key,
    w_value,
    rel_table,
    w_out,
    norm2_gain,
    w_gate,
    w_up,
    w_down,
    cotangent,
):
    width = byte_embeds.shape[1]
    assert lengths.shape[0] == 1 and lax.axis_size("mp") == 4
    quarter = cotangent.shape[0]
    half = 2 * quarter
    heads = w_query.shape[1] // DH
    units = w_gate.shape[1]
    own = heads * DH
    peers = lax.axis_size("dp")

    cots = [cotangent, swapped(cotangent, "mp", 1), swapped(cotangent, "mp", 2)]
    projections = [w_out, swapped(w_out, "mp", 1), swapped(w_out, "mp", 2)]
    h0, n1, q, k, v, weights, masses, mixing, near, *fetched = pool_forward(
        lengths,
        rel_table.T,
        byte_embeds,
        score_weight,
        norm1_gain,
        w_query.T,
        w_key.T,
        w_value.T,
        norm2_gain,
        w_gate,
        w_up,
        w_down,
        w_out,
        cotangent,
    )
    score_vector, gain_one, wq, wk, wv, gain_two, wg, wu, wd, wo, own_rows = fetched
    mixes, sums, turned = [None, None], [None, None], [None, None]
    mixes[0], sums[0], turned[0] = attend(near, q, k, v, 0, half, [])
    mixes[1], sums[1], turned[1], *passed = attend(
        near, q, k, v, half, half, [mixes[0]], (cots[2], projections[2])
    )
    cots = (own_rows, cots[1], passed[0], swapped(passed[0], "mp", 1))
    projections = (wo, projections[1], passed[1], swapped(passed[1], "mp", 1))
    far = [swapped(mix, "mp", 2) for mix in mixes]
    next_far = copied(far[0], [mixes[1]])
    order = []
    fed, second = [], []
    for chunk in range(2):
        mixed = (mixes[chunk], swapped(mixes[chunk], "mp", 1), far[chunk], swapped(next_far, "mp", 1))
        h1, n2, hidden, backs, keep, *sends = feed(
            h0, cots, gain_two, wg, wu, wd, mixed, projections, chunk, order
        )
        passed = [far[1]] if chunk == 0 else []
        mine, *passed = added(keep, near_pieces(sends), [], passed)
        if passed:
            next_far = passed[0]
        fed.append((h1, n2, hidden, backs))
        second.append((mine, swapped(mine, "mp", 2)))
        order = [mine]
    h1s, n2s, hiddens, backs = zip(*fed)
    out_keep, out_send, *feed_sums = feed_grads(n2s, hiddens, backs, wd, cots, peers, order)
    out_near = swapped(out_send, "mp", 1)

    def received(sums, distances):
        return [
            swapped(sums[k], "dp", distances[k // 2]) if k % 2 else sums[k] for k in range(len(sums))
        ]

    def both(pair, after):
        total, *pieces = added(pair[0], pair[1:], after, cut=True)
        return total, *near_pieces(pieces)

    def back(chunk, pieces, *more):
        return attend_back(
            gain_two, h1s[chunk], q, k, near, sums[chunk], turned[chunk], v, wo, pieces, cots, chunk, *more
        )

    halving = len(feed_sums) == 4 and peers == 8
    lowa, backa, gain_two_sum, dqa, tiles, dk, dv = back(0, both(second[0], [feed_sums[0]]))
    pieces = both(second[1], [lowa])
    out_mine, out_far = out_split(out_keep, out_near, [pieces[0]])
    lowb, backb, gain_two_sum, dqb, tiles, keepa, keepb, dkv, *sends = back(
        1, pieces, (dk, dv, tiles, gain_two_sum, dqa, wq, wk, wv), [out_mine]
    )
    order = [lowb]
    if halving:
        feed_sums = halve(STREAMS[::-1], received(feed_sums, STREAMS), order)
        order = [feed_sums[0]]
    (firsta,) = added(keepa, near_pieces(sends[:PIECES]), order)
    (firstb,) = added(keepb, near_pieces(sends[PIECES:]), [firsta])
    first = [(one, swapped(one, "mp", 2)) for one in (firsta, firstb)]
    table_sum, *joint_sums = joint_grads(
        n1, dqa, dqb, dkv, (lowa, lowb), mixes, tiles, peers, [firstb]
    )
    order = [table_sum]
    feed_plan = ((0, units, False), (units, 2 * units, False), (2 * units, 3 * units, True))
    joint_plan = tuple((n * own, (n + 1) * own, n == 3) for n in range(4))
    if halving:
        feed_sums = halve_last(4, received(feed_sums, STREAMS[::-1]), order)
        joint_sums = halve(STREAMS[::-1], received(joint_sums, STREAMS), [feed_sums[0]])
        order = [joint_sums[0]]
    firsts = both(first[0], order)
    firsts = [*firsts, *both(first[1], [firsts[0]])]
    factors, small, grad_rows = pool_scores(
        lengths,
        byte_embeds,
        h0,
        (backa, backb),
        gain_one,
        weights,
        gain_two_sum,
        table_sum,
        masses,
        firsts,
        order,
    )
    distances = [2**n for n in range(peers.bit_length() - 1)]
    pair = (small, swapped(small, "dp", 1))
    (byte_grad,) = pool_bytes(score_vector, mixing, factors, grad_rows, [small])
    pair = summed_over(pair, "dp", distances[1:2], [(byte_grad, pltpu.HBM)])
    order = [pair[0]]
    if halving:
        joint_sums = halve_last(4, received(joint_sums, STREAMS[::-1]), order)
        order = [joint_sums[0]]
        feed_parts = last_sums(feed_plan, received(feed_sums, (4,)), order)
        order = [(feed_parts[0], pltpu.HBM)]
    out_rows = finished_rows(h1s, out_mine, swapped(out_far, "mp", 2), order)
    pair = summed_over(pair, "dp", distances[2:], [(out_rows, pltpu.HBM)])
    if halving:
        joint_parts = last_sums(joint_plan, received(joint_sums, (4,)), [pair[0]])
    else:
        parts = []
        for sums, plan in ((feed_sums, feed_plan), (joint_sums, joint_plan)):
            total = scattered(sums)
            parts.append([total[:, a:b].T if turned else total[:, a:b] for a, b, turned in plan])
        feed_parts, joint_parts = parts
    score_part, gain_one_part, gain_two_part, table_part, size_dist = finished(
        *pair,
        heads,
        width // peers,
        [(joint_parts[0], pltpu.HBM)] if halving else [],
    )
    return (
        out_rows,
        byte_grad,
        score_part,
        gain_one_part,
        *joint_parts[:3],
        table_part.T,
        joint_parts[3],
        gain_two_part,
        *feed_parts,
        size_dist,
    )


def solution(mesh):
    placed = (
        P("dp", None),
        P("dp"),
        P(),
        P(),
        P(None, "mp"),
        P(None, "mp"),
        P(None, "mp"),
        P(None, "mp"),
        P("mp", None),
        P(),
        P(None, "mp"),
        P(None, "mp"),
        P("mp", None),
        P(("dp", "mp"), None),
    )
    return jax.shard_map(
        body,
        mesh=mesh,
        in_specs=placed,
        out_specs=(
            P(("dp", "mp"), None),
            P("dp", None),
            P("dp"),
            P(),
            P("dp", "mp"),
            P("dp", "mp"),
            P("dp", "mp"),
            P(None, "mp"),
            P("mp", "dp"),
            P(),
            P("dp", "mp"),
            P("dp", "mp"),
            P("mp", "dp"),
            P(),
        ),
        check_vma=False,
    )
```
